32 devices in a mesh: dp: 8 (over z, x), expert: 4 (over y, core).
Axes of the slice: x: 2, y: 2, z: 4, core: 2. Of those that a mesh axis runs over, the one named last changes fastest.
Arguments:
- grads: bfloat16 [8, 4, 512, 1024], P('dp', 'expert'), may hold values from -100 to 100
- signs: int32 [4, 1024], P('expert'), may hold values from -1 to 1, as said below
- weights: bfloat16 [4, 512, 1024], P('expert', 'dp'), may hold values from -4 to 4
- compensation: bfloat16 [4, 512, 1024], P('expert', 'dp'), may hold values from -0.099609375 to 0.099609375
Outputs:
- new_weights: bfloat16 [4, 512, 1024], P('expert')
- update_grad: float32 [4, 512, 1024], P('expert', 'dp')
The draws below stay inside these ranges and needn't reach their ends.
Inputs may be any that keep to these rules, and one draw needn't show every extreme that they name: `signs`: each entry is -1 or +1.
All inputs are finite; a program needn't handle non-finite values.
Results may differ from the reference program's by a relative error of at most 0.0018.
The reference program's roundings to bfloat16 on the way (of `quant`) count: a program that leaves them out, or rounds other values in their place, can miss the bound.
Values may be sent and summed in bfloat16 or wider, within the bound.
No kernel may reach another device: no remote copies, remote signals or barrier semaphores. Data moves between devices by JAX's collectives and lax.ppermute only.
A program may use at most 64 MiB of HBM per device.

```python
import math
import jax
import jax.numpy as jnp
from jax import lax

HBLOCK = 1024
REPLICAS = 8
EXPERTS = 4
BLOCKS = 512


def draw_grads(key, part):
    first, second = jax.random.split(key, 2)
    shape = (REPLICAS, EXPERTS, BLOCKS, HBLOCK)
    noise = jnp.clip(jax.random.normal(first, shape, jnp.float32), -6.0, 6.0)
    steps = jnp.arange(REPLICAS, dtype=jnp.float32) / max(REPLICAS - 1, 1)
    rising = jnp.exp(steps * math.log(3.0))
    factor = jnp.exp(jax.random.uniform(second, (REPLICAS, EXPERTS, BLOCKS, 1), jnp.float32, math.log(0.5), math.log(5.0)))
    return (noise * rising[:, None, None, None] * factor).astype(jnp.bfloat16)


def draw_signs(key, part):
    picks = jax.random.randint(jax.random.fold_in(key, 7), (EXPERTS, HBLOCK), 0, 2)
    return (2 * picks - 1).astype(jnp.int32)


def level_of(stream_key, extent, shards, low, top_value):
    def one(dim, shards_of):
        steps = jax.random.uniform(jax.random.fold_in(jax.random.fold_in(stream_key, 6), dim), (shards_of,), jnp.float32, low / len(shards), top_value / len(shards))
        return jnp.repeat(jnp.exp(steps), extent[dim] // shards_of).reshape((-1,) + (1,) * (len(extent) - dim - 1))

    gain = one(*shards[0])
    for cut in shards[1:]:
        gain = gain * one(*cut)
    return gain


def bell_draw(rng, extent, spread, reach, cuts=(), kind=jnp.bfloat16):
    values = spread * jax.random.normal(rng, extent, jnp.float32)
    if cuts:
        values = values * level_of(rng, extent, cuts, -0.22, 0.18)
    return jnp.clip(values, -reach, reach).astype(kind)


def setup_inputs(seed: int = 0) -> dict:
    key_of = jax.random.split(jax.random.key(seed), 5)
    return {
        "grads": draw_grads(jax.random.fold_in(key_of[4], 71), 0),
        "signs": draw_signs(jax.random.fold_in(key_of[4], 71), 0),
        "weights": bell_draw(key_of[2], (EXPERTS, BLOCKS, HBLOCK), 1.0, 4.0, ((0, 4), (1, 8))),
        "compensation": jnp.clip(jax.random.uniform(key_of[3], (EXPERTS, BLOCKS, HBLOCK), jnp.float32, -0.099609375, 0.099609375) * level_of(key_of[3], (EXPERTS, BLOCKS, HBLOCK), ((0, 4), (1, 8)), -0.4, 0.0), -0.099609375, 0.099609375).astype(jnp.bfloat16),
    }


clamp_level = 2.0
target_rms = 0.2
learn_rate = 0.02

def walsh(values):
    width = values.shape[-1]
    lead = values.shape[:-1]
    half = 1
    while half < width:
        pairs = values.reshape(lead + (width // (2 * half), 2, half))
        upper = pairs[..., 0, :]
        lower = pairs[..., 1, :]
        values = jnp.stack([upper + lower, upper - lower], axis=-2).reshape(lead + (width,))
        half = half * 2
    return values

def reference(grads, signs, weights, compensation):
    inverse_root = 1.0 / math.sqrt(HBLOCK)
    sign_rows = signs.astype(jnp.float32)

    def per_expert(inputs):
        expert_grads, sign_row = inputs
        rotated = walsh(expert_grads.astype(jnp.float32) * sign_row) * inverse_root
        rms = jnp.sqrt(lax.optimization_barrier(jnp.mean(rotated * rotated, axis=-1)) + 1e-06)
        scale = lax.optimization_barrier(jnp.max(rms, axis=0))
        quant = jnp.clip(rotated / scale[None, :, None], -clamp_level, clamp_level).astype(jnp.bfloat16)
        quant = lax.optimization_barrier(quant)
        total = lax.optimization_barrier(jnp.sum(quant.astype(jnp.float32), axis=0))
        mean_rot = total * scale[:, None] / REPLICAS
        return walsh(mean_rot) * inverse_root * sign_row
    unrot = lax.map(per_expert, (jnp.transpose(grads, (1, 0, 2, 3)), sign_rows))
    squares = jnp.sum(unrot * unrot)
    limit = target_rms * math.sqrt(EXPERTS * BLOCKS * HBLOCK)
    factor = limit / jnp.maximum(jnp.sqrt(squares), limit)
    update_grad = unrot * factor
    summed = weights.astype(jnp.float32) + (compensation.astype(jnp.float32) - learn_rate * update_grad)
    new_weights = summed.astype(jnp.bfloat16)
    return (new_weights, update_grad)
```

```python
import functools
import math

import jax
import jax.numpy as jnp
import numpy as np
from jax import lax
from jax.experimental import pallas as pl
from jax.experimental.pallas import tpu as pltpu
from jax.sharding import PartitionSpec as P

clamp_level = 2.0
target_rms = 0.2
learn_rate = 0.02
lanes = 128
vmem_bytes = 40 * 1024 * 1024


def hadamard(width):
    matrix = np.ones((1, 1), np.float32)
    while matrix.shape[0] < width:
        matrix = np.block([[matrix, matrix], [matrix, -matrix]])
    return matrix


def butterfly(groups):
    half = 1
    groups = list(groups)
    while half < len(groups):
        for start in range(0, len(groups), 2 * half):
            for i in range(start, start + half):
                upper, lower = groups[i], groups[i + half]
                groups[i], groups[i + half] = upper + lower, upper - lower
        half *= 2
    return groups


def rotate_groups(pieces, matrix, base):
    count = pieces[0].shape[1] // base
    groups = []
    for g in range(count):
        part = None
        for piece in pieces:
            term = jnp.dot(
                piece[:, g * base : (g + 1) * base], matrix, preferred_element_type=jnp.float32
            )
            part = term if part is None else part + term
        groups.append(part)
    return butterfly(groups)


def reduce_kernel(replicas, base, x_ref, sign_ref, matrix_ref, unrot_ref, square_ref, rotated):
    owned, width = x_ref.shape[1:]
    count = width // base
    matrix = matrix_ref[...]
    signs = sign_ref[...].astype(jnp.float32)
    sign_half = signs.astype(jnp.bfloat16)
    biggest = jnp.zeros((owned, 1), jnp.float32)

    def forward(r, biggest):
        groups = rotate_groups([x_ref[r] * sign_half], matrix, base)
        squares = None
        for g, group in enumerate(groups):
            rotated[r, :, g * base : (g + 1) * base] = group
            term = group * group
            squares = term if squares is None else squares + term
        return jnp.maximum(biggest, jnp.sum(squares, axis=1, keepdims=True))

    biggest = lax.fori_loop(0, replicas, forward, biggest, unroll=replicas <= 8)
    scale = jnp.sqrt(biggest * (1.0 / (width * width)) + 1e-06)
    inverse = (1.0 / math.sqrt(width)) / scale

    def add(r, total):
        level = jnp.clip(rotated[r] * inverse, -clamp_level, clamp_level)
        return total + level.astype(jnp.bfloat16).astype(jnp.float32)

    total = lax.fori_loop(
        0, replicas, add, jnp.zeros((owned, width), jnp.float32), unroll=replicas <= 8
    )
    mean_scale = scale / replicas
    mean_rot = total * mean_scale
    squares = jnp.sum(mean_rot * mean_rot)
    square_ref[...] = jnp.full(square_ref.shape, squares, jnp.float32)
    high = total.astype(jnp.bfloat16)
    low = (total - high.astype(jnp.float32)).astype(jnp.bfloat16)
    groups = rotate_groups([high, low], matrix, base)
    back = mean_scale * (1.0 / math.sqrt(width))
    for g in range(count):
        cut = slice(g * base, (g + 1) * base)
        unrot_ref[:, cut] = groups[g] * back * signs[:, cut]


def update_kernel(limit, square_ref, unrot_ref, weight_ref, comp_ref, new_ref, update_ref):
    squares = jnp.sum(square_ref[...], axis=0, keepdims=True)[:, 0:1]
    factor = limit / jnp.maximum(jnp.sqrt(squares), limit)
    update = unrot_ref[...] * factor
    update_ref[...] = update
    summed = weight_ref[...].astype(jnp.float32) + (
        comp_ref[...].astype(jnp.float32) - learn_rate * update
    )
    new_ref[...] = summed.astype(jnp.bfloat16)


def gather_blocks(block, replicas):
    x_count = 1 << ((replicas.bit_length() - 1) // 2)
    z_count = replicas // x_count
    me = lax.axis_index("dp")

    def swap(value, mask):
        return lax.ppermute(value, "dp", [(i, i ^ mask) for i in range(replicas)])

    pieces = {0: block}
    for x in range(1, x_count):
        pieces[x] = swap(block, x)
    for z in range(1, z_count):
        pieces[z * x_count] = swap(block, z * x_count)
    for z in range(1, z_count):
        for x in range(1, x_count):
            pieces[z * x_count + x] = swap(pieces[z * x_count], x)
    owned, width = block.shape
    out = jnp.zeros((replicas, owned, width), block.dtype)
    for mask, piece in pieces.items():
        out = lax.dynamic_update_slice(out, piece[None], (me ^ mask, 0, 0))
    return out.reshape(1, replicas * owned, width)


def on_device(grads, signs, weights, compensation):
    blocks, width = grads.shape[2:]
    replicas = lax.axis_size("dp")
    devices = replicas * lax.axis_size("expert")
    owned = blocks // replicas
    base = min(width, 256)
    matrix = jnp.asarray(hadamard(base), jnp.bfloat16)
    received = lax.all_to_all(
        grads.reshape(replicas, owned, width), "dp", split_axis=0, concat_axis=0, tiled=True
    )
    unrot, squares = pl.pallas_call(
        functools.partial(reduce_kernel, replicas, base),
        out_shape=(
            jax.ShapeDtypeStruct((owned, width), jnp.float32),
            jax.ShapeDtypeStruct((devices, 1, lanes), jnp.float32),
        ),
        scratch_shapes=[pltpu.VMEM((replicas, owned, width), jnp.float32)],
        compiler_params=pltpu.CompilerParams(vmem_limit_bytes=vmem_bytes),
        cost_estimate=pl.CostEstimate(
            flops=2 * blocks * width * base, bytes_accessed=2 * blocks * width, transcendentals=0
        ),
        name="reduce_blocks",
    )(received, signs, matrix)
    squares = lax.all_to_all(squares, ("dp", "expert"), split_axis=0, concat_axis=0, tiled=True)
    limit = target_rms * math.sqrt(blocks * width * lax.axis_size("expert"))
    new_weights, update_grad = pl.pallas_call(
        functools.partial(update_kernel, limit),
        out_shape=(
            jax.ShapeDtypeStruct((owned, width), jnp.bfloat16),
            jax.ShapeDtypeStruct((owned, width), jnp.float32),
        ),
        compiler_params=pltpu.CompilerParams(vmem_limit_bytes=vmem_bytes),
        name="update_blocks",
    )(
        squares.reshape(devices, lanes),
        unrot,
        weights.reshape(owned, width),
        compensation.reshape(owned, width),
    )
    return gather_blocks(new_weights, replicas), update_grad.reshape(weights.shape)


def solution(mesh):
    in_specs = (
        P("dp", "expert", None, None),
        P("expert", None),
        P("expert", "dp", None),
        P("expert", "dp", None),
    )
    out_specs = (P("expert", None, None), P("expert", "dp", None))
    return jax.shard_map(
        on_device, mesh=mesh, in_specs=in_specs, out_specs=out_specs, check_vma=False
    )
```

```python
import functools
import math

import jax
import jax.numpy as jnp
import numpy as np
from jax import lax
from jax.experimental import pallas as pl
from jax.experimental.pallas import tpu as pltpu
from jax.sharding import PartitionSpec as P

clamp_level = 2.0
target_rms = 0.2
learn_rate = 0.02
lanes = 128
vmem_bytes = 40 * 1024 * 1024


def hadamard(width):
    matrix = np.ones((1, 1), np.float32)
    while matrix.shape[0] < width:
        matrix = np.block([[matrix, matrix], [matrix, -matrix]])
    return matrix


def butterfly(groups):
    half = 1
    groups = list(groups)
    while half < len(groups):
        for start in range(0, len(groups), 2 * half):
            for i in range(start, start + half):
                upper, lower = groups[i], groups[i + half]
                groups[i], groups[i + half] = upper + lower, upper - lower
        half *= 2
    return groups


def rotate_groups(pieces, matrix, base):
    count = pieces[0].shape[1] // base
    groups = []
    for g in range(count):
        part = None
        for piece in pieces:
            term = jnp.dot(
                piece[:, g * base : (g + 1) * base], matrix, preferred_element_type=jnp.float32
            )
            part = term if part is None else part + term
        groups.append(part)
    return butterfly(groups)


def rotate_kernel(count, base, *refs):
    pieces, (sign_ref, matrix_ref, rotated, biggest_ref) = refs[:count], refs[count:]
    rotate_pieces(pieces, sign_ref, matrix_ref, rotated, biggest_ref, None, base)


def rotate_pieces(pieces, sign_ref, matrix_ref, rotated, biggest_ref, biggest, base):
    matrix = matrix_ref[...]
    signs = sign_ref[...].astype(jnp.float32).astype(jnp.bfloat16)
    for r, piece in enumerate(pieces):
        groups = rotate_groups([piece[...] * signs], matrix, base)
        squares = None
        for g, group in enumerate(groups):
            rotated[r, :, g * base : (g + 1) * base] = group
            term = group * group
            squares = term if squares is None else squares + term
        squares = jnp.sum(squares, axis=1, keepdims=True)
        biggest = squares if biggest is None else jnp.maximum(biggest, squares)
    if biggest_ref is not None:
        biggest_ref[...] = jnp.broadcast_to(biggest, biggest_ref.shape)
    return biggest


def reduce_kernel(count, base, *refs):
    pieces, rest = refs[:count], refs[count:]
    near_ref, biggest_ref, sign_ref, matrix_ref, unrot_ref, square_ref, rotated = rest
    owned, width = unrot_ref.shape
    near = near_ref.shape[0]
    replicas = near + count
    biggest = rotate_pieces(
        pieces, sign_ref, matrix_ref, rotated, None, biggest_ref[:, 0:1], base
    )
    scale = jnp.sqrt(biggest * (1.0 / (width * width)) + 1e-06)
    inverse = (1.0 / math.sqrt(width)) / scale
    total = None
    for source, r in [(near_ref, r) for r in range(near)] + [(rotated, r) for r in range(count)]:
        level = jnp.clip(source[r] * inverse, -clamp_level, clamp_level)
        level = level.astype(jnp.bfloat16).astype(jnp.float32)
        total = level if total is None else total + level
    mean_scale = scale / replicas
    mean_rot = total * mean_scale
    squares = jnp.sum(mean_rot * mean_rot)
    square_ref[...] = jnp.full(square_ref.shape, squares, jnp.float32)
    high = total.astype(jnp.bfloat16)
    low = (total - high.astype(jnp.float32)).astype(jnp.bfloat16)
    groups = rotate_groups([high, low], matrix_ref[...], base)
    back = mean_scale * (1.0 / math.sqrt(width))
    signs = sign_ref[...].astype(jnp.float32)
    for g, group in enumerate(groups):
        cut = slice(g * base, (g + 1) * base)
        unrot_ref[:, cut] = group * back * signs[:, cut]


def update_kernel(limit, square_ref, unrot_ref, weight_ref, comp_ref, new_ref, update_ref):
    squares = jnp.sum(square_ref[...], axis=0, keepdims=True)[:, 0:1]
    factor = limit / jnp.maximum(jnp.sqrt(squares), limit)
    update = unrot_ref[...] * factor
    update_ref[...] = update
    summed = weight_ref[...].astype(jnp.float32) + (
        comp_ref[...].astype(jnp.float32) - learn_rate * update
    )
    new_ref[...] = summed.astype(jnp.bfloat16)


def swap(value, mask):
    size = lax.axis_size("dp")
    return lax.ppermute(value, "dp", [(i, i ^ mask) for i in range(size)])


def gather_blocks(block, replicas):
    x_count = 1 << ((replicas.bit_length() - 1) // 2)
    z_count = replicas // x_count
    me = lax.axis_index("dp")

    pieces = {0: block}
    for x in range(1, x_count):
        pieces[x] = swap(block, x)
    for z in range(1, z_count):
        pieces[z * x_count] = swap(block, z * x_count)
    for z in range(1, z_count):
        for x in range(1, x_count):
            pieces[z * x_count + x] = swap(pieces[z * x_count], x)
    owned, width = block.shape
    out = jnp.zeros((replicas, owned, width), block.dtype)
    for mask, piece in pieces.items():
        out = lax.dynamic_update_slice(out, piece[None], (me ^ mask, 0, 0))
    return out.reshape(1, replicas * owned, width)


def on_device(grads, signs, weights, compensation):
    blocks, width = grads.shape[2:]
    replicas = lax.axis_size("dp")
    devices = replicas * lax.axis_size("expert")
    owned = blocks // replicas
    base = min(width, 256)
    matrix = jnp.asarray(hadamard(base), jnp.bfloat16)
    me = lax.axis_index("dp")
    local = grads.reshape(replicas, owned, width)

    def block_of(index):
        return lax.dynamic_slice_in_dim(local, index, 1, 0).reshape(owned, width)

    near = max(replicas // 2, 1)
    pieces = {}
    for mask in list(range(near, replicas)) + list(range(1, near)):
        pieces[mask] = swap(block_of(me ^ mask), mask)
    pieces[0] = block_of(me)
    params = pltpu.CompilerParams(vmem_limit_bytes=vmem_bytes)
    cost = pl.CostEstimate(
        flops=blocks * width * base, bytes_accessed=3 * blocks * width, transcendentals=0
    )
    near_rotated, biggest = pl.pallas_call(
        functools.partial(rotate_kernel, near, base),
        out_shape=(
            jax.ShapeDtypeStruct((near, owned, width), jnp.float32),
            jax.ShapeDtypeStruct((owned, lanes), jnp.float32),
        ),
        compiler_params=params,
        cost_estimate=cost,
        name="rotate_near",
    )(*[pieces[mask] for mask in range(near)], signs, matrix)
    far = replicas - near
    unrot, squares = pl.pallas_call(
        functools.partial(reduce_kernel, far, base),
        out_shape=(
            jax.ShapeDtypeStruct((owned, width), jnp.float32),
            jax.ShapeDtypeStruct((devices, 1, lanes), jnp.float32),
        ),
        scratch_shapes=[pltpu.VMEM((max(far, 1), owned, width), jnp.float32)],
        compiler_params=params,
        cost_estimate=cost,
        name="reduce_blocks",
    )(*[pieces[mask] for mask in range(near, replicas)], near_rotated, biggest, signs, matrix)
    squares = lax.all_to_all(squares, ("dp", "expert"), split_axis=0, concat_axis=0, tiled=True)
    limit = target_rms * math.sqrt(blocks * width * lax.axis_size("expert"))
    new_weights, update_grad = pl.pallas_call(
        functools.partial(update_kernel, limit),
        out_shape=(
            jax.ShapeDtypeStruct((owned, width), jnp.bfloat16),
            jax.ShapeDtypeStruct((owned, width), jnp.float32),
        ),
        compiler_params=pltpu.CompilerParams(vmem_limit_bytes=vmem_bytes),
        name="update_blocks",
    )(
        squares.reshape(devices, lanes),
        unrot,
        weights.reshape(owned, width),
        compensation.reshape(owned, width),
    )
    return gather_blocks(new_weights, replicas), update_grad.reshape(weights.shape)


def solution(mesh):
    in_specs = (
        P("dp", "expert", None, None),
        P("expert", None),
        P("expert", "dp", None),
        P("expert", "dp", None),
    )
    out_specs = (P("expert", None, None), P("expert", "dp", None))
    return jax.shard_map(
        on_device, mesh=mesh, in_specs=in_specs, out_specs=out_specs, check_vma=False
    )
```

```python
import functools
import math

import jax
import jax.numpy as jnp
import numpy as np
from jax import lax
from jax.experimental import pallas as pl
from jax.experimental.pallas import tpu as pltpu
from jax.sharding import PartitionSpec as P

clamp_level = 2.0
target_rms = 0.2
learn_rate = 0.02
lanes = 128
vmem_bytes = 40 * 1024 * 1024


def hadamard(width):
    matrix = np.ones((1, 1), np.float32)
    while matrix.shape[0] < width:
        matrix = np.block([[matrix, matrix], [matrix, -matrix]])
    return matrix


def butterfly(groups):
    half = 1
    groups = list(groups)
    while half < len(groups):
        for start in range(0, len(groups), 2 * half):
            for i in range(start, start + half):
                upper, lower = groups[i], groups[i + half]
                groups[i], groups[i + half] = upper + lower, upper - lower
        half *= 2
    return groups


def rotate_groups(pieces, matrix, base):
    count = pieces[0].shape[1] // base
    groups = []
    for g in range(count):
        part = None
        for piece in pieces:
            term = jnp.dot(
                piece[:, g * base : (g + 1) * base], matrix, preferred_element_type=jnp.float32
            )
            part = term if part is None else part + term
        groups.append(part)
    return butterfly(groups)


def rotate_kernel(count, base, *refs):
    pieces, (sign_ref, matrix_ref, rotated, biggest_ref) = refs[:count], refs[count:]
    rotate_pieces(pieces, sign_ref, matrix_ref, rotated, biggest_ref, None, base)


def rotate_pieces(pieces, sign_ref, matrix_ref, rotated, biggest_ref, biggest, base):
    matrix = matrix_ref[...]
    signs = sign_ref[...].astype(jnp.float32).astype(jnp.bfloat16)
    for r, piece in enumerate(pieces):
        groups = rotate_groups([piece[...] * signs], matrix, base)
        squares = None
        for g, group in enumerate(groups):
            rotated[r, :, g * base : (g + 1) * base] = group
            term = group * group
            squares = term if squares is None else squares + term
        squares = jnp.sum(squares, axis=1, keepdims=True)
        biggest = squares if biggest is None else jnp.maximum(biggest, squares)
    if biggest_ref is not None:
        biggest_ref[...] = jnp.broadcast_to(biggest, biggest_ref.shape)
    return biggest


def reduce_kernel(count, base, *refs):
    pieces, rest = refs[:count], refs[count:]
    near_ref, biggest_ref, sign_ref, matrix_ref, unrot_ref, square_ref, rotated = rest
    owned, width = unrot_ref.shape
    near = near_ref.shape[0]
    replicas = near + count
    biggest = rotate_pieces(
        pieces, sign_ref, matrix_ref, rotated, None, biggest_ref[:, 0:1], base
    )
    scale = jnp.sqrt(biggest * (1.0 / (width * width)) + 1e-06)
    inverse = (1.0 / math.sqrt(width)) / scale
    total = None
    for source, r in [(near_ref, r) for r in range(near)] + [(rotated, r) for r in range(count)]:
        level = jnp.clip(source[r] * inverse, -clamp_level, clamp_level)
        level = level.astype(jnp.bfloat16).astype(jnp.float32)
        total = level if total is None else total + level
    mean_scale = scale / replicas
    mean_rot = total * mean_scale
    squares = jnp.sum(mean_rot * mean_rot)
    square_ref[...] = jnp.full(square_ref.shape, squares, jnp.float32)
    high = total.astype(jnp.bfloat16)
    low = (total - high.astype(jnp.float32)).astype(jnp.bfloat16)
    groups = rotate_groups([high, low], matrix_ref[...], base)
    back = mean_scale * (1.0 / math.sqrt(width))
    signs = sign_ref[...].astype(jnp.float32)
    for g, group in enumerate(groups):
        cut = slice(g * base, (g + 1) * base)
        unrot_ref[:, cut] = group * back * signs[:, cut]


def update_kernel(limit, square_ref, unrot_ref, weight_ref, comp_ref, new_ref, update_ref):
    squares = jnp.sum(square_ref[...], axis=0, keepdims=True)[:, 0:1]
    factor = limit / jnp.maximum(jnp.sqrt(squares), limit)
    update = unrot_ref[...] * factor
    update_ref[...] = update
    summed = weight_ref[...].astype(jnp.float32) + (
        comp_ref[...].astype(jnp.float32) - learn_rate * update
    )
    new_ref[...] = summed.astype(jnp.bfloat16)


def swap(value, mask):
    size = lax.axis_size("dp")
    return lax.ppermute(value, "dp", [(i, i ^ mask) for i in range(size)])


def gather_blocks(block, replicas):
    x_count = 1 << ((replicas.bit_length() - 1) // 2)
    near = max(replicas // 2, 1)
    me = lax.axis_index("dp")
    pieces = {0: block}

    def spread(start):
        for z in range(x_count, near, x_count):
            pieces[start + z] = swap(pieces[start], z)
        for z in range(0, near, x_count):
            for x in range(1, min(x_count, near)):
                pieces[start + z + x] = swap(pieces[start + z], x)

    if replicas > 1:
        pieces[near] = swap(block, near)
    spread(0)
    if replicas > 1:
        spread(near)
    owned, width = block.shape
    out = jnp.zeros((replicas, owned, width), block.dtype)
    for mask, piece in pieces.items():
        out = lax.dynamic_update_slice(out, piece[None], (me ^ mask, 0, 0))
    return out.reshape(1, replicas * owned, width)


def on_device(grads, signs, weights, compensation):
    blocks, width = grads.shape[2:]
    replicas = lax.axis_size("dp")
    devices = replicas * lax.axis_size("expert")
    owned = blocks // replicas
    base = min(width, 256)
    matrix = jnp.asarray(hadamard(base), jnp.bfloat16)
    me = lax.axis_index("dp")
    local = grads.reshape(replicas, owned, width)

    def block_of(index):
        return lax.dynamic_slice_in_dim(local, index, 1, 0).reshape(owned, width)

    near = max(replicas // 2, 1)
    pieces = {}
    for mask in list(range(near, replicas)) + list(range(1, near)):
        pieces[mask] = swap(block_of(me ^ mask), mask)
    pieces[0] = block_of(me)
    params = pltpu.CompilerParams(vmem_limit_bytes=vmem_bytes)
    cost = pl.CostEstimate(
        flops=blocks * width * base, bytes_accessed=3 * blocks * width, transcendentals=0
    )
    near_rotated, biggest = pl.pallas_call(
        functools.partial(rotate_kernel, near, base),
        out_shape=(
            jax.ShapeDtypeStruct((near, owned, width), jnp.float32),
            jax.ShapeDtypeStruct((owned, lanes), jnp.float32),
        ),
        compiler_params=params,
        cost_estimate=cost,
        name="rotate_near",
    )(*[pieces[mask] for mask in range(near)], signs, matrix)
    far = replicas - near
    unrot, squares = pl.pallas_call(
        functools.partial(reduce_kernel, far, base),
        out_shape=(
            jax.ShapeDtypeStruct((owned, width), jnp.float32),
            jax.ShapeDtypeStruct((devices, 1, lanes), jnp.float32),
        ),
        scratch_shapes=[pltpu.VMEM((max(far, 1), owned, width), jnp.float32)],
        compiler_params=params,
        cost_estimate=cost,
        name="reduce_blocks",
    )(*[pieces[mask] for mask in range(near, replicas)], near_rotated, biggest, signs, matrix)
    squares = lax.all_to_all(squares, ("dp", "expert"), split_axis=0, concat_axis=0, tiled=True)
    limit = target_rms * math.sqrt(blocks * width * lax.axis_size("expert"))
    new_weights, update_grad = pl.pallas_call(
        functools.partial(update_kernel, limit),
        out_shape=(
            jax.ShapeDtypeStruct((owned, width), jnp.bfloat16),
            jax.ShapeDtypeStruct((owned, width), jnp.float32),
        ),
        compiler_params=pltpu.CompilerParams(vmem_limit_bytes=vmem_bytes),
        name="update_blocks",
    )(
        squares.reshape(devices, lanes),
        unrot,
        weights.reshape(owned, width),
        compensation.reshape(owned, width),
    )
    return gather_blocks(new_weights, replicas), update_grad.reshape(weights.shape)


def solution(mesh):
    in_specs = (
        P("dp", "expert", None, None),
        P("expert", None),
        P("expert", "dp", None),
        P("expert", "dp", None),
    )
    out_specs = (P("expert", None, None), P("expert", "dp", None))
    return jax.shard_map(
        on_device, mesh=mesh, in_specs=in_specs, out_specs=out_specs, check_vma=False
    )
```

```python
import functools
import math

import jax
import jax.numpy as jnp
import numpy as np
from jax import lax
from jax.experimental import pallas as pl
from jax.experimental.pallas import tpu as pltpu
from jax.sharding import PartitionSpec as P

clamp_level = 2.0
target_rms = 0.2
learn_rate = 0.02
lanes = 128
vmem_bytes = 40 * 1024 * 1024


def hadamard(width):
    matrix = np.ones((1, 1), np.float32)
    while matrix.shape[0] < width:
        matrix = np.block([[matrix, matrix], [matrix, -matrix]])
    return matrix


def butterfly(groups):
    half = 1
    groups = list(groups)
    while half < len(groups):
        for start in range(0, len(groups), 2 * half):
            for i in range(start, start + half):
                upper, lower = groups[i], groups[i + half]
                groups[i], groups[i + half] = upper + lower, upper - lower
        half *= 2
    return groups


def rotate_groups(pieces, matrix, base):
    count = pieces[0].shape[1] // base
    groups = []
    for g in range(count):
        part = None
        for piece in pieces:
            term = jnp.dot(
                piece[:, g * base : (g + 1) * base], matrix, preferred_element_type=jnp.float32
            )
            part = term if part is None else part + term
        groups.append(part)
    return butterfly(groups)


def square_rows(groups):
    squares = None
    for group in groups:
        squares = group * group if squares is None else squares + group * group
    return jnp.sum(squares, axis=1, keepdims=True)


def sums_kernel(base, x_ref, sign_ref, matrix_ref, sums_ref):
    owned, width = x_ref.shape[2:]
    signs = sign_ref[...].astype(jnp.float32).astype(jnp.bfloat16)
    rows = x_ref[...].reshape(2 * owned, width) * signs
    squares = square_rows(rotate_groups([rows], matrix_ref[...], base))
    shape = (2 * owned, 2 * owned)
    row, lane = (lax.broadcasted_iota(jnp.int32, shape, axis) for axis in (0, 1))
    line = jnp.sum(jnp.where(row == lane, squares, 0.0), axis=0, keepdims=True)
    sums_ref[...] = jnp.broadcast_to(line, sums_ref.shape)


def scale_rows(sums_ref, offset, owned, width, near):
    biggest = jnp.max(sums_ref[...], axis=0, keepdims=True)
    shape = (owned, 2 * owned)
    row, lane = (lax.broadcasted_iota(jnp.int32, shape, axis) for axis in (0, 1))
    biggest = jnp.sum(jnp.where(lane == row + offset, biggest, 0.0), axis=1, keepdims=True)
    mean = biggest * (1.0 / (width * width))
    scale = jnp.sqrt(mean + 1e-06)
    peak = jnp.sqrt(mean * width) / scale
    step = near * jnp.where(
        peak >= clamp_level, clamp_level / 32768.0, jnp.maximum(peak, 1e-20) / 32767.0
    )
    return scale, step


def add_levels(pieces, scale, sign_ref, matrix_ref, base):
    width = pieces[0].shape[1]
    signs = sign_ref[...].astype(jnp.float32).astype(jnp.bfloat16)
    matrix = matrix_ref[...]
    inverse = (1.0 / math.sqrt(width)) / scale
    totals = None
    for piece in pieces:
        groups = rotate_groups([piece[...] * signs], matrix, base)
        levels = [
            jnp.clip(group * inverse, -clamp_level, clamp_level)
            .astype(jnp.bfloat16)
            .astype(jnp.float32)
            for group in groups
        ]
        totals = levels if totals is None else [t + v for t, v in zip(totals, levels)]
    return totals


def proxy_kernel(near, base, offset_ref, *refs):
    pieces, (sums_ref, sign_ref, matrix_ref, sent_ref) = refs[:near], refs[near:]
    owned, width = sent_ref.shape
    scale, step = scale_rows(sums_ref, owned - offset_ref[0, 0], owned, width, near)
    totals = add_levels(pieces, scale, sign_ref, matrix_ref, base)
    for g, total in enumerate(totals):
        value = jnp.clip(jnp.round(total / step), -32767.0, 32767.0)
        sent_ref[:, g * base : (g + 1) * base] = value.astype(jnp.int16)


def owner_kernel(near, base, offset_ref, *refs):
    pieces, (sums_ref, sign_ref, matrix_ref, total_ref) = refs[:near], refs[near:]
    owned, width = total_ref.shape
    scale, _ = scale_rows(sums_ref, offset_ref[0, 0], owned, width, near)
    totals = add_levels(pieces, scale, sign_ref, matrix_ref, base)
    for g, total in enumerate(totals):
        total_ref[:, g * base : (g + 1) * base] = total


def finish_kernel(
    near, base, offset_ref, near_ref, far_ref, sums_ref, sign_ref, matrix_ref, unrot_ref, square_ref
):
    owned, width = near_ref.shape
    scale, step = scale_rows(sums_ref, offset_ref[0, 0], owned, width, near)
    total = near_ref[...] + far_ref[...].astype(jnp.float32) * step
    mean_scale = scale / (2 * near)
    mean_rot = total * mean_scale
    squares = jnp.sum(mean_rot * mean_rot)
    square_ref[...] = jnp.full(square_ref.shape, squares, jnp.float32)
    high = total.astype(jnp.bfloat16)
    low = (total - high.astype(jnp.float32)).astype(jnp.bfloat16)
    groups = rotate_groups([high, low], matrix_ref[...], base)
    back = mean_scale * (1.0 / math.sqrt(width))
    signs = sign_ref[...].astype(jnp.float32)
    for g, group in enumerate(groups):
        cut = slice(g * base, (g + 1) * base)
        unrot_ref[:, cut] = group * back * signs[:, cut]


def update_kernel(limit, square_ref, unrot_ref, weight_ref, comp_ref, new_ref, update_ref):
    squares = jnp.sum(square_ref[...], axis=0, keepdims=True)[:, 0:1]
    factor = limit / jnp.maximum(jnp.sqrt(squares), limit)
    update = unrot_ref[...] * factor
    update_ref[...] = update
    summed = weight_ref[...].astype(jnp.float32) + (
        comp_ref[...].astype(jnp.float32) - learn_rate * update
    )
    new_ref[...] = summed.astype(jnp.bfloat16)


def swap(value, mask):
    size = lax.axis_size("dp")
    return lax.ppermute(value, "dp", [(i, i ^ mask) for i in range(size)])


def gather_blocks(block, replicas):
    x_count = 1 << ((replicas.bit_length() - 1) // 2)
    near = max(replicas // 2, 1)
    me = lax.axis_index("dp")
    pieces = {0: block}

    def spread(start):
        for z in range(x_count, near, x_count):
            pieces[start + z] = swap(pieces[start], z)
        for z in range(0, near, x_count):
            for x in range(1, min(x_count, near)):
                pieces[start + z + x] = swap(pieces[start + z], x)

    if replicas > 1:
        pieces[near] = swap(block, near)
    spread(0)
    if replicas > 1:
        spread(near)
    owned, width = block.shape
    out = jnp.zeros((replicas, owned, width), block.dtype)
    for mask, piece in pieces.items():
        out = lax.dynamic_update_slice(out, piece[None], (me ^ mask, 0, 0))
    return out.reshape(1, replicas * owned, width)


def on_device(grads, signs, weights, compensation):
    blocks, width = grads.shape[2:]
    replicas = lax.axis_size("dp")
    devices = replicas * lax.axis_size("expert")
    owned = blocks // replicas
    base = min(width, 256)
    matrix = jnp.asarray(hadamard(base), jnp.bfloat16)
    me = lax.axis_index("dp")
    near = replicas // 2
    offset = (me // near * owned).astype(jnp.int32).reshape(1, 1)
    params = pltpu.CompilerParams(vmem_limit_bytes=vmem_bytes)
    scalar = pl.BlockSpec(memory_space=pltpu.SMEM)
    array = pl.BlockSpec(memory_space=pltpu.VMEM)

    def block_of(source, index):
        source = source.reshape(replicas, owned, width)
        return lax.dynamic_slice_in_dim(source, index, 1, 0).reshape(owned, width)

    far_pieces = [swap(block_of(grads, me ^ mask ^ near), mask) for mask in range(1, near)]
    far_pieces.append(block_of(grads, me ^ near))
    sums = pl.pallas_call(
        functools.partial(sums_kernel, base),
        grid=(near,),
        in_specs=[
            pl.BlockSpec((2, 1, owned, width), lambda j: (0, j, 0, 0)),
            pl.BlockSpec((1, width), lambda j: (0, 0)),
            pl.BlockSpec((base, base), lambda j: (0, 0)),
        ],
        out_specs=pl.BlockSpec((2, 1, 1, 2 * owned), lambda j: (0, j, 0, 0)),
        out_shape=jax.ShapeDtypeStruct((2, near, 1, 2 * owned), jnp.float32),
        compiler_params=params,
        name="sum_squares",
    )(grads.reshape(2, near, owned, width), signs, matrix)
    grads, sums = lax.optimization_barrier((grads, sums))
    sums = lax.all_to_all(
        sums.reshape(replicas, 1, 2 * owned), "dp", split_axis=0, concat_axis=0, tiled=True
    ).reshape(replicas, 2 * owned)
    near_pieces = [swap(block_of(grads, me ^ mask), mask) for mask in range(1, near)]
    near_pieces.append(block_of(grads, me))
    sent = pl.pallas_call(
        functools.partial(proxy_kernel, near, base),
        in_specs=[scalar] + [array] * (near + 3),
        out_shape=jax.ShapeDtypeStruct((owned, width), jnp.int16),
        compiler_params=params,
        name="proxy_blocks",
    )(offset, *far_pieces, sums, signs, matrix)
    far_total = swap(sent, near)
    near_total = pl.pallas_call(
        functools.partial(owner_kernel, near, base),
        in_specs=[scalar] + [array] * (near + 3),
        out_shape=jax.ShapeDtypeStruct((owned, width), jnp.float32),
        compiler_params=params,
        name="owner_blocks",
    )(offset, *near_pieces, sums, signs, matrix)
    unrot, squares = pl.pallas_call(
        functools.partial(finish_kernel, near, base),
        in_specs=[scalar] + [array] * 5,
        out_shape=(
            jax.ShapeDtypeStruct((owned, width), jnp.float32),
            jax.ShapeDtypeStruct((devices, 1, lanes), jnp.float32),
        ),
        compiler_params=params,
        name="finish_blocks",
    )(offset, near_total, far_total, sums, signs, matrix)
    squares = lax.all_to_all(squares, ("dp", "expert"), split_axis=0, concat_axis=0, tiled=True)
    limit = target_rms * math.sqrt(blocks * width * lax.axis_size("expert"))
    new_weights, update_grad = pl.pallas_call(
        functools.partial(update_kernel, limit),
        out_shape=(
            jax.ShapeDtypeStruct((owned, width), jnp.bfloat16),
            jax.ShapeDtypeStruct((owned, width), jnp.float32),
        ),
        compiler_params=pltpu.CompilerParams(vmem_limit_bytes=vmem_bytes),
        name="update_blocks",
    )(
        squares.reshape(devices, lanes),
        unrot,
        weights.reshape(owned, width),
        compensation.reshape(owned, width),
    )
    return gather_blocks(new_weights, replicas), update_grad.reshape(weights.shape)


def solution(mesh):
    in_specs = (
        P("dp", "expert", None, None),
        P("expert", None),
        P("expert", "dp", None),
        P("expert", "dp", None),
    )
    out_specs = (P("expert", None, None), P("expert", "dp", None))
    return jax.shard_map(
        on_device, mesh=mesh, in_specs=in_specs, out_specs=out_specs, check_vma=False
    )
```

```python
import functools
import math

import jax
import jax.numpy as jnp
import numpy as np
from jax import lax
from jax.experimental import pallas as pl
from jax.experimental.pallas import tpu as pltpu
from jax.sharding import PartitionSpec as P

clamp_level = 2.0
target_rms = 0.2
learn_rate = 0.02
lanes = 128
vmem_bytes = 40 * 1024 * 1024


def hadamard(width):
    matrix = np.ones((1, 1), np.float32)
    while matrix.shape[0] < width:
        matrix = np.block([[matrix, matrix], [matrix, -matrix]])
    return matrix


def butterfly(groups):
    half = 1
    groups = list(groups)
    while half < len(groups):
        for start in range(0, len(groups), 2 * half):
            for i in range(start, start + half):
                upper, lower = groups[i], groups[i + half]
                groups[i], groups[i + half] = upper + lower, upper - lower
        half *= 2
    return groups


def rotate_groups(pieces, matrix, base):
    count = pieces[0].shape[1] // base
    groups = []
    for g in range(count):
        part = None
        for piece in pieces:
            term = jnp.dot(
                piece[:, g * base : (g + 1) * base], matrix, preferred_element_type=jnp.float32
            )
            part = term if part is None else part + term
        groups.append(part)
    return butterfly(groups)


def sums_kernel(x_ref, sums_ref):
    owned, width = x_ref.shape[2:]
    rows = x_ref[...].reshape(2 * owned, width).astype(jnp.float32)
    squares = jnp.sum(rows * rows, axis=1, keepdims=True)
    shape = (2 * owned, 2 * owned)
    row, lane = (lax.broadcasted_iota(jnp.int32, shape, axis) for axis in (0, 1))
    line = jnp.sum(jnp.where(row == lane, squares, 0.0), axis=0, keepdims=True)
    sums_ref[...] = jnp.broadcast_to(line, sums_ref.shape)


def scale_rows(sums_ref, offset, owned, width, near):
    biggest = jnp.max(sums_ref[...], axis=0, keepdims=True)
    shape = (owned, 2 * owned)
    row, lane = (lax.broadcasted_iota(jnp.int32, shape, axis) for axis in (0, 1))
    biggest = jnp.sum(jnp.where(lane == row + offset, biggest, 0.0), axis=1, keepdims=True)
    mean = biggest * (1.0 / width)
    scale = jnp.sqrt(mean + 1e-06)
    peak = jnp.sqrt(mean * width) / scale
    step = near * jnp.where(
        peak >= clamp_level, clamp_level / 32768.0, jnp.maximum(peak, 1e-20) / 32767.0
    )
    return scale, step


def add_levels(pieces, scale, sign_ref, matrix_ref, base):
    width = pieces[0].shape[1]
    signs = sign_ref[...].astype(jnp.float32).astype(jnp.bfloat16)
    matrix = matrix_ref[...]
    inverse = (1.0 / math.sqrt(width)) / scale
    totals = None
    for piece in pieces:
        groups = rotate_groups([piece[...] * signs], matrix, base)
        levels = [
            jnp.clip(group * inverse, -clamp_level, clamp_level)
            .astype(jnp.bfloat16)
            .astype(jnp.float32)
            for group in groups
        ]
        totals = levels if totals is None else [t + v for t, v in zip(totals, levels)]
    return totals


def proxy_kernel(near, base, offset_ref, *refs):
    pieces, (sums_ref, sign_ref, matrix_ref, sent_ref) = refs[:near], refs[near:]
    owned, width = sent_ref.shape
    scale, step = scale_rows(sums_ref, owned - offset_ref[0, 0], owned, width, near)
    totals = add_levels(pieces, scale, sign_ref, matrix_ref, base)
    for g, total in enumerate(totals):
        value = jnp.clip(jnp.round(total / step), -32767.0, 32767.0)
        sent_ref[:, g * base : (g + 1) * base] = value.astype(jnp.int16)


def owner_kernel(near, base, offset_ref, *refs):
    pieces, (sums_ref, sign_ref, matrix_ref, total_ref) = refs[:near], refs[near:]
    owned, width = total_ref.shape
    scale, _ = scale_rows(sums_ref, offset_ref[0, 0], owned, width, near)
    totals = add_levels(pieces, scale, sign_ref, matrix_ref, base)
    for g, total in enumerate(totals):
        total_ref[:, g * base : (g + 1) * base] = total


def finish_kernel(
    near, offset_ref, near_ref, far_ref, sums_ref, total_ref, scale_ref, square_ref
):
    owned, width = near_ref.shape
    scale, step = scale_rows(sums_ref, offset_ref[0, 0], owned, width, near)
    total = near_ref[...] + far_ref[...].astype(jnp.float32) * step
    mean_scale = scale / (2 * near)
    mean_rot = total * mean_scale
    squares = jnp.sum(mean_rot * mean_rot)
    square_ref[...] = jnp.full(square_ref.shape, squares, jnp.float32)
    total_ref[...] = total
    scale_ref[...] = jnp.broadcast_to(mean_scale, scale_ref.shape)


def back_kernel(base, total_ref, scale_ref, sign_ref, matrix_ref, unrot_ref):
    owned, width = total_ref.shape
    total = total_ref[...]
    high = total.astype(jnp.bfloat16)
    low = (total - high.astype(jnp.float32)).astype(jnp.bfloat16)
    groups = rotate_groups([high, low], matrix_ref[...], base)
    back = scale_ref[:, 0:1] * (1.0 / math.sqrt(width))
    signs = sign_ref[...].astype(jnp.float32)
    for g, group in enumerate(groups):
        cut = slice(g * base, (g + 1) * base)
        unrot_ref[:, cut] = group * back * signs[:, cut]


def update_kernel(limit, square_ref, unrot_ref, weight_ref, comp_ref, new_ref, update_ref):
    squares = jnp.sum(square_ref[...], axis=0, keepdims=True)[:, 0:1]
    factor = limit / jnp.maximum(jnp.sqrt(squares), limit)
    update = unrot_ref[...] * factor
    update_ref[...] = update
    summed = weight_ref[...].astype(jnp.float32) + (
        comp_ref[...].astype(jnp.float32) - learn_rate * update
    )
    new_ref[...] = summed.astype(jnp.bfloat16)


def swap(value, mask):
    size = lax.axis_size("dp")
    return lax.ppermute(value, "dp", [(i, i ^ mask) for i in range(size)])


def gather_blocks(block, replicas):
    x_count = 1 << ((replicas.bit_length() - 1) // 2)
    near = max(replicas // 2, 1)
    me = lax.axis_index("dp")
    pieces = {0: block}

    def spread(start):
        for z in range(x_count, near, x_count):
            pieces[start + z] = swap(pieces[start], z)
        for z in range(0, near, x_count):
            for x in range(1, min(x_count, near)):
                pieces[start + z + x] = swap(pieces[start + z], x)

    if replicas > 1:
        pieces[near] = swap(block, near)
    spread(0)
    if replicas > 1:
        spread(near)
    owned, width = block.shape
    out = jnp.zeros((replicas, owned, width), block.dtype)
    for mask, piece in pieces.items():
        out = lax.dynamic_update_slice(out, piece[None], (me ^ mask, 0, 0))
    return out.reshape(1, replicas * owned, width)


def on_device(grads, signs, weights, compensation):
    blocks, width = grads.shape[2:]
    replicas = lax.axis_size("dp")
    devices = replicas * lax.axis_size("expert")
    owned = blocks // replicas
    base = min(width, 256)
    matrix = jnp.asarray(hadamard(base), jnp.bfloat16)
    me = lax.axis_index("dp")
    near = replicas // 2
    offset = (me // near * owned).astype(jnp.int32).reshape(1, 1)
    params = pltpu.CompilerParams(vmem_limit_bytes=vmem_bytes)
    scalar = pl.BlockSpec(memory_space=pltpu.SMEM)
    array = pl.BlockSpec(memory_space=pltpu.VMEM)

    def block_of(source, index):
        source = source.reshape(replicas, owned, width)
        return lax.dynamic_slice_in_dim(source, index, 1, 0).reshape(owned, width)

    sums = pl.pallas_call(
        sums_kernel,
        grid=(near,),
        in_specs=[pl.BlockSpec((2, 1, owned, width), lambda j: (0, j, 0, 0))],
        out_specs=pl.BlockSpec((2, 1, 1, 2 * owned), lambda j: (0, j, 0, 0)),
        out_shape=jax.ShapeDtypeStruct((2, near, 1, 2 * owned), jnp.float32),
        compiler_params=params,
        name="sum_squares",
    )(grads.reshape(2, near, owned, width))
    grads, sums = lax.optimization_barrier((grads, sums))
    sums = lax.all_to_all(
        sums.reshape(replicas, 1, 2 * owned), "dp", split_axis=0, concat_axis=0, tiled=True
    ).reshape(replicas, 2 * owned)
    far_pieces = [swap(block_of(grads, me ^ mask ^ near), mask) for mask in range(1, near)]
    far_pieces.append(block_of(grads, me ^ near))
    near_pieces = [swap(block_of(grads, me ^ mask), mask) for mask in range(1, near)]
    near_pieces.append(block_of(grads, me))
    sent = pl.pallas_call(
        functools.partial(proxy_kernel, near, base),
        in_specs=[scalar] + [array] * (near + 3),
        out_shape=jax.ShapeDtypeStruct((owned, width), jnp.int16),
        compiler_params=params,
        name="proxy_blocks",
    )(offset, *far_pieces, sums, signs, matrix)
    far_total = swap(sent, near)
    near_total = pl.pallas_call(
        functools.partial(owner_kernel, near, base),
        in_specs=[scalar] + [array] * (near + 3),
        out_shape=jax.ShapeDtypeStruct((owned, width), jnp.float32),
        compiler_params=params,
        name="owner_blocks",
    )(offset, *near_pieces, sums, signs, matrix)
    total, mean_scale, squares = pl.pallas_call(
        functools.partial(finish_kernel, near),
        in_specs=[scalar] + [array] * 3,
        out_shape=(
            jax.ShapeDtypeStruct((owned, width), jnp.float32),
            jax.ShapeDtypeStruct((owned, lanes), jnp.float32),
            jax.ShapeDtypeStruct((devices, 1, lanes), jnp.float32),
        ),
        compiler_params=params,
        name="finish_blocks",
    )(offset, near_total, far_total, sums)
    unrot = pl.pallas_call(
        functools.partial(back_kernel, base),
        out_shape=jax.ShapeDtypeStruct((owned, width), jnp.float32),
        compiler_params=params,
        name="rotate_back",
    )(total, mean_scale, signs, matrix)
    squares = lax.all_to_all(squares, ("dp", "expert"), split_axis=0, concat_axis=0, tiled=True)
    limit = target_rms * math.sqrt(blocks * width * lax.axis_size("expert"))
    new_weights, update_grad = pl.pallas_call(
        functools.partial(update_kernel, limit),
        out_shape=(
            jax.ShapeDtypeStruct((owned, width), jnp.bfloat16),
            jax.ShapeDtypeStruct((owned, width), jnp.float32),
        ),
        compiler_params=pltpu.CompilerParams(vmem_limit_bytes=vmem_bytes),
        name="update_blocks",
    )(
        squares.reshape(devices, lanes),
        unrot,
        weights.reshape(owned, width),
        compensation.reshape(owned, width),
    )
    return gather_blocks(new_weights, replicas), update_grad.reshape(weights.shape)


def solution(mesh):
    in_specs = (
        P("dp", "expert", None, None),
        P("expert", None),
        P("expert", "dp", None),
        P("expert", "dp", None),
    )
    out_specs = (P("expert", None, None), P("expert", "dp", None))
    return jax.shard_map(
        on_device, mesh=mesh, in_specs=in_specs, out_specs=out_specs, check_vma=False
    )
```

```python
import functools
import math

import jax
import jax.numpy as jnp
import numpy as np
from jax import lax
from jax.experimental import pallas as pl
from jax.experimental.pallas import tpu as pltpu
from jax.sharding import PartitionSpec as P

clamp_level = 2.0
target_rms = 0.2
learn_rate = 0.02
lanes = 128
vmem_bytes = 40 * 1024 * 1024


def hadamard(width):
    matrix = np.ones((1, 1), np.float32)
    while matrix.shape[0] < width:
        matrix = np.block([[matrix, matrix], [matrix, -matrix]])
    return matrix


def butterfly(groups):
    half = 1
    groups = list(groups)
    while half < len(groups):
        for start in range(0, len(groups), 2 * half):
            for i in range(start, start + half):
                upper, lower = groups[i], groups[i + half]
                groups[i], groups[i + half] = upper + lower, upper - lower
        half *= 2
    return groups


def rotate_groups(pieces, matrix, base):
    count = pieces[0].shape[1] // base
    groups = []
    for g in range(count):
        part = None
        for piece in pieces:
            term = jnp.dot(
                piece[:, g * base : (g + 1) * base], matrix, preferred_element_type=jnp.float32
            )
            part = term if part is None else part + term
        groups.append(part)
    return butterfly(groups)


def sums_kernel(x_ref, sums_ref):
    near, owned, width = x_ref.shape[1:]
    shape = (2 * owned, 2 * owned)
    row, lane = (lax.broadcasted_iota(jnp.int32, shape, axis) for axis in (0, 1))
    for j in range(near):
        rows = x_ref[:, j].reshape(2 * owned, width).astype(jnp.float32)
        squares = jnp.sum(rows * rows, axis=1, keepdims=True)
        line = jnp.sum(jnp.where(row == lane, squares, 0.0), axis=0, keepdims=True)
        sums_ref[0, j] = line
        sums_ref[1, j] = line


def scale_rows(sums_ref, offset, owned, width, near):
    biggest = jnp.max(sums_ref[...], axis=0, keepdims=True)
    shape = (owned, 2 * owned)
    row, lane = (lax.broadcasted_iota(jnp.int32, shape, axis) for axis in (0, 1))
    biggest = jnp.sum(jnp.where(lane == row + offset, biggest, 0.0), axis=1, keepdims=True)
    mean = biggest * (1.0 / width)
    scale = jnp.sqrt(mean + 1e-06)
    peak = jnp.sqrt(mean * width) / scale
    step = near * jnp.where(
        peak >= clamp_level, clamp_level / 32768.0, jnp.maximum(peak, 1e-20) / 32767.0
    )
    return scale, step


def add_levels(pieces, scale, sign_ref, matrix_ref, base):
    width = pieces[0].shape[1]
    signs = sign_ref[...].astype(jnp.float32).astype(jnp.bfloat16)
    matrix = matrix_ref[...]
    inverse = (1.0 / math.sqrt(width)) / scale
    totals = None
    for piece in pieces:
        groups = rotate_groups([piece[...] * signs], matrix, base)
        levels = [
            jnp.clip(group * inverse, -clamp_level, clamp_level)
            .astype(jnp.bfloat16)
            .astype(jnp.float32)
            for group in groups
        ]
        totals = levels if totals is None else [t + v for t, v in zip(totals, levels)]
    return totals


def proxy_kernel(near, base, offset_ref, *refs):
    pieces, (sums_ref, sign_ref, matrix_ref, sent_ref) = refs[:near], refs[near:]
    owned, width = sent_ref.shape
    scale, step = scale_rows(sums_ref, owned - offset_ref[0, 0], owned, width, near)
    totals = add_levels(pieces, scale, sign_ref, matrix_ref, base)
    for g, total in enumerate(totals):
        value = jnp.clip(jnp.round(total / step), -32767.0, 32767.0)
        sent_ref[:, g * base : (g + 1) * base] = value.astype(jnp.int16)


def owner_kernel(near, base, offset_ref, *refs):
    pieces, (sums_ref, sign_ref, matrix_ref, total_ref) = refs[:near], refs[near:]
    owned, width = total_ref.shape
    scale, _ = scale_rows(sums_ref, offset_ref[0, 0], owned, width, near)
    totals = add_levels(pieces, scale, sign_ref, matrix_ref, base)
    for g, total in enumerate(totals):
        total_ref[:, g * base : (g + 1) * base] = total


def finish_kernel(
    near, offset_ref, near_ref, far_ref, sums_ref, total_ref, scale_ref, square_ref
):
    owned, width = near_ref.shape
    scale, step = scale_rows(sums_ref, offset_ref[0, 0], owned, width, near)
    total = near_ref[...] + far_ref[...].astype(jnp.float32) * step
    mean_scale = scale / (2 * near)
    mean_rot = total * mean_scale
    squares = jnp.sum(mean_rot * mean_rot)
    square_ref[...] = jnp.full(square_ref.shape, squares, jnp.float32)
    total_ref[...] = total
    scale_ref[...] = jnp.broadcast_to(mean_scale, scale_ref.shape)


def back_kernel(base, total_ref, scale_ref, sign_ref, matrix_ref, unrot_ref):
    owned, width = total_ref.shape
    total = total_ref[...]
    high = total.astype(jnp.bfloat16)
    low = (total - high.astype(jnp.float32)).astype(jnp.bfloat16)
    groups = rotate_groups([high, low], matrix_ref[...], base)
    back = scale_ref[:, 0:1] * (1.0 / math.sqrt(width))
    signs = sign_ref[...].astype(jnp.float32)
    for g, group in enumerate(groups):
        cut = slice(g * base, (g + 1) * base)
        unrot_ref[:, cut] = group * back * signs[:, cut]


def update_kernel(limit, square_ref, unrot_ref, weight_ref, comp_ref, new_ref, update_ref):
    squares = jnp.sum(square_ref[...], axis=0, keepdims=True)[:, 0:1]
    factor = limit / jnp.maximum(jnp.sqrt(squares), limit)
    update = unrot_ref[...] * factor
    update_ref[...] = update
    summed = weight_ref[...].astype(jnp.float32) + (
        comp_ref[...].astype(jnp.float32) - learn_rate * update
    )
    new_ref[...] = summed.astype(jnp.bfloat16)


def swap(value, mask):
    size = lax.axis_size("dp")
    return lax.ppermute(value, "dp", [(i, i ^ mask) for i in range(size)])


def gather_blocks(block, replicas):
    x_count = 1 << ((replicas.bit_length() - 1) // 2)
    near = max(replicas // 2, 1)
    me = lax.axis_index("dp")
    pieces = {0: block}

    def spread(start):
        for z in range(x_count, near, x_count):
            pieces[start + z] = swap(pieces[start], z)
        for z in range(0, near, x_count):
            for x in range(1, min(x_count, near)):
                pieces[start + z + x] = swap(pieces[start + z], x)

    if replicas > 1:
        pieces[near] = swap(block, near)
    spread(0)
    if replicas > 1:
        spread(near)
    owned, width = block.shape
    out = jnp.zeros((replicas, owned, width), block.dtype)
    for mask, piece in pieces.items():
        out = lax.dynamic_update_slice(out, piece[None], (me ^ mask, 0, 0))
    return out.reshape(1, replicas * owned, width)


def on_device(grads, signs, weights, compensation):
    blocks, width = grads.shape[2:]
    replicas = lax.axis_size("dp")
    devices = replicas * lax.axis_size("expert")
    owned = blocks // replicas
    base = min(width, 256)
    matrix = jnp.asarray(hadamard(base), jnp.bfloat16)
    me = lax.axis_index("dp")
    near = replicas // 2
    offset = (me // near * owned).astype(jnp.int32).reshape(1, 1)
    params = pltpu.CompilerParams(vmem_limit_bytes=vmem_bytes)
    scalar = pl.BlockSpec(memory_space=pltpu.SMEM)
    array = pl.BlockSpec(memory_space=pltpu.VMEM)

    def block_of(source, index):
        source = source.reshape(replicas, owned, width)
        return lax.dynamic_slice_in_dim(source, index, 1, 0).reshape(owned, width)

    far_pieces = [swap(block_of(grads, me ^ mask ^ near), mask) for mask in range(1, near)]
    sums = pl.pallas_call(
        sums_kernel,
        in_specs=[array],
        out_shape=jax.ShapeDtypeStruct((2, near, 1, 2 * owned), jnp.float32),
        compiler_params=params,
        name="sum_squares",
    )(grads.reshape(2, near, owned, width))
    later, sums = lax.optimization_barrier((grads, sums))
    sums = lax.all_to_all(
        sums.reshape(replicas, 1, 2 * owned), "dp", split_axis=0, concat_axis=0, tiled=True
    ).reshape(replicas, 2 * owned)
    near_pieces = [swap(block_of(later, me ^ mask), mask) for mask in range(1, near)]
    far_pieces.append(block_of(later, me ^ near))
    near_pieces.append(block_of(later, me))
    sent = pl.pallas_call(
        functools.partial(proxy_kernel, near, base),
        in_specs=[scalar] + [array] * (near + 3),
        out_shape=jax.ShapeDtypeStruct((owned, width), jnp.int16),
        compiler_params=params,
        name="proxy_blocks",
    )(offset, *far_pieces, sums, signs, matrix)
    far_total = swap(sent, near)
    near_total = pl.pallas_call(
        functools.partial(owner_kernel, near, base),
        in_specs=[scalar] + [array] * (near + 3),
        out_shape=jax.ShapeDtypeStruct((owned, width), jnp.float32),
        compiler_params=params,
        name="owner_blocks",
    )(offset, *near_pieces, sums, signs, matrix)
    total, mean_scale, squares = pl.pallas_call(
        functools.partial(finish_kernel, near),
        in_specs=[scalar] + [array] * 3,
        out_shape=(
            jax.ShapeDtypeStruct((owned, width), jnp.float32),
            jax.ShapeDtypeStruct((owned, lanes), jnp.float32),
            jax.ShapeDtypeStruct((devices, 1, lanes), jnp.float32),
        ),
        compiler_params=params,
        name="finish_blocks",
    )(offset, near_total, far_total, sums)
    unrot = pl.pallas_call(
        functools.partial(back_kernel, base),
        out_shape=jax.ShapeDtypeStruct((owned, width), jnp.float32),
        compiler_params=params,
        name="rotate_back",
    )(total, mean_scale, signs, matrix)
    squares = lax.all_to_all(squares, ("dp", "expert"), split_axis=0, concat_axis=0, tiled=True)
    limit = target_rms * math.sqrt(blocks * width * lax.axis_size("expert"))
    new_weights, update_grad = pl.pallas_call(
        functools.partial(update_kernel, limit),
        out_shape=(
            jax.ShapeDtypeStruct((owned, width), jnp.bfloat16),
            jax.ShapeDtypeStruct((owned, width), jnp.float32),
        ),
        compiler_params=pltpu.CompilerParams(vmem_limit_bytes=vmem_bytes),
        name="update_blocks",
    )(
        squares.reshape(devices, lanes),
        unrot,
        weights.reshape(owned, width),
        compensation.reshape(owned, width),
    )
    return gather_blocks(new_weights, replicas), update_grad.reshape(weights.shape)


def solution(mesh):
    in_specs = (
        P("dp", "expert", None, None),
        P("expert", None),
        P("expert", "dp", None),
        P("expert", "dp", None),
    )
    out_specs = (P("expert", None, None), P("expert", "dp", None))
    return jax.shard_map(
        on_device, mesh=mesh, in_specs=in_specs, out_specs=out_specs, check_vma=False
    )
```

```python
import functools
import math

import jax
import jax.numpy as jnp
import numpy as np
from jax import lax
from jax.experimental import pallas as pl
from jax.experimental.pallas import tpu as pltpu
from jax.sharding import PartitionSpec as P

clamp_level = 2.0
target_rms = 0.2
learn_rate = 0.02
lanes = 128
vmem_bytes = 40 * 1024 * 1024


def hadamard(width):
    matrix = np.ones((1, 1), np.float32)
    while matrix.shape[0] < width:
        matrix = np.block([[matrix, matrix], [matrix, -matrix]])
    return matrix


def butterfly(groups):
    half = 1
    groups = list(groups)
    while half < len(groups):
        for start in range(0, len(groups), 2 * half):
            for i in range(start, start + half):
                upper, lower = groups[i], groups[i + half]
                groups[i], groups[i + half] = upper + lower, upper - lower
        half *= 2
    return groups


def rotate_groups(pieces, matrix, base):
    count = pieces[0].shape[1] // base
    groups = []
    for g in range(count):
        part = None
        for piece in pieces:
            term = jnp.dot(
                piece[:, g * base : (g + 1) * base], matrix, preferred_element_type=jnp.float32
            )
            part = term if part is None else part + term
        groups.append(part)
    return butterfly(groups)


def sums_kernel(x_ref, sums_ref):
    near, owned, width = x_ref.shape[1:]
    shape = (2 * owned, 2 * owned)
    row, lane = (lax.broadcasted_iota(jnp.int32, shape, axis) for axis in (0, 1))
    for j in range(near):
        rows = x_ref[:, j].reshape(2 * owned, width).astype(jnp.float32)
        squares = jnp.sum(rows * rows, axis=1, keepdims=True)
        line = jnp.sum(jnp.where(row == lane, squares, 0.0), axis=0, keepdims=True)
        sums_ref[0, j] = line
        sums_ref[1, j] = line


def scale_rows(sums_ref, offset, owned, width, near):
    biggest = jnp.max(sums_ref[...], axis=0, keepdims=True)
    shape = (owned, 2 * owned)
    row, lane = (lax.broadcasted_iota(jnp.int32, shape, axis) for axis in (0, 1))
    biggest = jnp.sum(jnp.where(lane == row + offset, biggest, 0.0), axis=1, keepdims=True)
    mean = biggest * (1.0 / width)
    scale = jnp.sqrt(mean + 1e-06)
    peak = jnp.sqrt(mean * width) / scale
    step = near * jnp.where(
        peak >= clamp_level, clamp_level / 32768.0, jnp.maximum(peak, 1e-20) / 32767.0
    )
    return scale, step


def add_levels(pieces, scale, sign_ref, matrix_ref, base):
    width = pieces[0].shape[1]
    signs = sign_ref[...].astype(jnp.float32).astype(jnp.bfloat16)
    matrix = matrix_ref[...]
    inverse = (1.0 / math.sqrt(width)) / scale
    totals = None
    for piece in pieces:
        groups = rotate_groups([piece[...] * signs], matrix, base)
        levels = [
            jnp.clip(group * inverse, -clamp_level, clamp_level)
            .astype(jnp.bfloat16)
            .astype(jnp.float32)
            for group in groups
        ]
        totals = levels if totals is None else [t + v for t, v in zip(totals, levels)]
    return totals


def proxy_kernel(near, base, offset_ref, *refs):
    pieces, (sums_ref, sign_ref, matrix_ref, sent_ref) = refs[:near], refs[near:]
    owned, width = sent_ref.shape
    scale, step = scale_rows(sums_ref, owned - offset_ref[0, 0], owned, width, near)
    totals = add_levels(pieces, scale, sign_ref, matrix_ref, base)
    for g, total in enumerate(totals):
        value = jnp.clip(jnp.round(total / step), -32767.0, 32767.0)
        sent_ref[:, g * base : (g + 1) * base] = value.astype(jnp.int16)


def owner_kernel(near, base, offset_ref, *refs):
    pieces, (sums_ref, sign_ref, matrix_ref, total_ref) = refs[:near], refs[near:]
    owned, width = total_ref.shape
    scale, _ = scale_rows(sums_ref, offset_ref[0, 0], owned, width, near)
    totals = add_levels(pieces, scale, sign_ref, matrix_ref, base)
    for g, total in enumerate(totals):
        total_ref[:, g * base : (g + 1) * base] = total


def finish_kernel(
    near, offset_ref, near_ref, far_ref, sums_ref, total_ref, scale_ref, square_ref
):
    owned, width = near_ref.shape
    scale, step = scale_rows(sums_ref, offset_ref[0, 0], owned, width, near)
    total = near_ref[...] + far_ref[...].astype(jnp.float32) * step
    mean_scale = scale / (2 * near)
    mean_rot = total * mean_scale
    squares = jnp.sum(mean_rot * mean_rot)
    square_ref[...] = jnp.full(square_ref.shape, squares, jnp.float32)
    total_ref[...] = total
    scale_ref[...] = jnp.broadcast_to(mean_scale, scale_ref.shape)


def back_kernel(base, total_ref, scale_ref, sign_ref, matrix_ref, unrot_ref):
    owned, width = total_ref.shape
    total = total_ref[...]
    high = total.astype(jnp.bfloat16)
    low = (total - high.astype(jnp.float32)).astype(jnp.bfloat16)
    groups = rotate_groups([high, low], matrix_ref[...], base)
    back = scale_ref[:, 0:1] * (1.0 / math.sqrt(width))
    signs = sign_ref[...].astype(jnp.float32)
    for g, group in enumerate(groups):
        cut = slice(g * base, (g + 1) * base)
        unrot_ref[:, cut] = group * back * signs[:, cut]


def update_kernel(limit, square_ref, unrot_ref, weight_ref, comp_ref, new_ref, update_ref):
    squares = jnp.sum(square_ref[...], axis=0, keepdims=True)[:, 0:1]
    factor = limit / jnp.maximum(jnp.sqrt(squares), limit)
    update = unrot_ref[...] * factor
    update_ref[...] = update
    summed = weight_ref[...].astype(jnp.float32) + (
        comp_ref[...].astype(jnp.float32) - learn_rate * update
    )
    new_ref[...] = summed.astype(jnp.bfloat16)


def swap(value, mask):
    size = lax.axis_size("dp")
    return lax.ppermute(value, "dp", [(i, i ^ mask) for i in range(size)])


def gather_blocks(block, replicas):
    x_count = 1 << ((replicas.bit_length() - 1) // 2)
    near = replicas // 2
    me = lax.axis_index("dp")
    owned, width = block.shape
    parts = 2 if owned % 32 == 0 else 1
    rows = owned // parts
    pieces = []

    def spread(start, piece, row):
        pieces.append((start, row, piece))
        along = {0: piece}
        for z in range(x_count, near, x_count):
            along[z] = swap(piece, z)
            pieces.append((start + z, row, along[z]))
        for z in range(0, near, x_count):
            for x in range(1, x_count):
                pieces.append((start + z + x, row, swap(along[z], x)))

    across = [swap(block[p * rows : (p + 1) * rows], near) for p in range(parts)]
    spread(0, block, 0)
    for p, piece in enumerate(across):
        spread(near, piece, p * rows)
    out = jnp.zeros((replicas, owned, width), block.dtype)
    for mask, row, piece in pieces:
        out = lax.dynamic_update_slice(out, piece[None], (me ^ mask, row, 0))
    return out.reshape(1, replicas * owned, width)


def on_device(grads, signs, weights, compensation):
    blocks, width = grads.shape[2:]
    replicas = lax.axis_size("dp")
    devices = replicas * lax.axis_size("expert")
    owned = blocks // replicas
    base = min(width, 256)
    matrix = jnp.asarray(hadamard(base), jnp.bfloat16)
    me = lax.axis_index("dp")
    near = replicas // 2
    offset = (me // near * owned).astype(jnp.int32).reshape(1, 1)
    params = pltpu.CompilerParams(vmem_limit_bytes=vmem_bytes)
    scalar = pl.BlockSpec(memory_space=pltpu.SMEM)
    array = pl.BlockSpec(memory_space=pltpu.VMEM)

    def block_of(source, index):
        source = source.reshape(replicas, owned, width)
        return lax.dynamic_slice_in_dim(source, index, 1, 0).reshape(owned, width)

    far_pieces = [swap(block_of(grads, me ^ mask ^ near), mask) for mask in range(1, near)]
    sums = pl.pallas_call(
        sums_kernel,
        in_specs=[array],
        out_shape=jax.ShapeDtypeStruct((2, near, 1, 2 * owned), jnp.float32),
        compiler_params=params,
        name="sum_squares",
    )(grads.reshape(2, near, owned, width))
    later, sums = lax.optimization_barrier((grads, sums))
    sums = lax.all_to_all(
        sums.reshape(replicas, 1, 2 * owned), "dp", split_axis=0, concat_axis=0, tiled=True
    ).reshape(replicas, 2 * owned)
    near_pieces = [swap(block_of(later, me ^ mask), mask) for mask in range(1, near)]
    far_pieces.append(block_of(later, me ^ near))
    near_pieces.append(block_of(later, me))
    sent = pl.pallas_call(
        functools.partial(proxy_kernel, near, base),
        in_specs=[scalar] + [array] * (near + 3),
        out_shape=jax.ShapeDtypeStruct((owned, width), jnp.int16),
        compiler_params=params,
        name="proxy_blocks",
    )(offset, *far_pieces, sums, signs, matrix)
    far_total = swap(sent, near)
    near_total = pl.pallas_call(
        functools.partial(owner_kernel, near, base),
        in_specs=[scalar] + [array] * (near + 3),
        out_shape=jax.ShapeDtypeStruct((owned, width), jnp.float32),
        compiler_params=params,
        name="owner_blocks",
    )(offset, *near_pieces, sums, signs, matrix)
    total, mean_scale, squares = pl.pallas_call(
        functools.partial(finish_kernel, near),
        in_specs=[scalar] + [array] * 3,
        out_shape=(
            jax.ShapeDtypeStruct((owned, width), jnp.float32),
            jax.ShapeDtypeStruct((owned, lanes), jnp.float32),
            jax.ShapeDtypeStruct((devices, 1, lanes), jnp.float32),
        ),
        compiler_params=params,
        name="finish_blocks",
    )(offset, near_total, far_total, sums)
    unrot = pl.pallas_call(
        functools.partial(back_kernel, base),
        out_shape=jax.ShapeDtypeStruct((owned, width), jnp.float32),
        compiler_params=params,
        name="rotate_back",
    )(total, mean_scale, signs, matrix)
    squares = lax.all_to_all(squares, ("dp", "expert"), split_axis=0, concat_axis=0, tiled=True)
    limit = target_rms * math.sqrt(blocks * width * lax.axis_size("expert"))
    new_weights, update_grad = pl.pallas_call(
        functools.partial(update_kernel, limit),
        out_shape=(
            jax.ShapeDtypeStruct((owned, width), jnp.bfloat16),
            jax.ShapeDtypeStruct((owned, width), jnp.float32),
        ),
        compiler_params=pltpu.CompilerParams(vmem_limit_bytes=vmem_bytes),
        name="update_blocks",
    )(
        squares.reshape(devices, lanes),
        unrot,
        weights.reshape(owned, width),
        compensation.reshape(owned, width),
    )
    return gather_blocks(new_weights, replicas), update_grad.reshape(weights.shape)


def solution(mesh):
    in_specs = (
        P("dp", "expert", None, None),
        P("expert", None),
        P("expert", "dp", None),
        P("expert", "dp", None),
    )
    out_specs = (P("expert", None, None), P("expert", "dp", None))
    return jax.shard_map(
        on_device, mesh=mesh, in_specs=in_specs, out_specs=out_specs, check_vma=False
    )
```

```python
import functools
import math

import jax
import jax.numpy as jnp
import numpy as np
from jax import lax
from jax.experimental import pallas as pl
from jax.experimental.pallas import tpu as pltpu
from jax.sharding import PartitionSpec as P

clamp_level = 2.0
target_rms = 0.2
learn_rate = 0.02
lanes = 128
vmem_bytes = 40 * 1024 * 1024


def hadamard(width):
    matrix = np.ones((1, 1), np.float32)
    while matrix.shape[0] < width:
        matrix = np.block([[matrix, matrix], [matrix, -matrix]])
    return matrix


def butterfly(groups):
    half = 1
    groups = list(groups)
    while half < len(groups):
        for start in range(0, len(groups), 2 * half):
            for i in range(start, start + half):
                upper, lower = groups[i], groups[i + half]
                groups[i], groups[i + half] = upper + lower, upper - lower
        half *= 2
    return groups


def rotate_groups(pieces, matrix, base):
    count = pieces[0].shape[1] // base
    groups = []
    for g in range(count):
        part = None
        for piece in pieces:
            term = jnp.dot(
                piece[:, g * base : (g + 1) * base], matrix, preferred_element_type=jnp.float32
            )
            part = term if part is None else part + term
        groups.append(part)
    return butterfly(groups)


def sums_kernel(x_ref, sums_ref):
    near, owned, width = x_ref.shape[1:]
    shape = (2 * owned, 2 * owned)
    row, lane = (lax.broadcasted_iota(jnp.int32, shape, axis) for axis in (0, 1))
    for j in range(near):
        rows = x_ref[:, j].reshape(2 * owned, width).astype(jnp.float32)
        squares = jnp.sum(rows * rows, axis=1, keepdims=True)
        line = jnp.sum(jnp.where(row == lane, squares, 0.0), axis=0, keepdims=True)
        sums_ref[0, j] = line
        sums_ref[1, j] = line


def scale_rows(sums_ref, offset, owned, width, near):
    biggest = jnp.max(sums_ref[...], axis=0, keepdims=True)
    shape = (owned, 2 * owned)
    row, lane = (lax.broadcasted_iota(jnp.int32, shape, axis) for axis in (0, 1))
    biggest = jnp.sum(jnp.where(lane == row + offset, biggest, 0.0), axis=1, keepdims=True)
    mean = biggest * (1.0 / width)
    scale = jnp.sqrt(mean + 1e-06)
    peak = jnp.sqrt(mean * width) / scale
    step = near * jnp.where(
        peak >= clamp_level, clamp_level / 32768.0, jnp.maximum(peak, 1e-20) / 32767.0
    )
    return scale, step


def add_levels(pieces, half, scale, sign_ref, matrix_ref, base):
    width = pieces[0].shape[2]
    signs = sign_ref[...].astype(jnp.float32).astype(jnp.bfloat16)
    matrix = matrix_ref[...]
    inverse = (1.0 / math.sqrt(width)) / scale
    totals = None
    for piece in pieces:
        groups = rotate_groups([piece[half] * signs], matrix, base)
        levels = [
            jnp.clip(group * inverse, -clamp_level, clamp_level)
            .astype(jnp.bfloat16)
            .astype(jnp.float32)
            for group in groups
        ]
        totals = levels if totals is None else [t + v for t, v in zip(totals, levels)]
    return totals


def proxy_kernel(near, base, half_ref, *refs):
    pieces, (sums_ref, sign_ref, matrix_ref, sent_ref) = refs[:near], refs[near:]
    owned, width = sent_ref.shape
    half = 1 - half_ref[0, 0]
    scale, step = scale_rows(sums_ref, half * owned, owned, width, near)
    totals = add_levels(pieces, half, scale, sign_ref, matrix_ref, base)
    for g, total in enumerate(totals):
        value = jnp.clip(jnp.round(total / step), -32767.0, 32767.0)
        sent_ref[:, g * base : (g + 1) * base] = value.astype(jnp.int16)


def owner_kernel(near, base, half_ref, *refs):
    pieces, (sums_ref, sign_ref, matrix_ref, total_ref) = refs[:near], refs[near:]
    owned, width = total_ref.shape
    half = half_ref[0, 0]
    scale, _ = scale_rows(sums_ref, half * owned, owned, width, near)
    totals = add_levels(pieces, half, scale, sign_ref, matrix_ref, base)
    for g, total in enumerate(totals):
        total_ref[:, g * base : (g + 1) * base] = total


def finish_kernel(
    near, half_ref, near_ref, far_ref, sums_ref, total_ref, scale_ref, square_ref
):
    owned, width = near_ref.shape
    scale, step = scale_rows(sums_ref, half_ref[0, 0] * owned, owned, width, near)
    total = near_ref[...] + far_ref[...].astype(jnp.float32) * step
    mean_scale = scale / (2 * near)
    mean_rot = total * mean_scale
    squares = jnp.sum(mean_rot * mean_rot)
    square_ref[...] = jnp.full(square_ref.shape, squares, jnp.float32)
    total_ref[...] = total
    scale_ref[...] = jnp.broadcast_to(mean_scale, scale_ref.shape)


def back_kernel(base, total_ref, scale_ref, sign_ref, matrix_ref, unrot_ref):
    owned, width = total_ref.shape
    total = total_ref[...]
    high = total.astype(jnp.bfloat16)
    low = (total - high.astype(jnp.float32)).astype(jnp.bfloat16)
    groups = rotate_groups([high, low], matrix_ref[...], base)
    back = scale_ref[:, 0:1] * (1.0 / math.sqrt(width))
    signs = sign_ref[...].astype(jnp.float32)
    for g, group in enumerate(groups):
        cut = slice(g * base, (g + 1) * base)
        unrot_ref[:, cut] = group * back * signs[:, cut]


def update_kernel(limit, square_ref, unrot_ref, weight_ref, comp_ref, new_ref, update_ref):
    squares = jnp.sum(square_ref[...], axis=0, keepdims=True)[:, 0:1]
    factor = limit / jnp.maximum(jnp.sqrt(squares), limit)
    update = unrot_ref[...] * factor
    update_ref[...] = update
    summed = weight_ref[...].astype(jnp.float32) + (
        comp_ref[...].astype(jnp.float32) - learn_rate * update
    )
    new_ref[...] = summed.astype(jnp.bfloat16)


def swap(value, mask):
    size = lax.axis_size("dp")
    return lax.ppermute(value, "dp", [(i, i ^ mask) for i in range(size)])


def gather_blocks(block, replicas):
    x_count = 1 << ((replicas.bit_length() - 1) // 2)
    near = replicas // 2
    me = lax.axis_index("dp")
    owned, width = block.shape
    parts = 2 if owned % 32 == 0 else 1
    rows = owned // parts
    pieces = []

    def spread(start, piece, row):
        pieces.append((start, row, piece))
        along = {0: piece}
        for z in range(x_count, near, x_count):
            along[z] = swap(piece, z)
            pieces.append((start + z, row, along[z]))
        for z in range(0, near, x_count):
            for x in range(1, x_count):
                pieces.append((start + z + x, row, swap(along[z], x)))

    across = [swap(block[p * rows : (p + 1) * rows], near) for p in range(parts)]
    spread(0, block, 0)
    for p, piece in enumerate(across):
        spread(near, piece, p * rows)
    out = jnp.zeros((replicas, owned, width), block.dtype)
    for mask, row, piece in pieces:
        out = lax.dynamic_update_slice(out, piece[None], (me ^ mask, row, 0))
    return out.reshape(1, replicas * owned, width)


def on_device(grads, signs, weights, compensation):
    blocks, width = grads.shape[2:]
    replicas = lax.axis_size("dp")
    devices = replicas * lax.axis_size("expert")
    owned = blocks // replicas
    base = min(width, 256)
    matrix = jnp.asarray(hadamard(base), jnp.bfloat16)
    me = lax.axis_index("dp")
    near = replicas // 2
    half = (me // near).astype(jnp.int32).reshape(1, 1)
    params = pltpu.CompilerParams(vmem_limit_bytes=vmem_bytes)
    scalar = pl.BlockSpec(memory_space=pltpu.SMEM)
    array = pl.BlockSpec(memory_space=pltpu.VMEM)

    halves = grads.reshape(2, near, owned, width)

    def pair_of(index):
        return lax.dynamic_slice_in_dim(halves, index % near, 1, 1).reshape(2, owned, width)

    pieces = [swap(pair_of(me ^ mask), mask) for mask in range(1, near)] + [pair_of(me)]
    sums = pl.pallas_call(
        sums_kernel,
        in_specs=[array],
        out_shape=jax.ShapeDtypeStruct((2, near, 1, 2 * owned), jnp.float32),
        compiler_params=params,
        name="sum_squares",
    )(halves)
    sums = lax.all_to_all(
        sums.reshape(replicas, 1, 2 * owned), "dp", split_axis=0, concat_axis=0, tiled=True
    ).reshape(replicas, 2 * owned)
    sent = pl.pallas_call(
        functools.partial(proxy_kernel, near, base),
        in_specs=[scalar] + [array] * (near + 3),
        out_shape=jax.ShapeDtypeStruct((owned, width), jnp.int16),
        compiler_params=params,
        name="proxy_blocks",
    )(half, *pieces, sums, signs, matrix)
    far_total = swap(sent, near)
    near_total = pl.pallas_call(
        functools.partial(owner_kernel, near, base),
        in_specs=[scalar] + [array] * (near + 3),
        out_shape=jax.ShapeDtypeStruct((owned, width), jnp.float32),
        compiler_params=params,
        name="owner_blocks",
    )(half, *pieces, sums, signs, matrix)
    total, mean_scale, squares = pl.pallas_call(
        functools.partial(finish_kernel, near),
        in_specs=[scalar] + [array] * 3,
        out_shape=(
            jax.ShapeDtypeStruct((owned, width), jnp.float32),
            jax.ShapeDtypeStruct((owned, lanes), jnp.float32),
            jax.ShapeDtypeStruct((devices, 1, lanes), jnp.float32),
        ),
        compiler_params=params,
        name="finish_blocks",
    )(half, near_total, far_total, sums)
    unrot = pl.pallas_call(
        functools.partial(back_kernel, base),
        out_shape=jax.ShapeDtypeStruct((owned, width), jnp.float32),
        compiler_params=params,
        name="rotate_back",
    )(total, mean_scale, signs, matrix)
    squares = lax.all_to_all(squares, ("dp", "expert"), split_axis=0, concat_axis=0, tiled=True)
    limit = target_rms * math.sqrt(blocks * width * lax.axis_size("expert"))
    new_weights, update_grad = pl.pallas_call(
        functools.partial(update_kernel, limit),
        out_shape=(
            jax.ShapeDtypeStruct((owned, width), jnp.bfloat16),
            jax.ShapeDtypeStruct((owned, width), jnp.float32),
        ),
        compiler_params=pltpu.CompilerParams(vmem_limit_bytes=vmem_bytes),
        name="update_blocks",
    )(
        squares.reshape(devices, lanes),
        unrot,
        weights.reshape(owned, width),
        compensation.reshape(owned, width),
    )
    return gather_blocks(new_weights, replicas), update_grad.reshape(weights.shape)


def solution(mesh):
    in_specs = (
        P("dp", "expert", None, None),
        P("expert", None),
        P("expert", "dp", None),
        P("expert", "dp", None),
    )
    out_specs = (P("expert", None, None), P("expert", "dp", None))
    return jax.shard_map(
        on_device, mesh=mesh, in_specs=in_specs, out_specs=out_specs, check_vma=False
    )
```

```python
import functools
import math

import jax
import jax.numpy as jnp
import numpy as np
from jax import lax
from jax.experimental import pallas as pl
from jax.experimental.pallas import tpu as pltpu
from jax.sharding import PartitionSpec as P

clamp_level = 2.0
target_rms = 0.2
learn_rate = 0.02
lanes = 128
vmem_bytes = 40 * 1024 * 1024


def hadamard(width):
    matrix = np.ones((1, 1), np.float32)
    while matrix.shape[0] < width:
        matrix = np.block([[matrix, matrix], [matrix, -matrix]])
    return matrix


def butterfly(groups):
    half = 1
    groups = list(groups)
    while half < len(groups):
        for start in range(0, len(groups), 2 * half):
            for i in range(start, start + half):
                upper, lower = groups[i], groups[i + half]
                groups[i], groups[i + half] = upper + lower, upper - lower
        half *= 2
    return groups


def rotate_groups(pieces, matrix, base):
    count = pieces[0].shape[1] // base
    groups = []
    for g in range(count):
        part = None
        for piece in pieces:
            term = jnp.dot(
                piece[:, g * base : (g + 1) * base], matrix, preferred_element_type=jnp.float32
            )
            part = term if part is None else part + term
        groups.append(part)
    return butterfly(groups)


def sums_kernel(x_ref, sums_ref):
    near, owned, width = x_ref.shape[1:]
    shape = (2 * owned, 2 * owned)
    row, lane = (lax.broadcasted_iota(jnp.int32, shape, axis) for axis in (0, 1))
    for j in range(near):
        rows = x_ref[:, j].reshape(2 * owned, width).astype(jnp.float32)
        squares = jnp.sum(rows * rows, axis=1, keepdims=True)
        line = jnp.sum(jnp.where(row == lane, squares, 0.0), axis=0, keepdims=True)
        sums_ref[0, j] = line
        sums_ref[1, j] = line


def scale_rows(sums_ref, offset, owned, width, near):
    biggest = jnp.max(sums_ref[...], axis=0, keepdims=True)
    shape = (owned, 2 * owned)
    row, lane = (lax.broadcasted_iota(jnp.int32, shape, axis) for axis in (0, 1))
    biggest = jnp.sum(jnp.where(lane == row + offset, biggest, 0.0), axis=1, keepdims=True)
    mean = biggest * (1.0 / width)
    scale = jnp.sqrt(mean + 1e-06)
    peak = jnp.sqrt(mean * width) / scale
    step = near * jnp.where(
        peak >= clamp_level, clamp_level / 32768.0, jnp.maximum(peak, 1e-20) / 32767.0
    )
    return scale, step


def add_levels(pieces, half, scale, sign_ref, matrix_ref, base):
    width = pieces[0].shape[2]
    signs = sign_ref[...].astype(jnp.float32).astype(jnp.bfloat16)
    matrix = matrix_ref[...]
    inverse = (1.0 / math.sqrt(width)) / scale
    totals = None
    for piece in pieces:
        groups = rotate_groups([piece[half] * signs], matrix, base)
        levels = [
            jnp.clip(group * inverse, -clamp_level, clamp_level)
            .astype(jnp.bfloat16)
            .astype(jnp.float32)
            for group in groups
        ]
        totals = levels if totals is None else [t + v for t, v in zip(totals, levels)]
    return totals


def proxy_kernel(near, base, half_ref, *refs):
    pieces, (sums_ref, sign_ref, matrix_ref, sent_ref) = refs[:near], refs[near:]
    owned, width = sent_ref.shape
    half = 1 - half_ref[0, 0]
    scale, step = scale_rows(sums_ref, half * owned, owned, width, near)
    totals = add_levels(pieces, half, scale, sign_ref, matrix_ref, base)
    for g, total in enumerate(totals):
        value = jnp.clip(jnp.round(total / step), -32767.0, 32767.0)
        sent_ref[:, g * base : (g + 1) * base] = value.astype(jnp.int16)


def owner_kernel(near, base, half_ref, *refs):
    pieces, (sums_ref, sign_ref, matrix_ref, total_ref) = refs[:near], refs[near:]
    owned, width = total_ref.shape
    half = half_ref[0, 0]
    scale, _ = scale_rows(sums_ref, half * owned, owned, width, near)
    totals = add_levels(pieces, half, scale, sign_ref, matrix_ref, base)
    for g, total in enumerate(totals):
        total_ref[:, g * base : (g + 1) * base] = total


def finish_kernel(
    near, half_ref, near_ref, far_ref, sums_ref, total_ref, scale_ref, square_ref
):
    owned, width = near_ref.shape
    scale, step = scale_rows(sums_ref, half_ref[0, 0] * owned, owned, width, near)
    total = near_ref[...] + far_ref[...].astype(jnp.float32) * step
    mean_scale = scale / (2 * near)
    mean_rot = total * mean_scale
    squares = jnp.sum(mean_rot * mean_rot)
    square_ref[...] = jnp.full(square_ref.shape, squares, jnp.float32)
    total_ref[...] = total
    scale_ref[...] = jnp.broadcast_to(mean_scale, scale_ref.shape)


def back_kernel(base, total_ref, scale_ref, sign_ref, matrix_ref, unrot_ref):
    owned, width = total_ref.shape
    total = total_ref[...]
    high = total.astype(jnp.bfloat16)
    low = (total - high.astype(jnp.float32)).astype(jnp.bfloat16)
    groups = rotate_groups([high, low], matrix_ref[...], base)
    back = scale_ref[:, 0:1] * (1.0 / math.sqrt(width))
    signs = sign_ref[...].astype(jnp.float32)
    for g, group in enumerate(groups):
        cut = slice(g * base, (g + 1) * base)
        unrot_ref[:, cut] = group * back * signs[:, cut]


def update_kernel(limit, square_ref, unrot_ref, weight_ref, comp_ref, new_ref, update_ref):
    squares = jnp.sum(square_ref[...], axis=0, keepdims=True)[:, 0:1]
    factor = limit / jnp.maximum(jnp.sqrt(squares), limit)
    update = unrot_ref[...] * factor
    update_ref[...] = update
    summed = weight_ref[...].astype(jnp.float32) + (
        comp_ref[...].astype(jnp.float32) - learn_rate * update
    )
    new_ref[...] = summed.astype(jnp.bfloat16)


def swap(value, even, odd=None):
    odd = even if odd is None else odd
    size, experts = lax.axis_size("dp"), lax.axis_size("expert")
    pairs = []
    for i in range(size):
        for e in range(experts):
            mask = odd if e % 2 else even
            pairs.append((i * experts + e, (i ^ mask) * experts + e))
    return lax.ppermute(value, ("dp", "expert"), pairs)


def near_masks(replicas):
    x_count = 1 << ((replicas.bit_length() - 1) // 2)
    z_count = replicas // 2 // x_count
    along_x = list(range(1, x_count))
    along_z = [z * x_count for z in range(1, z_count)]
    if len(along_x) == len(along_z):
        return along_z, along_x, along_x, along_z
    return along_z, along_x, along_z, along_x


def gather_blocks(block, replicas):
    near = replicas // 2
    me = lax.axis_index("dp")
    odd = lax.axis_index("expert") % 2 == 1
    owned, width = block.shape
    first_even, second_even, first_odd, second_odd = near_masks(replicas)
    pieces = []

    def keep(even_mask, odd_mask, piece):
        pieces.append((jnp.where(odd, me ^ odd_mask, me ^ even_mask), piece))

    def spread(start, piece):
        keep(start, start, piece)
        firsts = [(a, b, swap(piece, a, b)) for a, b in zip(first_even, first_odd)]
        for a, b, value in firsts:
            keep(start + a, start + b, value)
        for c, d in zip(second_even, second_odd):
            keep(start + c, start + d, swap(piece, c, d))
        for a, b, value in firsts:
            for c, d in zip(second_even, second_odd):
                keep(start + a + c, start + b + d, swap(value, c, d))

    across = swap(block, near)
    spread(0, block)
    spread(near, across)
    out = jnp.zeros((replicas, owned, width), block.dtype)
    for index, piece in pieces:
        out = lax.dynamic_update_slice(out, piece[None], (index, 0, 0))
    return out.reshape(1, replicas * owned, width)


def on_device(grads, signs, weights, compensation):
    blocks, width = grads.shape[2:]
    replicas = lax.axis_size("dp")
    devices = replicas * lax.axis_size("expert")
    owned = blocks // replicas
    base = min(width, 256)
    matrix = jnp.asarray(hadamard(base), jnp.bfloat16)
    me = lax.axis_index("dp")
    near = replicas // 2
    half = (me // near).astype(jnp.int32).reshape(1, 1)
    params = pltpu.CompilerParams(vmem_limit_bytes=vmem_bytes)
    scalar = pl.BlockSpec(memory_space=pltpu.SMEM)
    array = pl.BlockSpec(memory_space=pltpu.VMEM)

    halves = grads.reshape(2, near, owned, width)

    def pair_of(index):
        return lax.dynamic_slice_in_dim(halves, index % near, 1, 1).reshape(2, owned, width)

    odd = lax.axis_index("expert") % 2 == 1

    def pair_to(even, odd_mask):
        return swap(pair_of(jnp.where(odd, me ^ odd_mask, me ^ even)), even, odd_mask)

    first_even, second_even, first_odd, second_odd = near_masks(replicas)
    pieces = [pair_to(a, b) for a, b in zip(first_even, first_odd)]
    pieces += [pair_to(c, d) for c, d in zip(second_even, second_odd)]
    pieces += [pair_to(a + c, a + c) for a in first_even for c in second_even]
    pieces.append(pair_of(me))
    sums = pl.pallas_call(
        sums_kernel,
        in_specs=[array],
        out_shape=jax.ShapeDtypeStruct((2, near, 1, 2 * owned), jnp.float32),
        compiler_params=params,
        name="sum_squares",
    )(halves)
    sums = lax.all_to_all(
        sums.reshape(replicas, 1, 2 * owned), "dp", split_axis=0, concat_axis=0, tiled=True
    ).reshape(replicas, 2 * owned)
    sent = pl.pallas_call(
        functools.partial(proxy_kernel, near, base),
        in_specs=[scalar] + [array] * (near + 3),
        out_shape=jax.ShapeDtypeStruct((owned, width), jnp.int16),
        compiler_params=params,
        name="proxy_blocks",
    )(half, *pieces, sums, signs, matrix)
    far_total = swap(sent, near)
    near_total = pl.pallas_call(
        functools.partial(owner_kernel, near, base),
        in_specs=[scalar] + [array] * (near + 3),
        out_shape=jax.ShapeDtypeStruct((owned, width), jnp.float32),
        compiler_params=params,
        name="owner_blocks",
    )(half, *pieces, sums, signs, matrix)
    total, mean_scale, squares = pl.pallas_call(
        functools.partial(finish_kernel, near),
        in_specs=[scalar] + [array] * 3,
        out_shape=(
            jax.ShapeDtypeStruct((owned, width), jnp.float32),
            jax.ShapeDtypeStruct((owned, lanes), jnp.float32),
            jax.ShapeDtypeStruct((devices, 1, lanes), jnp.float32),
        ),
        compiler_params=params,
        name="finish_blocks",
    )(half, near_total, far_total, sums)
    unrot = pl.pallas_call(
        functools.partial(back_kernel, base),
        out_shape=jax.ShapeDtypeStruct((owned, width), jnp.float32),
        compiler_params=params,
        name="rotate_back",
    )(total, mean_scale, signs, matrix)
    squares = lax.all_to_all(squares, ("dp", "expert"), split_axis=0, concat_axis=0, tiled=True)
    limit = target_rms * math.sqrt(blocks * width * lax.axis_size("expert"))
    new_weights, update_grad = pl.pallas_call(
        functools.partial(update_kernel, limit),
        out_shape=(
            jax.ShapeDtypeStruct((owned, width), jnp.bfloat16),
            jax.ShapeDtypeStruct((owned, width), jnp.float32),
        ),
        compiler_params=pltpu.CompilerParams(vmem_limit_bytes=vmem_bytes),
        name="update_blocks",
    )(
        squares.reshape(devices, lanes),
        unrot,
        weights.reshape(owned, width),
        compensation.reshape(owned, width),
    )
    return gather_blocks(new_weights, replicas), update_grad.reshape(weights.shape)


def solution(mesh):
    in_specs = (
        P("dp", "expert", None, None),
        P("expert", None),
        P("expert", "dp", None),
        P("expert", "dp", None),
    )
    out_specs = (P("expert", None, None), P("expert", "dp", None))
    return jax.shard_map(
        on_device, mesh=mesh, in_specs=in_specs, out_specs=out_specs, check_vma=False
    )
```

```python
import functools
import math

import jax
import jax.numpy as jnp
import numpy as np
from jax import lax
from jax.experimental import pallas as pl
from jax.experimental.pallas import tpu as pltpu
from jax.sharding import PartitionSpec as P

clamp_level = 2.0
target_rms = 0.2
learn_rate = 0.02
lanes = 128
vmem_bytes = 40 * 1024 * 1024


def hadamard(width):
    matrix = np.ones((1, 1), np.float32)
    while matrix.shape[0] < width:
        matrix = np.block([[matrix, matrix], [matrix, -matrix]])
    return matrix


def butterfly(groups):
    half = 1
    groups = list(groups)
    while half < len(groups):
        for start in range(0, len(groups), 2 * half):
            for i in range(start, start + half):
                upper, lower = groups[i], groups[i + half]
                groups[i], groups[i + half] = upper + lower, upper - lower
        half *= 2
    return groups


def rotate_groups(pieces, matrix, base):
    count = pieces[0].shape[1] // base
    groups = []
    for g in range(count):
        part = None
        for piece in pieces:
            term = jnp.dot(
                piece[:, g * base : (g + 1) * base], matrix, preferred_element_type=jnp.float32
            )
            part = term if part is None else part + term
        groups.append(part)
    return butterfly(groups)


def sums_kernel(x_ref, sums_ref):
    near, owned, width = x_ref.shape[1:]
    shape = (2 * owned, 2 * owned)
    row, lane = (lax.broadcasted_iota(jnp.int32, shape, axis) for axis in (0, 1))
    for j in range(near):
        rows = x_ref[:, j].reshape(2 * owned, width).astype(jnp.float32)
        squares = jnp.sum(rows * rows, axis=1, keepdims=True)
        line = jnp.sum(jnp.where(row == lane, squares, 0.0), axis=0, keepdims=True)
        sums_ref[0, j] = line
        sums_ref[1, j] = line


def scale_rows(sums_ref, offset, owned, width, near):
    biggest = jnp.max(sums_ref[...], axis=0, keepdims=True)
    shape = (owned, 2 * owned)
    row, lane = (lax.broadcasted_iota(jnp.int32, shape, axis) for axis in (0, 1))
    biggest = jnp.sum(jnp.where(lane == row + offset, biggest, 0.0), axis=1, keepdims=True)
    mean = biggest * (1.0 / width)
    scale = jnp.sqrt(mean + 1e-06)
    peak = jnp.sqrt(mean * width) / scale
    step = near * jnp.where(
        peak >= clamp_level, clamp_level / 32768.0, jnp.maximum(peak, 1e-20) / 32767.0
    )
    return scale, step


def add_levels(pieces, scale, sign_ref, matrix_ref, base):
    width = pieces[0].shape[1]
    signs = sign_ref[...].astype(jnp.float32).astype(jnp.bfloat16)
    matrix = matrix_ref[...]
    inverse = (1.0 / math.sqrt(width)) / scale
    totals = None
    for piece in pieces:
        groups = rotate_groups([piece[...] * signs], matrix, base)
        levels = [
            jnp.clip(group * inverse, -clamp_level, clamp_level)
            .astype(jnp.bfloat16)
            .astype(jnp.float32)
            for group in groups
        ]
        totals = levels if totals is None else [t + v for t, v in zip(totals, levels)]
    return totals


def proxy_kernel(near, base, offset_ref, *refs):
    pieces, (sums_ref, sign_ref, matrix_ref, sent_ref) = refs[:near], refs[near:]
    owned, width = sent_ref.shape
    scale, step = scale_rows(sums_ref, owned - offset_ref[0, 0], owned, width, near)
    totals = add_levels(pieces, scale, sign_ref, matrix_ref, base)
    for g, total in enumerate(totals):
        value = jnp.clip(jnp.round(total / step), -32767.0, 32767.0)
        sent_ref[:, g * base : (g + 1) * base] = value.astype(jnp.int16)


def owner_kernel(near, base, offset_ref, *refs):
    pieces, (sums_ref, sign_ref, matrix_ref, total_ref) = refs[:near], refs[near:]
    owned, width = total_ref.shape
    scale, _ = scale_rows(sums_ref, offset_ref[0, 0], owned, width, near)
    totals = add_levels(pieces, scale, sign_ref, matrix_ref, base)
    for g, total in enumerate(totals):
        total_ref[:, g * base : (g + 1) * base] = total


def finish_kernel(
    near, offset_ref, near_ref, far_ref, sums_ref, total_ref, scale_ref, square_ref
):
    owned, width = near_ref.shape
    scale, step = scale_rows(sums_ref, offset_ref[0, 0], owned, width, near)
    total = near_ref[...] + far_ref[...].astype(jnp.float32) * step
    mean_scale = scale / (2 * near)
    mean_rot = total * mean_scale
    squares = jnp.sum(mean_rot * mean_rot)
    square_ref[...] = jnp.full(square_ref.shape, squares, jnp.float32)
    total_ref[...] = total
    scale_ref[...] = jnp.broadcast_to(mean_scale, scale_ref.shape)


def back_kernel(base, total_ref, scale_ref, sign_ref, matrix_ref, unrot_ref):
    owned, width = total_ref.shape
    total = total_ref[...]
    high = total.astype(jnp.bfloat16)
    low = (total - high.astype(jnp.float32)).astype(jnp.bfloat16)
    groups = rotate_groups([high, low], matrix_ref[...], base)
    back = scale_ref[:, 0:1] * (1.0 / math.sqrt(width))
    signs = sign_ref[...].astype(jnp.float32)
    for g, group in enumerate(groups):
        cut = slice(g * base, (g + 1) * base)
        unrot_ref[:, cut] = group * back * signs[:, cut]


def clip_factor(limit, square_ref):
    squares = jnp.sum(square_ref[...], axis=0, keepdims=True)[:, 0:1]
    return limit / jnp.maximum(jnp.sqrt(squares), limit)


def weights_kernel(limit, square_ref, unrot_ref, weight_ref, comp_ref, new_ref, *part_refs):
    update = unrot_ref[...] * clip_factor(limit, square_ref)
    summed = weight_ref[...].astype(jnp.float32) + (
        comp_ref[...].astype(jnp.float32) - learn_rate * update
    )
    new_ref[...] = summed.astype(jnp.bfloat16)
    for p, part_ref in enumerate(part_refs):
        rows = part_ref.shape[0]
        part_ref[...] = summed[p * rows : (p + 1) * rows].astype(jnp.bfloat16)


def update_kernel(limit, square_ref, unrot_ref, update_ref):
    update_ref[...] = unrot_ref[...] * clip_factor(limit, square_ref)


def swap(value, mask):
    size = lax.axis_size("dp")
    return lax.ppermute(value, "dp", [(i, i ^ mask) for i in range(size)])


def gather_blocks(block, parts, replicas):
    x_count = 1 << ((replicas.bit_length() - 1) // 2)
    near = replicas // 2
    me = lax.axis_index("dp")
    owned, width = block.shape
    rows = owned // len(parts)
    along_x = range(1, x_count)
    along_z = range(x_count, near, x_count)
    across = [swap(part, near) for part in parts]
    pieces = [(near, p * rows, piece) for p, piece in enumerate(across)] + [(0, 0, block)]
    own_x = {x: swap(block, x) for x in along_x}
    own_z = {z: swap(block, z) for z in along_z}
    pieces += [(mask, 0, piece) for mask, piece in (own_x | own_z).items()]
    for p, piece in enumerate(across):
        row = p * rows
        moved = {z: swap(piece, z) for z in along_z}
        pieces += [(near + z, row, value) for z, value in moved.items()]
        moved[0] = piece
        for z, value in moved.items():
            pieces += [(near + z + x, row, swap(value, x)) for x in along_x]
    for x, piece in own_x.items():
        piece, _ = lax.optimization_barrier((piece, across[-1]))
        pieces += [(x + z, 0, swap(piece, z)) for z in along_z]
    out = jnp.zeros((replicas, owned, width), block.dtype)
    for mask, row, piece in pieces:
        out = lax.dynamic_update_slice(out, piece[None], (me ^ mask, row, 0))
    return out.reshape(1, replicas * owned, width)


def on_device(grads, signs, weights, compensation):
    blocks, width = grads.shape[2:]
    replicas = lax.axis_size("dp")
    devices = replicas * lax.axis_size("expert")
    owned = blocks // replicas
    base = min(width, 256)
    matrix = jnp.asarray(hadamard(base), jnp.bfloat16)
    me = lax.axis_index("dp")
    near = replicas // 2
    offset = (me // near * owned).astype(jnp.int32).reshape(1, 1)
    params = pltpu.CompilerParams(vmem_limit_bytes=vmem_bytes)
    scalar = pl.BlockSpec(memory_space=pltpu.SMEM)
    array = pl.BlockSpec(memory_space=pltpu.VMEM)

    def block_of(source, index):
        source = source.reshape(replicas, owned, width)
        return lax.dynamic_slice_in_dim(source, index, 1, 0).reshape(owned, width)

    far_pieces = [swap(block_of(grads, me ^ mask ^ near), mask) for mask in range(1, near)]
    sums = pl.pallas_call(
        sums_kernel,
        in_specs=[array],
        out_shape=jax.ShapeDtypeStruct((2, near, 1, 2 * owned), jnp.float32),
        compiler_params=params,
        name="sum_squares",
    )(grads.reshape(2, near, owned, width))
    later, sums = lax.optimization_barrier((grads, sums))
    sums = lax.all_to_all(
        sums.reshape(replicas, 1, 2 * owned), "dp", split_axis=0, concat_axis=0, tiled=True
    ).reshape(replicas, 2 * owned)
    near_pieces = [swap(block_of(later, me ^ mask), mask) for mask in range(1, near)]
    far_pieces.append(block_of(later, me ^ near))
    near_pieces.append(block_of(later, me))
    sent = pl.pallas_call(
        functools.partial(proxy_kernel, near, base),
        in_specs=[scalar] + [array] * (near + 3),
        out_shape=jax.ShapeDtypeStruct((owned, width), jnp.int16),
        compiler_params=params,
        name="proxy_blocks",
    )(offset, *far_pieces, sums, signs, matrix)
    far_total = swap(sent, near)
    near_total = pl.pallas_call(
        functools.partial(owner_kernel, near, base),
        in_specs=[scalar] + [array] * (near + 3),
        out_shape=jax.ShapeDtypeStruct((owned, width), jnp.float32),
        compiler_params=params,
        name="owner_blocks",
    )(offset, *near_pieces, sums, signs, matrix)
    total, mean_scale, squares = pl.pallas_call(
        functools.partial(finish_kernel, near),
        in_specs=[scalar] + [array] * 3,
        out_shape=(
            jax.ShapeDtypeStruct((owned, width), jnp.float32),
            jax.ShapeDtypeStruct((owned, lanes), jnp.float32),
            jax.ShapeDtypeStruct((devices, 1, lanes), jnp.float32),
        ),
        compiler_params=params,
        name="finish_blocks",
    )(offset, near_total, far_total, sums)
    unrot = pl.pallas_call(
        functools.partial(back_kernel, base),
        out_shape=jax.ShapeDtypeStruct((owned, width), jnp.float32),
        compiler_params=params,
        name="rotate_back",
    )(total, mean_scale, signs, matrix)
    squares = lax.all_to_all(squares, ("dp", "expert"), split_axis=0, concat_axis=0, tiled=True)
    limit = target_rms * math.sqrt(blocks * width * lax.axis_size("expert"))
    squares = squares.reshape(devices, lanes)
    count = 2 if owned % 32 == 0 else 1
    new_weights, *parts = pl.pallas_call(
        functools.partial(weights_kernel, limit),
        out_shape=[jax.ShapeDtypeStruct((owned, width), jnp.bfloat16)]
        + [jax.ShapeDtypeStruct((owned // count, width), jnp.bfloat16)] * count,
        compiler_params=params,
        name="new_weights",
    )(squares, unrot, weights.reshape(owned, width), compensation.reshape(owned, width))
    update_grad = pl.pallas_call(
        functools.partial(update_kernel, limit),
        out_shape=jax.ShapeDtypeStruct((owned, width), jnp.float32),
        compiler_params=params,
        name="update_grad",
    )(squares, unrot)
    return gather_blocks(new_weights, parts, replicas), update_grad.reshape(weights.shape)


def solution(mesh):
    in_specs = (
        P("dp", "expert", None, None),
        P("expert", None),
        P("expert", "dp", None),
        P("expert", "dp", None),
    )
    out_specs = (P("expert", None, None), P("expert", "dp", None))
    return jax.shard_map(
        on_device, mesh=mesh, in_specs=in_specs, out_specs=out_specs, check_vma=False
    )
```

```python
import functools
import math

import jax
import jax.numpy as jnp
import numpy as np
from jax import lax
from jax.experimental import pallas as pl
from jax.experimental.pallas import tpu as pltpu
from jax.sharding import PartitionSpec as P

clamp_level = 2.0
target_rms = 0.2
learn_rate = 0.02
lanes = 128
vmem_bytes = 40 * 1024 * 1024


def hadamard(width):
    matrix = np.ones((1, 1), np.float32)
    while matrix.shape[0] < width:
        matrix = np.block([[matrix, matrix], [matrix, -matrix]])
    return matrix


def butterfly(groups):
    half = 1
    groups = list(groups)
    while half < len(groups):
        for start in range(0, len(groups), 2 * half):
            for i in range(start, start + half):
                upper, lower = groups[i], groups[i + half]
                groups[i], groups[i + half] = upper + lower, upper - lower
        half *= 2
    return groups


def rotate_groups(pieces, matrix, base):
    count = pieces[0].shape[1] // base
    groups = []
    for g in range(count):
        part = None
        for piece in pieces:
            term = jnp.dot(
                piece[:, g * base : (g + 1) * base], matrix, preferred_element_type=jnp.float32
            )
            part = term if part is None else part + term
        groups.append(part)
    return butterfly(groups)


def sums_kernel(near, place_ref, *refs):
    own_refs, far_refs, sums_ref = refs[:near], refs[near : 2 * near], refs[2 * near]
    owned, width = own_refs[0].shape
    half, column = place_ref[0, 0], place_ref[0, 1]
    shape = (2 * owned, 2 * owned)
    row, lane = (lax.broadcasted_iota(jnp.int32, shape, axis) for axis in (0, 1))
    target = row + half * owned
    target = jnp.where(target >= 2 * owned, target - 2 * owned, target)
    place = lax.broadcasted_iota(jnp.int32, sums_ref.shape, 0)
    sums = jnp.zeros(sums_ref.shape, jnp.float32)
    for mask in range(near):
        pair = []
        for ref in (own_refs[mask], far_refs[mask]):
            rows = ref[...].astype(jnp.float32)
            pair.append(jnp.sum(rows * rows, axis=1, keepdims=True))
        squares = jnp.concatenate(pair, axis=0)
        line = jnp.sum(jnp.where(lane == target, squares, 0.0), axis=0, keepdims=True)
        sums = jnp.where(place == (column ^ mask), line, sums)
    sums_ref[...] = sums


def scale_rows(sums_ref, column, half, owned, width, near):
    place = lax.broadcasted_iota(jnp.int32, sums_ref.shape, 0)
    biggest = jnp.where(place == column, sums_ref[...], 0.0)
    biggest = jnp.sum(biggest, axis=0, keepdims=True)
    shape = (owned, 2 * owned)
    row, lane = (lax.broadcasted_iota(jnp.int32, shape, axis) for axis in (0, 1))
    target = row + half * owned
    biggest = jnp.sum(jnp.where(lane == target, biggest, 0.0), axis=1, keepdims=True)
    mean = biggest * (1.0 / width)
    scale = jnp.sqrt(mean + 1e-06)
    peak = jnp.sqrt(mean * width) / scale
    step = near * jnp.where(
        peak >= clamp_level, clamp_level / 32768.0, jnp.maximum(peak, 1e-20) / 32767.0
    )
    return scale, step


def add_levels(pieces, scale, sign_ref, matrix_ref, base):
    width = pieces[0].shape[1]
    signs = sign_ref[...].astype(jnp.float32).astype(jnp.bfloat16)
    matrix = matrix_ref[...]
    inverse = (1.0 / math.sqrt(width)) / scale
    totals = None
    for piece in pieces:
        groups = rotate_groups([piece[...] * signs], matrix, base)
        levels = [
            jnp.clip(group * inverse, -clamp_level, clamp_level)
            .astype(jnp.bfloat16)
            .astype(jnp.float32)
            for group in groups
        ]
        totals = levels if totals is None else [t + v for t, v in zip(totals, levels)]
    return totals


def proxy_kernel(near, base, place_ref, *refs):
    pieces, (sums_ref, sign_ref, matrix_ref, sent_ref) = refs[:near], refs[near:]
    owned, width = sent_ref.shape
    scale, step = scale_rows(
        sums_ref, place_ref[0, 1], 1 - place_ref[0, 0], owned, width, near
    )
    totals = add_levels(pieces, scale, sign_ref, matrix_ref, base)
    for g, total in enumerate(totals):
        value = jnp.clip(jnp.round(total / step), -32767.0, 32767.0)
        sent_ref[:, g * base : (g + 1) * base] = value.astype(jnp.int16)


def owner_kernel(near, base, place_ref, *refs):
    pieces, (sums_ref, sign_ref, matrix_ref, total_ref) = refs[:near], refs[near:]
    owned, width = total_ref.shape
    scale, _ = scale_rows(
        sums_ref, place_ref[0, 1], place_ref[0, 0], owned, width, near
    )
    totals = add_levels(pieces, scale, sign_ref, matrix_ref, base)
    for g, total in enumerate(totals):
        total_ref[:, g * base : (g + 1) * base] = total


def finish_kernel(
    near, place_ref, near_ref, far_ref, sums_ref, total_ref, scale_ref, square_ref
):
    owned, width = near_ref.shape
    scale, step = scale_rows(
        sums_ref, place_ref[0, 1], place_ref[0, 0], owned, width, near
    )
    total = near_ref[...] + far_ref[...].astype(jnp.float32) * step
    mean_scale = scale / (2 * near)
    mean_rot = total * mean_scale
    squares = jnp.sum(mean_rot * mean_rot)
    square_ref[...] = jnp.full(square_ref.shape, squares, jnp.float32)
    total_ref[...] = total
    scale_ref[...] = jnp.broadcast_to(mean_scale, scale_ref.shape)


def back_kernel(base, total_ref, scale_ref, sign_ref, matrix_ref, unrot_ref):
    owned, width = total_ref.shape
    total = total_ref[...]
    high = total.astype(jnp.bfloat16)
    low = (total - high.astype(jnp.float32)).astype(jnp.bfloat16)
    groups = rotate_groups([high, low], matrix_ref[...], base)
    back = scale_ref[:, 0:1] * (1.0 / math.sqrt(width))
    signs = sign_ref[...].astype(jnp.float32)
    for g, group in enumerate(groups):
        cut = slice(g * base, (g + 1) * base)
        unrot_ref[:, cut] = group * back * signs[:, cut]


def clip_factor(limit, square_ref):
    squares = jnp.sum(square_ref[...], axis=0, keepdims=True)[:, 0:1]
    return limit / jnp.maximum(jnp.sqrt(squares), limit)


def weights_kernel(limit, square_ref, unrot_ref, weight_ref, comp_ref, new_ref, *part_refs):
    update = unrot_ref[...] * clip_factor(limit, square_ref)
    summed = weight_ref[...].astype(jnp.float32) + (
        comp_ref[...].astype(jnp.float32) - learn_rate * update
    )
    new_ref[...] = summed.astype(jnp.bfloat16)
    for p, part_ref in enumerate(part_refs):
        rows = part_ref.shape[0]
        part_ref[...] = summed[p * rows : (p + 1) * rows].astype(jnp.bfloat16)


def update_kernel(limit, square_ref, unrot_ref, update_ref):
    update_ref[...] = unrot_ref[...] * clip_factor(limit, square_ref)


def swap(value, mask):
    size = lax.axis_size("dp")
    return lax.ppermute(value, "dp", [(i, i ^ mask) for i in range(size)])


def gather_blocks(block, parts, replicas):
    x_count = 1 << ((replicas.bit_length() - 1) // 2)
    near = replicas // 2
    me = lax.axis_index("dp")
    owned, width = block.shape
    rows = owned // len(parts)
    along_x = range(1, x_count)
    along_z = range(x_count, near, x_count)
    across = [swap(part, near) for part in parts]
    pieces = [(near, p * rows, piece) for p, piece in enumerate(across)] + [(0, 0, block)]
    own_x = {x: swap(block, x) for x in along_x}
    own_z = {z: swap(block, z) for z in along_z}
    pieces += [(mask, 0, piece) for mask, piece in (own_x | own_z).items()]
    for p, piece in enumerate(across):
        row = p * rows
        moved = {z: swap(piece, z) for z in along_z}
        pieces += [(near + z, row, value) for z, value in moved.items()]
        moved[0] = piece
        for z, value in moved.items():
            pieces += [(near + z + x, row, swap(value, x)) for x in along_x]
    for x, piece in own_x.items():
        piece, _ = lax.optimization_barrier((piece, across[-1]))
        pieces += [(x + z, 0, swap(piece, z)) for z in along_z]
    out = jnp.zeros((replicas, owned, width), block.dtype)
    for mask, row, piece in pieces:
        out = lax.dynamic_update_slice(out, piece[None], (me ^ mask, row, 0))
    return out.reshape(1, replicas * owned, width)


def on_device(grads, signs, weights, compensation):
    blocks, width = grads.shape[2:]
    replicas = lax.axis_size("dp")
    devices = replicas * lax.axis_size("expert")
    owned = blocks // replicas
    base = min(width, 256)
    matrix = jnp.asarray(hadamard(base), jnp.bfloat16)
    me = lax.axis_index("dp")
    near = replicas // 2
    place = jnp.stack([me // near, me % near]).astype(jnp.int32).reshape(1, 2)
    params = pltpu.CompilerParams(vmem_limit_bytes=vmem_bytes)
    scalar = pl.BlockSpec(memory_space=pltpu.SMEM)
    array = pl.BlockSpec(memory_space=pltpu.VMEM)

    def block_of(source, index):
        source = source.reshape(replicas, owned, width)
        return lax.dynamic_slice_in_dim(source, index, 1, 0).reshape(owned, width)

    own_slices = [block_of(grads, me ^ mask) for mask in range(near)]
    far_slices = [block_of(grads, me ^ mask ^ near) for mask in range(near)]
    far_pieces = [far_slices[0]] + [swap(far_slices[mask], mask) for mask in range(1, near)]
    sums = pl.pallas_call(
        functools.partial(sums_kernel, near),
        in_specs=[scalar] + [array] * (2 * near),
        out_shape=jax.ShapeDtypeStruct((near, 2 * owned), jnp.float32),
        compiler_params=params,
        name="sum_squares",
    )(place, *own_slices, *far_slices)
    mask = 1
    while mask < replicas:
        if mask == near:
            sums, own_slices = lax.optimization_barrier((sums, own_slices))
        sums = jnp.maximum(sums, swap(sums, mask))
        mask *= 2
    near_pieces = [own_slices[0]] + [swap(own_slices[mask], mask) for mask in range(1, near)]
    sent = pl.pallas_call(
        functools.partial(proxy_kernel, near, base),
        in_specs=[scalar] + [array] * (near + 3),
        out_shape=jax.ShapeDtypeStruct((owned, width), jnp.int16),
        compiler_params=params,
        name="proxy_blocks",
    )(place, *far_pieces, sums, signs, matrix)
    far_total = swap(sent, near)
    near_total = pl.pallas_call(
        functools.partial(owner_kernel, near, base),
        in_specs=[scalar] + [array] * (near + 3),
        out_shape=jax.ShapeDtypeStruct((owned, width), jnp.float32),
        compiler_params=params,
        name="owner_blocks",
    )(place, *near_pieces, sums, signs, matrix)
    total, mean_scale, squares = pl.pallas_call(
        functools.partial(finish_kernel, near),
        in_specs=[scalar] + [array] * 3,
        out_shape=(
            jax.ShapeDtypeStruct((owned, width), jnp.float32),
            jax.ShapeDtypeStruct((owned, lanes), jnp.float32),
            jax.ShapeDtypeStruct((devices, 1, lanes), jnp.float32),
        ),
        compiler_params=params,
        name="finish_blocks",
    )(place, near_total, far_total, sums)
    unrot = pl.pallas_call(
        functools.partial(back_kernel, base),
        out_shape=jax.ShapeDtypeStruct((owned, width), jnp.float32),
        compiler_params=params,
        name="rotate_back",
    )(total, mean_scale, signs, matrix)
    squares = lax.all_to_all(squares, ("dp", "expert"), split_axis=0, concat_axis=0, tiled=True)
    limit = target_rms * math.sqrt(blocks * width * lax.axis_size("expert"))
    squares = squares.reshape(devices, lanes)
    count = 2 if owned % 32 == 0 else 1
    new_weights, *parts = pl.pallas_call(
        functools.partial(weights_kernel, limit),
        out_shape=[jax.ShapeDtypeStruct((owned, width), jnp.bfloat16)]
        + [jax.ShapeDtypeStruct((owned // count, width), jnp.bfloat16)] * count,
        compiler_params=params,
        name="new_weights",
    )(squares, unrot, weights.reshape(owned, width), compensation.reshape(owned, width))
    update_grad = pl.pallas_call(
        functools.partial(update_kernel, limit),
        out_shape=jax.ShapeDtypeStruct((owned, width), jnp.float32),
        compiler_params=params,
        name="update_grad",
    )(squares, unrot)
    return gather_blocks(new_weights, parts, replicas), update_grad.reshape(weights.shape)


def solution(mesh):
    in_specs = (
        P("dp", "expert", None, None),
        P("expert", None),
        P("expert", "dp", None),
        P("expert", "dp", None),
    )
    out_specs = (P("expert", None, None), P("expert", "dp", None))
    return jax.shard_map(
        on_device, mesh=mesh, in_specs=in_specs, out_specs=out_specs, check_vma=False
    )
```

```python
import functools
import math

import jax
import jax.numpy as jnp
import numpy as np
from jax import lax
from jax.experimental import pallas as pl
from jax.experimental.pallas import tpu as pltpu
from jax.sharding import PartitionSpec as P

clamp_level = 2.0
target_rms = 0.2
learn_rate = 0.02
lanes = 128
vmem_bytes = 40 * 1024 * 1024


def hadamard(width):
    matrix = np.ones((1, 1), np.float32)
    while matrix.shape[0] < width:
        matrix = np.block([[matrix, matrix], [matrix, -matrix]])
    return matrix


def butterfly(groups):
    half = 1
    groups = list(groups)
    while half < len(groups):
        for start in range(0, len(groups), 2 * half):
            for i in range(start, start + half):
                upper, lower = groups[i], groups[i + half]
                groups[i], groups[i + half] = upper + lower, upper - lower
        half *= 2
    return groups


def rotate_groups(pieces, matrix, base):
    count = pieces[0].shape[1] // base
    groups = []
    for g in range(count):
        part = None
        for piece in pieces:
            term = jnp.dot(
                piece[:, g * base : (g + 1) * base], matrix, preferred_element_type=jnp.float32
            )
            part = term if part is None else part + term
        groups.append(part)
    return butterfly(groups)


def sums_kernel(x_ref, sums_ref):
    near, owned, width = x_ref.shape[1:]
    shape = (2 * owned, 2 * owned)
    row, lane = (lax.broadcasted_iota(jnp.int32, shape, axis) for axis in (0, 1))
    for j in range(near):
        rows = x_ref[:, j].reshape(2 * owned, width).astype(jnp.float32)
        squares = jnp.sum(rows * rows, axis=1, keepdims=True)
        line = jnp.sum(jnp.where(row == lane, squares, 0.0), axis=0, keepdims=True)
        sums_ref[0, j] = line
        sums_ref[1, j] = line


def scale_rows(sums_ref, offset, owned, width, near):
    biggest = jnp.max(sums_ref[...], axis=0, keepdims=True)
    shape = (owned, 2 * owned)
    row, lane = (lax.broadcasted_iota(jnp.int32, shape, axis) for axis in (0, 1))
    biggest = jnp.sum(jnp.where(lane == row + offset, biggest, 0.0), axis=1, keepdims=True)
    mean = biggest * (1.0 / width)
    scale = jnp.sqrt(mean + 1e-06)
    peak = jnp.sqrt(mean * width) / scale
    step = near * jnp.where(
        peak >= clamp_level, clamp_level / 32768.0, jnp.maximum(peak, 1e-20) / 32767.0
    )
    return scale, step


def add_levels(pieces, half, scale, sign_ref, matrix_ref, base):
    width = pieces[0].shape[-1]
    signs = sign_ref[...].astype(jnp.float32).astype(jnp.bfloat16)
    matrix = matrix_ref[...]
    inverse = (1.0 / math.sqrt(width)) / scale
    totals = None
    for piece in pieces:
        rows = piece[...] if len(piece.shape) == 2 else piece[half]
        groups = rotate_groups([rows * signs], matrix, base)
        levels = [
            jnp.clip(group * inverse, -clamp_level, clamp_level)
            .astype(jnp.bfloat16)
            .astype(jnp.float32)
            for group in groups
        ]
        totals = levels if totals is None else [t + v for t, v in zip(totals, levels)]
    return totals


def proxy_kernel(near, base, half_ref, *refs):
    pieces, (sums_ref, sign_ref, matrix_ref, sent_ref) = refs[:near], refs[near:]
    owned, width = sent_ref.shape
    half = 1 - half_ref[0, 0]
    scale, step = scale_rows(sums_ref, half * owned, owned, width, near)
    totals = add_levels(pieces, half, scale, sign_ref, matrix_ref, base)
    for g, total in enumerate(totals):
        value = jnp.clip(jnp.round(total / step), -32767.0, 32767.0)
        sent_ref[:, g * base : (g + 1) * base] = value.astype(jnp.int16)


def owner_kernel(near, base, half_ref, *refs):
    pieces, (sums_ref, sign_ref, matrix_ref, total_ref) = refs[:near], refs[near:]
    owned, width = total_ref.shape
    half = half_ref[0, 0]
    scale, _ = scale_rows(sums_ref, half * owned, owned, width, near)
    totals = add_levels(pieces, half, scale, sign_ref, matrix_ref, base)
    for g, total in enumerate(totals):
        total_ref[:, g * base : (g + 1) * base] = total


def finish_kernel(
    near, half_ref, near_ref, far_ref, sums_ref, total_ref, scale_ref, square_ref
):
    owned, width = near_ref.shape
    scale, step = scale_rows(sums_ref, half_ref[0, 0] * owned, owned, width, near)
    total = near_ref[...] + far_ref[...].astype(jnp.float32) * step
    mean_scale = scale / (2 * near)
    mean_rot = total * mean_scale
    squares = jnp.sum(mean_rot * mean_rot)
    square_ref[...] = jnp.full(square_ref.shape, squares, jnp.float32)
    total_ref[...] = total
    scale_ref[...] = jnp.broadcast_to(mean_scale, scale_ref.shape)


def back_kernel(base, total_ref, scale_ref, sign_ref, matrix_ref, unrot_ref):
    owned, width = total_ref.shape
    total = total_ref[...]
    high = total.astype(jnp.bfloat16)
    low = (total - high.astype(jnp.float32)).astype(jnp.bfloat16)
    groups = rotate_groups([high, low], matrix_ref[...], base)
    back = scale_ref[:, 0:1] * (1.0 / math.sqrt(width))
    signs = sign_ref[...].astype(jnp.float32)
    for g, group in enumerate(groups):
        cut = slice(g * base, (g + 1) * base)
        unrot_ref[:, cut] = group * back * signs[:, cut]


def clip_factor(limit, square_ref):
    squares = jnp.sum(square_ref[...], axis=0, keepdims=True)[:, 0:1]
    return limit / jnp.maximum(jnp.sqrt(squares), limit)


def weights_kernel(limit, square_ref, unrot_ref, weight_ref, comp_ref, new_ref, *part_refs):
    update = unrot_ref[...] * clip_factor(limit, square_ref)
    summed = weight_ref[...].astype(jnp.float32) + (
        comp_ref[...].astype(jnp.float32) - learn_rate * update
    )
    new_ref[...] = summed.astype(jnp.bfloat16)
    for p, part_ref in enumerate(part_refs):
        rows = part_ref.shape[0]
        part_ref[...] = summed[p * rows : (p + 1) * rows].astype(jnp.bfloat16)


def update_kernel(limit, square_ref, unrot_ref, update_ref):
    update_ref[...] = unrot_ref[...] * clip_factor(limit, square_ref)


def chips_along_x(replicas):
    return 1 << ((replicas.bit_length() - 1) // 2)


def swap(value, mask):
    size = lax.axis_size("dp")
    return lax.ppermute(value, "dp", [(i, i ^ mask) for i in range(size)])


def gather_blocks(block, parts, replicas):
    x_count = chips_along_x(replicas)
    near = replicas // 2
    me = lax.axis_index("dp")
    owned, width = block.shape
    rows = owned // len(parts)
    along_x = range(1, x_count)
    along_z = range(x_count, near, x_count)
    across = [swap(part, near) for part in parts]
    pieces = [(near, p * rows, piece) for p, piece in enumerate(across)] + [(0, 0, block)]
    own_x = {x: swap(block, x) for x in along_x}
    own_z = {z: swap(block, z) for z in along_z}
    pieces += [(mask, 0, piece) for mask, piece in (own_x | own_z).items()]
    for p, piece in enumerate(across):
        row = p * rows
        moved = {z: swap(piece, z) for z in along_z}
        pieces += [(near + z, row, value) for z, value in moved.items()]
        moved[0] = piece
        for z, value in moved.items():
            pieces += [(near + z + x, row, swap(value, x)) for x in along_x]
    for x, piece in own_x.items():
        piece, _ = lax.optimization_barrier((piece, across[-1]))
        pieces += [(x + z, 0, swap(piece, z)) for z in along_z]
    out = jnp.zeros((replicas, owned, width), block.dtype)
    for mask, row, piece in pieces:
        out = lax.dynamic_update_slice(out, piece[None], (me ^ mask, row, 0))
    return out.reshape(1, replicas * owned, width)


def on_device(grads, signs, weights, compensation):
    blocks, width = grads.shape[2:]
    replicas = lax.axis_size("dp")
    devices = replicas * lax.axis_size("expert")
    owned = blocks // replicas
    base = min(width, 256)
    matrix = jnp.asarray(hadamard(base), jnp.bfloat16)
    me = lax.axis_index("dp")
    near = replicas // 2
    half = (me // near).astype(jnp.int32).reshape(1, 1)
    params = pltpu.CompilerParams(vmem_limit_bytes=vmem_bytes)
    scalar = pl.BlockSpec(memory_space=pltpu.SMEM)
    array = pl.BlockSpec(memory_space=pltpu.VMEM)

    halves = grads.reshape(2, near, owned, width)

    def pair_of(index):
        return lax.dynamic_slice_in_dim(halves, index % near, 1, 1).reshape(2, owned, width)

    def block_of(source, index):
        source = source.reshape(replicas, owned, width)
        return lax.dynamic_slice_in_dim(source, index, 1, 0).reshape(owned, width)

    x_count = chips_along_x(replicas)
    aligned = [m for m in range(1, near) if m % x_count == 0 or m < x_count]
    diagonal = [m for m in range(1, near) if m not in aligned]
    pairs = [pair_of(me)] + [swap(pair_of(me ^ mask), mask) for mask in aligned]
    far_pieces = pairs + [swap(block_of(grads, me ^ mask ^ near), mask) for mask in diagonal]
    sums = pl.pallas_call(
        sums_kernel,
        in_specs=[array],
        out_shape=jax.ShapeDtypeStruct((2, near, 1, 2 * owned), jnp.float32),
        compiler_params=params,
        name="sum_squares",
    )(halves)
    later, sums = lax.optimization_barrier((grads, sums))
    sums = lax.all_to_all(
        sums.reshape(replicas, 1, 2 * owned), "dp", split_axis=0, concat_axis=0, tiled=True
    ).reshape(replicas, 2 * owned)
    near_pieces = pairs + [swap(block_of(later, me ^ mask), mask) for mask in diagonal]
    sent = pl.pallas_call(
        functools.partial(proxy_kernel, near, base),
        in_specs=[scalar] + [array] * (near + 3),
        out_shape=jax.ShapeDtypeStruct((owned, width), jnp.int16),
        compiler_params=params,
        name="proxy_blocks",
    )(half, *far_pieces, sums, signs, matrix)
    far_total = swap(sent, near)
    near_total = pl.pallas_call(
        functools.partial(owner_kernel, near, base),
        in_specs=[scalar] + [array] * (near + 3),
        out_shape=jax.ShapeDtypeStruct((owned, width), jnp.float32),
        compiler_params=params,
        name="owner_blocks",
    )(half, *near_pieces, sums, signs, matrix)
    total, mean_scale, squares = pl.pallas_call(
        functools.partial(finish_kernel, near),
        in_specs=[scalar] + [array] * 3,
        out_shape=(
            jax.ShapeDtypeStruct((owned, width), jnp.float32),
            jax.ShapeDtypeStruct((owned, lanes), jnp.float32),
            jax.ShapeDtypeStruct((devices, 1, lanes), jnp.float32),
        ),
        compiler_params=params,
        name="finish_blocks",
    )(half, near_total, far_total, sums)
    unrot = pl.pallas_call(
        functools.partial(back_kernel, base),
        out_shape=jax.ShapeDtypeStruct((owned, width), jnp.float32),
        compiler_params=params,
        name="rotate_back",
    )(total, mean_scale, signs, matrix)
    squares = lax.all_to_all(squares, ("dp", "expert"), split_axis=0, concat_axis=0, tiled=True)
    limit = target_rms * math.sqrt(blocks * width * lax.axis_size("expert"))
    squares = squares.reshape(devices, lanes)
    count = 2 if owned % 32 == 0 else 1
    new_weights, *parts = pl.pallas_call(
        functools.partial(weights_kernel, limit),
        out_shape=[jax.ShapeDtypeStruct((owned, width), jnp.bfloat16)]
        + [jax.ShapeDtypeStruct((owned // count, width), jnp.bfloat16)] * count,
        compiler_params=params,
        name="new_weights",
    )(squares, unrot, weights.reshape(owned, width), compensation.reshape(owned, width))
    update_grad = pl.pallas_call(
        functools.partial(update_kernel, limit),
        out_shape=jax.ShapeDtypeStruct((owned, width), jnp.float32),
        compiler_params=params,
        name="update_grad",
    )(squares, unrot)
    return gather_blocks(new_weights, parts, replicas), update_grad.reshape(weights.shape)


def solution(mesh):
    in_specs = (
        P("dp", "expert", None, None),
        P("expert", None),
        P("expert", "dp", None),
        P("expert", "dp", None),
    )
    out_specs = (P("expert", None, None), P("expert", "dp", None))
    return jax.shard_map(
        on_device, mesh=mesh, in_specs=in_specs, out_specs=out_specs, check_vma=False
    )
```

```python
import functools
import math

import jax
import jax.numpy as jnp
import numpy as np
from jax import lax
from jax.experimental import pallas as pl
from jax.experimental.pallas import tpu as pltpu
from jax.sharding import PartitionSpec as P

clamp_level = 2.0
target_rms = 0.2
learn_rate = 0.02
lanes = 128
vmem_bytes = 40 * 1024 * 1024


def hadamard(width):
    matrix = np.ones((1, 1), np.float32)
    while matrix.shape[0] < width:
        matrix = np.block([[matrix, matrix], [matrix, -matrix]])
    return matrix


def butterfly(groups):
    half = 1
    groups = list(groups)
    while half < len(groups):
        for start in range(0, len(groups), 2 * half):
            for i in range(start, start + half):
                upper, lower = groups[i], groups[i + half]
                groups[i], groups[i + half] = upper + lower, upper - lower
        half *= 2
    return groups


def rotate_groups(pieces, matrix, base):
    count = pieces[0].shape[1] // base
    groups = []
    for g in range(count):
        part = None
        for piece in pieces:
            term = jnp.dot(
                piece[:, g * base : (g + 1) * base], matrix, preferred_element_type=jnp.float32
            )
            part = term if part is None else part + term
        groups.append(part)
    return butterfly(groups)


def sums_kernel(x_ref, sums_ref):
    near, owned, width = x_ref.shape[1:]
    shape = (2 * owned, 2 * owned)
    row, lane = (lax.broadcasted_iota(jnp.int32, shape, axis) for axis in (0, 1))
    for j in range(near):
        rows = x_ref[:, j].reshape(2 * owned, width).astype(jnp.float32)
        squares = jnp.sum(rows * rows, axis=1, keepdims=True)
        line = jnp.sum(jnp.where(row == lane, squares, 0.0), axis=0, keepdims=True)
        sums_ref[0, j] = line
        sums_ref[1, j] = line


def scale_rows(sums_ref, offset, owned, width, near):
    biggest = jnp.max(sums_ref[...], axis=0, keepdims=True)
    shape = (owned, 2 * owned)
    row, lane = (lax.broadcasted_iota(jnp.int32, shape, axis) for axis in (0, 1))
    biggest = jnp.sum(jnp.where(lane == row + offset, biggest, 0.0), axis=1, keepdims=True)
    mean = biggest * (1.0 / width)
    scale = jnp.sqrt(mean + 1e-06)
    peak = jnp.sqrt(mean * width) / scale
    step = near * jnp.where(
        peak >= clamp_level, clamp_level / 32768.0, jnp.maximum(peak, 1e-20) / 32767.0
    )
    return scale, step


def add_levels(pieces, half, scale, sign_ref, matrix_ref, base):
    width = pieces[0].shape[-1]
    signs = sign_ref[...].astype(jnp.float32).astype(jnp.bfloat16)
    matrix = matrix_ref[...]
    inverse = (1.0 / math.sqrt(width)) / scale
    totals = None
    for piece in pieces:
        rows = piece[...] if len(piece.shape) == 2 else piece[half]
        groups = rotate_groups([rows * signs], matrix, base)
        levels = [
            jnp.clip(group * inverse, -clamp_level, clamp_level)
            .astype(jnp.bfloat16)
            .astype(jnp.float32)
            for group in groups
        ]
        totals = levels if totals is None else [t + v for t, v in zip(totals, levels)]
    return totals


def proxy_kernel(near, base, half_ref, *refs):
    pieces, (sums_ref, sign_ref, matrix_ref, sent_ref) = refs[:near], refs[near:]
    owned, width = sent_ref.shape
    half = 1 - half_ref[0, 0]
    scale, step = scale_rows(sums_ref, half * owned, owned, width, near)
    totals = add_levels(pieces, half, scale, sign_ref, matrix_ref, base)
    for g, total in enumerate(totals):
        value = jnp.clip(jnp.round(total / step), -32767.0, 32767.0)
        sent_ref[:, g * base : (g + 1) * base] = value.astype(jnp.int16)


def owner_kernel(near, base, half_ref, *refs):
    pieces, (sums_ref, sign_ref, matrix_ref, total_ref) = refs[:near], refs[near:]
    owned, width = total_ref.shape
    half = half_ref[0, 0]
    scale, _ = scale_rows(sums_ref, half * owned, owned, width, near)
    totals = add_levels(pieces, half, scale, sign_ref, matrix_ref, base)
    for g, total in enumerate(totals):
        total_ref[:, g * base : (g + 1) * base] = total


def finish_kernel(
    near, half_ref, near_ref, far_ref, sums_ref, total_ref, scale_ref, square_ref
):
    owned, width = near_ref.shape
    scale, step = scale_rows(sums_ref, half_ref[0, 0] * owned, owned, width, near)
    total = near_ref[...] + far_ref[...].astype(jnp.float32) * step
    mean_scale = scale / (2 * near)
    mean_rot = total * mean_scale
    squares = jnp.sum(mean_rot * mean_rot)
    square_ref[...] = jnp.full(square_ref.shape, squares, jnp.float32)
    total_ref[...] = total
    scale_ref[...] = jnp.broadcast_to(mean_scale, scale_ref.shape)


def back_kernel(base, total_ref, scale_ref, sign_ref, matrix_ref, unrot_ref):
    owned, width = total_ref.shape
    total = total_ref[...]
    high = total.astype(jnp.bfloat16)
    low = (total - high.astype(jnp.float32)).astype(jnp.bfloat16)
    groups = rotate_groups([high, low], matrix_ref[...], base)
    back = scale_ref[:, 0:1] * (1.0 / math.sqrt(width))
    signs = sign_ref[...].astype(jnp.float32)
    for g, group in enumerate(groups):
        cut = slice(g * base, (g + 1) * base)
        unrot_ref[:, cut] = group * back * signs[:, cut]


def clip_factor(limit, square_ref):
    squares = jnp.sum(square_ref[...], axis=0, keepdims=True)[:, 0:1]
    return limit / jnp.maximum(jnp.sqrt(squares), limit)


def weights_kernel(limit, square_ref, unrot_ref, weight_ref, comp_ref, new_ref):
    update = unrot_ref[...] * clip_factor(limit, square_ref)
    summed = weight_ref[...].astype(jnp.float32) + (
        comp_ref[...].astype(jnp.float32) - learn_rate * update
    )
    new_ref[...] = summed.astype(jnp.bfloat16)


def update_kernel(limit, square_ref, unrot_ref, update_ref):
    update_ref[...] = unrot_ref[...] * clip_factor(limit, square_ref)


def chips_along_x(replicas):
    return 1 << ((replicas.bit_length() - 1) // 2)


def swap(value, mask):
    size = lax.axis_size("dp")
    return lax.ppermute(value, "dp", [(i, i ^ mask) for i in range(size)])


def place_kernel(places, owned, me_ref, *refs):
    pieces, out_ref, sem = refs[: len(places)], refs[-2], refs[-1]
    copies = []
    for i, ((mask, row), piece) in enumerate(zip(places, pieces)):
        start = pl.multiple_of((me_ref[0, 0] ^ mask) * owned + row, 16)
        rows = pl.ds(start, piece.shape[0])
        copies.append(pltpu.make_async_copy(piece, out_ref.at[rows], sem.at[i]))
    for copy in copies:
        copy.start()
    for copy in copies:
        copy.wait()


def place_pieces(items, owned, replicas, out, name):
    places = [(mask, row) for mask, row, _ in items]
    values = [piece for _, _, piece in items]
    me = lax.axis_index("dp").astype(jnp.int32).reshape(1, 1)
    operands, aliases = [me, *values], {}
    specs = [pl.BlockSpec(memory_space=pltpu.SMEM)]
    specs += [pl.BlockSpec(memory_space=pltpu.VMEM)] * len(values)
    if out is not None:
        aliases = {len(operands): 0}
        operands.append(out)
        specs.append(pl.BlockSpec(memory_space=pl.ANY))
    width = values[0].shape[1]
    return pl.pallas_call(
        functools.partial(place_kernel, places, owned),
        in_specs=specs,
        out_specs=pl.BlockSpec(memory_space=pl.ANY),
        out_shape=jax.ShapeDtypeStruct((replicas * owned, width), values[0].dtype),
        scratch_shapes=[pltpu.SemaphoreType.DMA((len(values),))],
        input_output_aliases=aliases,
        compiler_params=pltpu.CompilerParams(vmem_limit_bytes=vmem_bytes),
        name=name,
    )(*operands)


def gather_blocks(block, replicas):
    x_count = chips_along_x(replicas)
    near = replicas // 2
    me = lax.axis_index("dp")
    owned, width = block.shape
    along_x = range(1, x_count)
    along_z = range(x_count, near, x_count)
    far = swap(block, near)
    own_x = {x: swap(block, x) for x in along_x}
    own_z = {z: swap(block, z) for z in along_z}
    pieces = [(near, 0, far), (0, 0, block)]
    pieces += [(mask, 0, piece) for mask, piece in (own_x | own_z).items()]
    aligned = [near + mask for mask in own_x | own_z]
    rows = owned // 2
    routes = []
    for p, (firsts, seconds) in enumerate([(along_z, along_x), (along_x, along_z)]):
        part = far[p * rows : (p + 1) * rows]
        routes.append((p * rows, part, {m: swap(part, m) for m in firsts}, seconds))
        pieces += [(near + m, p * rows, value) for m, value in routes[-1][2].items()]
    for row, part, moved, seconds in routes:
        pieces += [(near + k, row, swap(part, k)) for k in seconds]
    for x, piece in own_x.items():
        pieces += [(x + z, 0, swap(piece, z)) for z in along_z]
    for row, part, moved, seconds in routes:
        for m, value in moved.items():
            pieces += [(near + m + k, row, swap(value, k)) for k in seconds]
    last = [item for item in pieces if item[0] >= near and item[0] not in (near, *aligned)]
    early = [item for item in pieces if item not in last]
    out = place_pieces(early, owned, replicas, None, "place_early")
    out = place_pieces(last, owned, replicas, out, "place_last")
    return out.reshape(1, replicas * owned, width)


def on_device(grads, signs, weights, compensation):
    blocks, width = grads.shape[2:]
    replicas = lax.axis_size("dp")
    devices = replicas * lax.axis_size("expert")
    owned = blocks // replicas
    base = min(width, 256)
    matrix = jnp.asarray(hadamard(base), jnp.bfloat16)
    me = lax.axis_index("dp")
    near = replicas // 2
    half = (me // near).astype(jnp.int32).reshape(1, 1)
    params = pltpu.CompilerParams(vmem_limit_bytes=vmem_bytes)
    scalar = pl.BlockSpec(memory_space=pltpu.SMEM)
    array = pl.BlockSpec(memory_space=pltpu.VMEM)

    halves = grads.reshape(2, near, owned, width)

    def pair_of(index):
        return lax.dynamic_slice_in_dim(halves, index % near, 1, 1).reshape(2, owned, width)

    def block_of(source, index):
        source = source.reshape(replicas, owned, width)
        return lax.dynamic_slice_in_dim(source, index, 1, 0).reshape(owned, width)

    x_count = chips_along_x(replicas)
    aligned = [m for m in range(1, near) if m % x_count == 0 or m < x_count]
    diagonal = [m for m in range(1, near) if m not in aligned]
    pairs = [pair_of(me)] + [swap(pair_of(me ^ mask), mask) for mask in aligned]
    far_pieces = pairs + [swap(block_of(grads, me ^ mask ^ near), mask) for mask in diagonal]
    sums = pl.pallas_call(
        sums_kernel,
        in_specs=[array],
        out_shape=jax.ShapeDtypeStruct((2, near, 1, 2 * owned), jnp.float32),
        compiler_params=params,
        name="sum_squares",
    )(halves)
    later, sums = lax.optimization_barrier((grads, sums))
    sums = lax.all_to_all(
        sums.reshape(replicas, 1, 2 * owned), "dp", split_axis=0, concat_axis=0, tiled=True
    ).reshape(replicas, 2 * owned)
    near_pieces = pairs + [swap(block_of(later, me ^ mask), mask) for mask in diagonal]
    sent = pl.pallas_call(
        functools.partial(proxy_kernel, near, base),
        in_specs=[scalar] + [array] * (near + 3),
        out_shape=jax.ShapeDtypeStruct((owned, width), jnp.int16),
        compiler_params=params,
        name="proxy_blocks",
    )(half, *far_pieces, sums, signs, matrix)
    far_total = swap(sent, near)
    near_total = pl.pallas_call(
        functools.partial(owner_kernel, near, base),
        in_specs=[scalar] + [array] * (near + 3),
        out_shape=jax.ShapeDtypeStruct((owned, width), jnp.float32),
        compiler_params=params,
        name="owner_blocks",
    )(half, *near_pieces, sums, signs, matrix)
    total, mean_scale, squares = pl.pallas_call(
        functools.partial(finish_kernel, near),
        in_specs=[scalar] + [array] * 3,
        out_shape=(
            jax.ShapeDtypeStruct((owned, width), jnp.float32),
            jax.ShapeDtypeStruct((owned, lanes), jnp.float32),
            jax.ShapeDtypeStruct((devices, 1, lanes), jnp.float32),
        ),
        compiler_params=params,
        name="finish_blocks",
    )(half, near_total, far_total, sums)
    unrot = pl.pallas_call(
        functools.partial(back_kernel, base),
        out_shape=jax.ShapeDtypeStruct((owned, width), jnp.float32),
        compiler_params=params,
        name="rotate_back",
    )(total, mean_scale, signs, matrix)
    squares = lax.all_to_all(squares, ("dp", "expert"), split_axis=0, concat_axis=0, tiled=True)
    limit = target_rms * math.sqrt(blocks * width * lax.axis_size("expert"))
    squares = squares.reshape(devices, lanes)
    new_weights = pl.pallas_call(
        functools.partial(weights_kernel, limit),
        out_shape=jax.ShapeDtypeStruct((owned, width), jnp.bfloat16),
        compiler_params=params,
        name="new_weights",
    )(squares, unrot, weights.reshape(owned, width), compensation.reshape(owned, width))
    update_grad = pl.pallas_call(
        functools.partial(update_kernel, limit),
        out_shape=jax.ShapeDtypeStruct((owned, width), jnp.float32),
        compiler_params=params,
        name="update_grad",
    )(squares, unrot)
    return gather_blocks(new_weights, replicas), update_grad.reshape(weights.shape)


def solution(mesh):
    in_specs = (
        P("dp", "expert", None, None),
        P("expert", None),
        P("expert", "dp", None),
        P("expert", "dp", None),
    )
    out_specs = (P("expert", None, None), P("expert", "dp", None))
    return jax.shard_map(
        on_device, mesh=mesh, in_specs=in_specs, out_specs=out_specs, check_vma=False
    )
```

```python
import functools
import math

import jax
import jax.numpy as jnp
import numpy as np
from jax import lax
from jax.experimental import pallas as pl
from jax.experimental.pallas import tpu as pltpu
from jax.sharding import PartitionSpec as P

clamp_level = 2.0
target_rms = 0.2
learn_rate = 0.02
lanes = 128
vmem_bytes = 40 * 1024 * 1024


def hadamard(width):
    matrix = np.ones((1, 1), np.float32)
    while matrix.shape[0] < width:
        matrix = np.block([[matrix, matrix], [matrix, -matrix]])
    return matrix


def butterfly(groups):
    half = 1
    groups = list(groups)
    while half < len(groups):
        for start in range(0, len(groups), 2 * half):
            for i in range(start, start + half):
                upper, lower = groups[i], groups[i + half]
                groups[i], groups[i + half] = upper + lower, upper - lower
        half *= 2
    return groups


def rotate_groups(pieces, matrix, base):
    count = pieces[0].shape[1] // base
    groups = []
    for g in range(count):
        part = None
        for piece in pieces:
            term = jnp.dot(
                piece[:, g * base : (g + 1) * base], matrix, preferred_element_type=jnp.float32
            )
            part = term if part is None else part + term
        groups.append(part)
    return butterfly(groups)


def sums_kernel(x_ref, sums_ref):
    near, owned, width = x_ref.shape[1:]
    shape = (2 * owned, 2 * owned)
    row, lane = (lax.broadcasted_iota(jnp.int32, shape, axis) for axis in (0, 1))
    for j in range(near):
        rows = x_ref[:, j].reshape(2 * owned, width).astype(jnp.float32)
        squares = jnp.sum(rows * rows, axis=1, keepdims=True)
        line = jnp.sum(jnp.where(row == lane, squares, 0.0), axis=0, keepdims=True)
        sums_ref[0, j] = line
        sums_ref[1, j] = line


def scale_rows(sums_ref, offset, owned, width, near):
    biggest = jnp.max(sums_ref[...], axis=0, keepdims=True)
    shape = (owned, 2 * owned)
    row, lane = (lax.broadcasted_iota(jnp.int32, shape, axis) for axis in (0, 1))
    biggest = jnp.sum(jnp.where(lane == row + offset, biggest, 0.0), axis=1, keepdims=True)
    mean = biggest * (1.0 / width)
    scale = jnp.sqrt(mean + 1e-06)
    peak = jnp.sqrt(mean * width) / scale
    step = near * jnp.where(
        peak >= clamp_level, clamp_level / 32768.0, jnp.maximum(peak, 1e-20) / 32767.0
    )
    return scale, step


def add_levels(pieces, half, scale, sign_ref, matrix_ref, base):
    width = pieces[0].shape[-1]
    signs = sign_ref[...].astype(jnp.float32).astype(jnp.bfloat16)
    matrix = matrix_ref[...]
    inverse = (1.0 / math.sqrt(width)) / scale
    totals = None
    for piece in pieces:
        rows = piece[...] if len(piece.shape) == 2 else piece[half]
        groups = rotate_groups([rows * signs], matrix, base)
        levels = [
            jnp.clip(group * inverse, -clamp_level, clamp_level)
            .astype(jnp.bfloat16)
            .astype(jnp.float32)
            for group in groups
        ]
        totals = levels if totals is None else [t + v for t, v in zip(totals, levels)]
    return totals


def proxy_kernel(near, base, *refs):
    pieces, (sums_ref, sign_ref, matrix_ref, sent_ref) = refs[:near], refs[near:]
    owned, width = sent_ref.shape
    half = 1 - lax.axis_index("dp") // near
    scale, step = scale_rows(sums_ref, half * owned, owned, width, near)
    totals = add_levels(pieces, half, scale, sign_ref, matrix_ref, base)
    for g, total in enumerate(totals):
        value = jnp.clip(jnp.round(total / step), -32767.0, 32767.0)
        sent_ref[:, g * base : (g + 1) * base] = value.astype(jnp.int16)


def owner_kernel(near, base, *refs):
    pieces, (sums_ref, sign_ref, matrix_ref, total_ref) = refs[:near], refs[near:]
    owned, width = total_ref.shape
    half = lax.axis_index("dp") // near
    scale, _ = scale_rows(sums_ref, half * owned, owned, width, near)
    totals = add_levels(pieces, half, scale, sign_ref, matrix_ref, base)
    for g, total in enumerate(totals):
        total_ref[:, g * base : (g + 1) * base] = total


def finish_kernel(
    near, near_ref, far_ref, sums_ref, total_ref, scale_ref, square_ref
):
    owned, width = near_ref.shape
    scale, step = scale_rows(
        sums_ref, lax.axis_index("dp") // near * owned, owned, width, near
    )
    total = near_ref[...] + far_ref[...].astype(jnp.float32) * step
    mean_scale = scale / (2 * near)
    mean_rot = total * mean_scale
    squares = jnp.sum(mean_rot * mean_rot)
    square_ref[...] = jnp.full(square_ref.shape, squares, jnp.float32)
    total_ref[...] = total
    scale_ref[...] = jnp.broadcast_to(mean_scale, scale_ref.shape)


def back_kernel(base, total_ref, scale_ref, sign_ref, matrix_ref, unrot_ref):
    owned, width = total_ref.shape
    total = total_ref[...]
    high = total.astype(jnp.bfloat16)
    low = (total - high.astype(jnp.float32)).astype(jnp.bfloat16)
    groups = rotate_groups([high, low], matrix_ref[...], base)
    back = scale_ref[:, 0:1] * (1.0 / math.sqrt(width))
    signs = sign_ref[...].astype(jnp.float32)
    for g, group in enumerate(groups):
        cut = slice(g * base, (g + 1) * base)
        unrot_ref[:, cut] = group * back * signs[:, cut]


def clip_factor(limit, square_ref):
    squares = jnp.sum(square_ref[...], axis=0, keepdims=True)[:, 0:1]
    return limit / jnp.maximum(jnp.sqrt(squares), limit)


def weights_kernel(limit, square_ref, unrot_ref, weight_ref, comp_ref, new_ref):
    update = unrot_ref[...] * clip_factor(limit, square_ref)
    summed = weight_ref[...].astype(jnp.float32) + (
        comp_ref[...].astype(jnp.float32) - learn_rate * update
    )
    new_ref[...] = summed.astype(jnp.bfloat16)


def update_kernel(limit, square_ref, unrot_ref, update_ref):
    update_ref[...] = unrot_ref[...] * clip_factor(limit, square_ref)


def chips_along_x(replicas):
    return 1 << ((replicas.bit_length() - 1) // 2)


def swap(value, mask):
    size = lax.axis_size("dp")
    return lax.ppermute(value, "dp", [(i, i ^ mask) for i in range(size)])


def place_kernel(places, owned, *refs):
    pieces, out_ref, sem = refs[: len(places)], refs[-2], refs[-1]
    me = lax.axis_index("dp")
    copies = []
    for i, ((mask, row), piece) in enumerate(zip(places, pieces)):
        start = pl.multiple_of((me ^ mask) * owned + row, 16)
        rows = pl.ds(start, piece.shape[0])
        copies.append(pltpu.make_async_copy(piece, out_ref.at[rows], sem.at[i]))
    for copy in copies:
        copy.start()
    for copy in copies:
        copy.wait()


def place_pieces(items, owned, replicas, out, name):
    places = [(mask, row) for mask, row, _ in items]
    values = [piece for _, _, piece in items]
    operands, aliases = list(values), {}
    specs = [pl.BlockSpec(memory_space=pltpu.VMEM)] * len(values)
    if out is not None:
        aliases = {len(operands): 0}
        operands.append(out)
        specs.append(pl.BlockSpec(memory_space=pl.ANY))
    width = values[0].shape[1]
    return pl.pallas_call(
        functools.partial(place_kernel, places, owned),
        in_specs=specs,
        out_specs=pl.BlockSpec(memory_space=pl.ANY),
        out_shape=jax.ShapeDtypeStruct((replicas * owned, width), values[0].dtype),
        scratch_shapes=[pltpu.SemaphoreType.DMA((len(values),))],
        input_output_aliases=aliases,
        compiler_params=pltpu.CompilerParams(vmem_limit_bytes=vmem_bytes),
        name=name,
    )(*operands)


def gather_blocks(block, replicas):
    x_count = chips_along_x(replicas)
    near = replicas // 2
    me = lax.axis_index("dp")
    owned, width = block.shape
    along_x = range(1, x_count)
    along_z = range(x_count, near, x_count)
    far = swap(block, near)
    own_x = {x: swap(block, x) for x in along_x}
    own_z = {z: swap(block, z) for z in along_z}
    pieces = [(near, 0, far), (0, 0, block)]
    pieces += [(mask, 0, piece) for mask, piece in (own_x | own_z).items()]
    aligned = [near + mask for mask in own_x | own_z]
    rows = owned // 2
    routes = []
    for p, (firsts, seconds) in enumerate([(along_z, along_x), (along_x, along_z)]):
        part = far[p * rows : (p + 1) * rows]
        routes.append((p * rows, part, {m: swap(part, m) for m in firsts}, seconds))
        pieces += [(near + m, p * rows, value) for m, value in routes[-1][2].items()]
    for row, part, moved, seconds in routes:
        pieces += [(near + k, row, swap(part, k)) for k in seconds]
    for x, piece in own_x.items():
        pieces += [(x + z, 0, swap(piece, z)) for z in along_z]
    for row, part, moved, seconds in routes:
        for m, value in moved.items():
            pieces += [(near + m + k, row, swap(value, k)) for k in seconds]
    last = [item for item in pieces if item[0] >= near and item[0] not in (near, *aligned)]
    early = [item for item in pieces if item not in last]
    own = [item for item in early if item[0] < near]
    early = [item for item in early if item not in own]
    out = place_pieces(own, owned, replicas, None, "place_own")
    out = place_pieces(early, owned, replicas, out, "place_early")
    out = place_pieces(last, owned, replicas, out, "place_last")
    return out.reshape(1, replicas * owned, width)


def on_device(grads, signs, weights, compensation):
    blocks, width = grads.shape[2:]
    replicas = lax.axis_size("dp")
    devices = replicas * lax.axis_size("expert")
    owned = blocks // replicas
    base = min(width, 256)
    matrix = jnp.asarray(hadamard(base), jnp.bfloat16)
    me = lax.axis_index("dp")
    near = replicas // 2
    params = pltpu.CompilerParams(vmem_limit_bytes=vmem_bytes)
    array = pl.BlockSpec(memory_space=pltpu.VMEM)

    def pair_of(source, index):
        source = source.reshape(2, near, owned, width)
        return lax.dynamic_slice_in_dim(source, index % near, 1, 1).reshape(2, owned, width)

    def block_of(source, index):
        source = source.reshape(replicas, owned, width)
        return lax.dynamic_slice_in_dim(source, index, 1, 0).reshape(owned, width)

    x_count = chips_along_x(replicas)
    aligned = [m for m in range(1, near) if m % x_count == 0 or m < x_count]
    diagonal = [m for m in range(1, near) if m not in aligned]
    pairs = [swap(pair_of(grads, me ^ mask), mask) for mask in aligned]
    far_pieces = [swap(block_of(grads, me ^ mask ^ near), mask) for mask in diagonal]
    sums = pl.pallas_call(
        sums_kernel,
        in_specs=[array],
        out_shape=jax.ShapeDtypeStruct((2, near, 1, 2 * owned), jnp.float32),
        compiler_params=params,
        name="sum_squares",
    )(grads.reshape(2, near, owned, width))
    later, sums = lax.optimization_barrier((grads, sums))
    sums = lax.all_to_all(
        sums.reshape(replicas, 1, 2 * owned), "dp", split_axis=0, concat_axis=0, tiled=True
    ).reshape(replicas, 2 * owned)
    pairs.append(pair_of(later, me))
    far_pieces = pairs + far_pieces
    near_pieces = pairs + [swap(block_of(later, me ^ mask), mask) for mask in diagonal]
    sent = pl.pallas_call(
        functools.partial(proxy_kernel, near, base),
        in_specs=[array] * (near + 3),
        out_shape=jax.ShapeDtypeStruct((owned, width), jnp.int16),
        compiler_params=params,
        name="proxy_blocks",
    )(*far_pieces, sums, signs, matrix)
    far_total = swap(sent, near)
    near_total = pl.pallas_call(
        functools.partial(owner_kernel, near, base),
        in_specs=[array] * (near + 3),
        out_shape=jax.ShapeDtypeStruct((owned, width), jnp.float32),
        compiler_params=params,
        name="owner_blocks",
    )(*near_pieces, sums, signs, matrix)
    total, mean_scale, squares = pl.pallas_call(
        functools.partial(finish_kernel, near),
        in_specs=[array] * 3,
        out_shape=(
            jax.ShapeDtypeStruct((owned, width), jnp.float32),
            jax.ShapeDtypeStruct((owned, lanes), jnp.float32),
            jax.ShapeDtypeStruct((devices, 1, lanes), jnp.float32),
        ),
        compiler_params=params,
        name="finish_blocks",
    )(near_total, far_total, sums)
    unrot = pl.pallas_call(
        functools.partial(back_kernel, base),
        out_shape=jax.ShapeDtypeStruct((owned, width), jnp.float32),
        compiler_params=params,
        name="rotate_back",
    )(total, mean_scale, signs, matrix)
    squares = lax.all_to_all(squares, ("dp", "expert"), split_axis=0, concat_axis=0, tiled=True)
    limit = target_rms * math.sqrt(blocks * width * lax.axis_size("expert"))
    squares = squares.reshape(devices, lanes)
    new_weights = pl.pallas_call(
        functools.partial(weights_kernel, limit),
        out_shape=jax.ShapeDtypeStruct((owned, width), jnp.bfloat16),
        compiler_params=params,
        name="new_weights",
    )(squares, unrot, weights.reshape(owned, width), compensation.reshape(owned, width))
    update_grad = pl.pallas_call(
        functools.partial(update_kernel, limit),
        out_shape=jax.ShapeDtypeStruct((owned, width), jnp.float32),
        compiler_params=params,
        name="update_grad",
    )(squares, unrot)
    return gather_blocks(new_weights, replicas), update_grad.reshape(weights.shape)


def solution(mesh):
    in_specs = (
        P("dp", "expert", None, None),
        P("expert", None),
        P("expert", "dp", None),
        P("expert", "dp", None),
    )
    out_specs = (P("expert", None, None), P("expert", "dp", None))
    return jax.shard_map(
        on_device, mesh=mesh, in_specs=in_specs, out_specs=out_specs, check_vma=False
    )
```

```python
import functools
import math

import jax
import jax.numpy as jnp
import numpy as np
from jax import lax
from jax.experimental import pallas as pl
from jax.experimental.pallas import tpu as pltpu
from jax.sharding import PartitionSpec as P

clamp_level = 2.0
target_rms = 0.2
learn_rate = 0.02
lanes = 128
vmem_bytes = 40 * 1024 * 1024


def hadamard(width):
    matrix = np.ones((1, 1), np.float32)
    while matrix.shape[0] < width:
        matrix = np.block([[matrix, matrix], [matrix, -matrix]])
    return matrix


def butterfly(groups):
    half = 1
    groups = list(groups)
    while half < len(groups):
        for start in range(0, len(groups), 2 * half):
            for i in range(start, start + half):
                upper, lower = groups[i], groups[i + half]
                groups[i], groups[i + half] = upper + lower, upper - lower
        half *= 2
    return groups


def rotate_groups(pieces, matrix, base):
    count = pieces[0].shape[1] // base
    groups = []
    for g in range(count):
        part = None
        for piece in pieces:
            term = jnp.dot(
                piece[:, g * base : (g + 1) * base], matrix, preferred_element_type=jnp.float32
            )
            part = term if part is None else part + term
        groups.append(part)
    return butterfly(groups)


def sums_kernel(x_ref, sums_ref):
    near, owned, width = x_ref.shape[1:]
    shape = (2 * owned, 2 * owned)
    row, lane = (lax.broadcasted_iota(jnp.int32, shape, axis) for axis in (0, 1))
    for j in range(near):
        rows = x_ref[:, j].reshape(2 * owned, width).astype(jnp.float32)
        squares = jnp.sum(rows * rows, axis=1, keepdims=True)
        line = jnp.sum(jnp.where(row == lane, squares, 0.0), axis=0, keepdims=True)
        sums_ref[0, j] = line
        sums_ref[1, j] = line


def scale_rows(sums_ref, offset, owned, width, near):
    biggest = jnp.max(sums_ref[...], axis=0, keepdims=True)
    shape = (owned, 2 * owned)
    row, lane = (lax.broadcasted_iota(jnp.int32, shape, axis) for axis in (0, 1))
    biggest = jnp.sum(jnp.where(lane == row + offset, biggest, 0.0), axis=1, keepdims=True)
    mean = biggest * (1.0 / width)
    scale = jnp.sqrt(mean + 1e-06)
    peak = jnp.sqrt(mean * width) / scale
    step = near * jnp.where(
        peak >= clamp_level, clamp_level / 32768.0, jnp.maximum(peak, 1e-20) / 32767.0
    )
    return scale, step


def add_levels(pieces, half, scale, sign_ref, matrix_ref, base):
    width = pieces[0].shape[-1]
    signs = sign_ref[...].astype(jnp.float32).astype(jnp.bfloat16)
    matrix = matrix_ref[...]
    inverse = (1.0 / math.sqrt(width)) / scale
    totals = None
    for piece in pieces:
        rows = piece[...] if len(piece.shape) == 2 else piece[half]
        groups = rotate_groups([rows * signs], matrix, base)
        levels = [
            jnp.clip(group * inverse, -clamp_level, clamp_level)
            .astype(jnp.bfloat16)
            .astype(jnp.float32)
            for group in groups
        ]
        totals = levels if totals is None else [t + v for t, v in zip(totals, levels)]
    return totals


def proxy_kernel(near, base, *refs):
    pieces, (sums_ref, sign_ref, matrix_ref, sent_ref) = refs[:near], refs[near:]
    owned, width = sent_ref.shape
    half = 1 - lax.axis_index("dp") // near
    scale, step = scale_rows(sums_ref, half * owned, owned, width, near)
    totals = add_levels(pieces, half, scale, sign_ref, matrix_ref, base)
    for g, total in enumerate(totals):
        value = jnp.clip(jnp.round(total / step), -32767.0, 32767.0)
        sent_ref[:, g * base : (g + 1) * base] = value.astype(jnp.int16)


def owner_kernel(near, base, *refs):
    pieces, (sums_ref, sign_ref, matrix_ref, total_ref) = refs[:near], refs[near:]
    owned, width = total_ref.shape
    half = lax.axis_index("dp") // near
    scale, _ = scale_rows(sums_ref, half * owned, owned, width, near)
    totals = add_levels(pieces, half, scale, sign_ref, matrix_ref, base)
    for g, total in enumerate(totals):
        total_ref[:, g * base : (g + 1) * base] = total


def finish_kernel(
    near, near_ref, far_ref, sums_ref, total_ref, scale_ref, square_ref
):
    owned, width = near_ref.shape
    scale, step = scale_rows(
        sums_ref, lax.axis_index("dp") // near * owned, owned, width, near
    )
    total = near_ref[...] + far_ref[...].astype(jnp.float32) * step
    mean_scale = scale / (2 * near)
    mean_rot = total * mean_scale
    squares = jnp.sum(mean_rot * mean_rot)
    square_ref[...] = jnp.full(square_ref.shape, squares, jnp.float32)
    total_ref[...] = total
    scale_ref[...] = jnp.broadcast_to(mean_scale, scale_ref.shape)


def back_kernel(base, total_ref, scale_ref, sign_ref, matrix_ref, unrot_ref):
    owned, width = total_ref.shape
    total = total_ref[...]
    high = total.astype(jnp.bfloat16)
    low = (total - high.astype(jnp.float32)).astype(jnp.bfloat16)
    groups = rotate_groups([high, low], matrix_ref[...], base)
    back = scale_ref[:, 0:1] * (1.0 / math.sqrt(width))
    signs = sign_ref[...].astype(jnp.float32)
    for g, group in enumerate(groups):
        cut = slice(g * base, (g + 1) * base)
        unrot_ref[:, cut] = group * back * signs[:, cut]


def clip_factor(limit, square_ref):
    squares = jnp.sum(square_ref[...], axis=0, keepdims=True)[:, 0:1]
    return limit / jnp.maximum(jnp.sqrt(squares), limit)


def weights_kernel(limit, square_ref, unrot_ref, weight_ref, comp_ref, new_ref):
    update = unrot_ref[...] * clip_factor(limit, square_ref)
    summed = weight_ref[...].astype(jnp.float32) + (
        comp_ref[...].astype(jnp.float32) - learn_rate * update
    )
    new_ref[...] = summed.astype(jnp.bfloat16)


def update_kernel(limit, square_ref, unrot_ref, update_ref):
    update_ref[...] = unrot_ref[...] * clip_factor(limit, square_ref)


def chips_along_x(replicas):
    return 1 << ((replicas.bit_length() - 1) // 2)


def swap(value, mask):
    size = lax.axis_size("dp")
    return lax.ppermute(value, "dp", [(i, i ^ mask) for i in range(size)])


def place_kernel(places, owned, *refs):
    pieces, out_ref, sem = refs[: len(places)], refs[-2], refs[-1]
    me = lax.axis_index("dp")
    copies = []
    for i, ((mask, row), piece) in enumerate(zip(places, pieces)):
        start = pl.multiple_of((me ^ mask) * owned + row, 16)
        rows = pl.ds(start, piece.shape[0])
        copies.append(pltpu.make_async_copy(piece, out_ref.at[rows], sem.at[i]))
    for copy in copies:
        copy.start()
    for copy in copies:
        copy.wait()


def place_pieces(items, owned, replicas, out, name):
    places = [(mask, row) for mask, row, _ in items]
    values = [piece for _, _, piece in items]
    operands, aliases = list(values), {}
    specs = [pl.BlockSpec(memory_space=pltpu.VMEM)] * len(values)
    if out is not None:
        aliases = {len(operands): 0}
        operands.append(out)
        specs.append(pl.BlockSpec(memory_space=pl.ANY))
    width = values[0].shape[1]
    return pl.pallas_call(
        functools.partial(place_kernel, places, owned),
        in_specs=specs,
        out_specs=pl.BlockSpec(memory_space=pl.ANY),
        out_shape=jax.ShapeDtypeStruct((replicas * owned, width), values[0].dtype),
        scratch_shapes=[pltpu.SemaphoreType.DMA((len(values),))],
        input_output_aliases=aliases,
        compiler_params=pltpu.CompilerParams(vmem_limit_bytes=vmem_bytes),
        name=name,
    )(*operands)


def gather_blocks(block, replicas):
    near = replicas // 2
    owned, width = block.shape
    far = swap(block, near)
    own = [(0, 0, block)] + [(m, 0, swap(block, m)) for m in reversed(range(1, near))]
    spread = [(near + m, 0, swap(far, m)) for m in range(1, near)]
    out = place_pieces(own + [(near, 0, far)], owned, replicas, None, "place_own")
    out = place_pieces(spread, owned, replicas, out, "place_far")
    return out.reshape(1, replicas * owned, width)


def on_device(grads, signs, weights, compensation):
    blocks, width = grads.shape[2:]
    replicas = lax.axis_size("dp")
    devices = replicas * lax.axis_size("expert")
    owned = blocks // replicas
    base = min(width, 256)
    matrix = jnp.asarray(hadamard(base), jnp.bfloat16)
    me = lax.axis_index("dp")
    near = replicas // 2
    params = pltpu.CompilerParams(vmem_limit_bytes=vmem_bytes)
    array = pl.BlockSpec(memory_space=pltpu.VMEM)

    def pair_of(source, index):
        source = source.reshape(2, near, owned, width)
        return lax.dynamic_slice_in_dim(source, index % near, 1, 1).reshape(2, owned, width)

    def block_of(source, index):
        source = source.reshape(replicas, owned, width)
        return lax.dynamic_slice_in_dim(source, index, 1, 0).reshape(owned, width)

    x_count = chips_along_x(replicas)
    aligned = [m for m in range(1, near) if m % x_count == 0 or m < x_count]
    diagonal = [m for m in range(1, near) if m not in aligned]
    pairs = [swap(pair_of(grads, me ^ mask), mask) for mask in aligned]
    far_pieces = [swap(block_of(grads, me ^ mask ^ near), mask) for mask in diagonal]
    sums = pl.pallas_call(
        sums_kernel,
        in_specs=[array],
        out_shape=jax.ShapeDtypeStruct((2, near, 1, 2 * owned), jnp.float32),
        compiler_params=params,
        name="sum_squares",
    )(grads.reshape(2, near, owned, width))
    later, sums = lax.optimization_barrier((grads, sums))
    sums = lax.all_to_all(
        sums.reshape(replicas, 1, 2 * owned), "dp", split_axis=0, concat_axis=0, tiled=True
    ).reshape(replicas, 2 * owned)
    pairs.append(pair_of(later, me))
    far_pieces = pairs + far_pieces
    near_pieces = pairs + [swap(block_of(later, me ^ mask), mask) for mask in diagonal]
    sent = pl.pallas_call(
        functools.partial(proxy_kernel, near, base),
        in_specs=[array] * (near + 3),
        out_shape=jax.ShapeDtypeStruct((owned, width), jnp.int16),
        compiler_params=params,
        name="proxy_blocks",
    )(*far_pieces, sums, signs, matrix)
    far_total = swap(sent, near)
    near_total = pl.pallas_call(
        functools.partial(owner_kernel, near, base),
        in_specs=[array] * (near + 3),
        out_shape=jax.ShapeDtypeStruct((owned, width), jnp.float32),
        compiler_params=params,
        name="owner_blocks",
    )(*near_pieces, sums, signs, matrix)
    total, mean_scale, squares = pl.pallas_call(
        functools.partial(finish_kernel, near),
        in_specs=[array] * 3,
        out_shape=(
            jax.ShapeDtypeStruct((owned, width), jnp.float32),
            jax.ShapeDtypeStruct((owned, lanes), jnp.float32),
            jax.ShapeDtypeStruct((devices, 1, lanes), jnp.float32),
        ),
        compiler_params=params,
        name="finish_blocks",
    )(near_total, far_total, sums)
    unrot = pl.pallas_call(
        functools.partial(back_kernel, base),
        out_shape=jax.ShapeDtypeStruct((owned, width), jnp.float32),
        compiler_params=params,
        name="rotate_back",
    )(total, mean_scale, signs, matrix)
    squares = lax.all_to_all(squares, ("dp", "expert"), split_axis=0, concat_axis=0, tiled=True)
    limit = target_rms * math.sqrt(blocks * width * lax.axis_size("expert"))
    squares = squares.reshape(devices, lanes)
    new_weights = pl.pallas_call(
        functools.partial(weights_kernel, limit),
        out_shape=jax.ShapeDtypeStruct((owned, width), jnp.bfloat16),
        compiler_params=params,
        name="new_weights",
    )(squares, unrot, weights.reshape(owned, width), compensation.reshape(owned, width))
    update_grad = pl.pallas_call(
        functools.partial(update_kernel, limit),
        out_shape=jax.ShapeDtypeStruct((owned, width), jnp.float32),
        compiler_params=params,
        name="update_grad",
    )(squares, unrot)
    return gather_blocks(new_weights, replicas), update_grad.reshape(weights.shape)


def solution(mesh):
    in_specs = (
        P("dp", "expert", None, None),
        P("expert", None),
        P("expert", "dp", None),
        P("expert", "dp", None),
    )
    out_specs = (P("expert", None, None), P("expert", "dp", None))
    return jax.shard_map(
        on_device, mesh=mesh, in_specs=in_specs, out_specs=out_specs, check_vma=False
    )
```

```python
import functools
import math

import jax
import jax.numpy as jnp
import numpy as np
from jax import lax
from jax.experimental import pallas as pl
from jax.experimental.pallas import tpu as pltpu
from jax.sharding import PartitionSpec as P

clamp_level = 2.0
target_rms = 0.2
learn_rate = 0.02
lanes = 128
vmem_bytes = 40 * 1024 * 1024


def hadamard(width):
    matrix = np.ones((1, 1), np.float32)
    while matrix.shape[0] < width:
        matrix = np.block([[matrix, matrix], [matrix, -matrix]])
    return matrix


def butterfly(groups):
    half = 1
    groups = list(groups)
    while half < len(groups):
        for start in range(0, len(groups), 2 * half):
            for i in range(start, start + half):
                upper, lower = groups[i], groups[i + half]
                groups[i], groups[i + half] = upper + lower, upper - lower
        half *= 2
    return groups


def rotate_groups(pieces, matrix, base):
    count = pieces[0].shape[1] // base
    groups = []
    for g in range(count):
        part = None
        for piece in pieces:
            term = jnp.dot(
                piece[:, g * base : (g + 1) * base], matrix, preferred_element_type=jnp.float32
            )
            part = term if part is None else part + term
        groups.append(part)
    return butterfly(groups)


def sums_kernel(x_ref, sums_ref):
    near, owned, width = x_ref.shape[1:]
    shape = (2 * owned, 2 * owned)
    row, lane = (lax.broadcasted_iota(jnp.int32, shape, axis) for axis in (0, 1))
    for j in range(near):
        rows = x_ref[:, j].reshape(2 * owned, width).astype(jnp.float32)
        squares = jnp.sum(rows * rows, axis=1, keepdims=True)
        line = jnp.sum(jnp.where(row == lane, squares, 0.0), axis=0, keepdims=True)
        sums_ref[0, j] = line
        sums_ref[1, j] = line


def scale_rows(sums_ref, offset, owned, width, near):
    biggest = jnp.max(sums_ref[...], axis=0, keepdims=True)
    shape = (owned, 2 * owned)
    row, lane = (lax.broadcasted_iota(jnp.int32, shape, axis) for axis in (0, 1))
    biggest = jnp.sum(jnp.where(lane == row + offset, biggest, 0.0), axis=1, keepdims=True)
    mean = biggest * (1.0 / width)
    scale = jnp.sqrt(mean + 1e-06)
    peak = jnp.sqrt(mean * width) / scale
    step = near * jnp.where(
        peak >= clamp_level, clamp_level / 32768.0, jnp.maximum(peak, 1e-20) / 32767.0
    )
    return scale, step


def add_levels(pieces, scale, sign_ref, matrix_ref, base):
    width = pieces[0].shape[1]
    signs = sign_ref[...].astype(jnp.float32).astype(jnp.bfloat16)
    matrix = matrix_ref[...]
    inverse = (1.0 / math.sqrt(width)) / scale
    totals = None
    for piece in pieces:
        groups = rotate_groups([piece[...] * signs], matrix, base)
        levels = [
            jnp.clip(group * inverse, -clamp_level, clamp_level)
            .astype(jnp.bfloat16)
            .astype(jnp.float32)
            for group in groups
        ]
        totals = levels if totals is None else [t + v for t, v in zip(totals, levels)]
    return totals


def proxy_kernel(near, base, *refs):
    pieces, (sums_ref, sign_ref, matrix_ref, sent_ref) = refs[:near], refs[near:]
    owned, width = sent_ref.shape
    half = 1 - lax.axis_index("dp") // near
    scale, step = scale_rows(sums_ref, half * owned, owned, width, near)
    totals = add_levels(pieces, scale, sign_ref, matrix_ref, base)
    for g, total in enumerate(totals):
        value = jnp.clip(jnp.round(total / step), -32767.0, 32767.0)
        sent_ref[:, g * base : (g + 1) * base] = value.astype(jnp.int16)


def owner_kernel(near, base, *refs):
    pieces, (sums_ref, sign_ref, matrix_ref, total_ref) = refs[:near], refs[near:]
    owned, width = total_ref.shape
    half = lax.axis_index("dp") // near
    scale, _ = scale_rows(sums_ref, half * owned, owned, width, near)
    totals = add_levels(pieces, scale, sign_ref, matrix_ref, base)
    for g, total in enumerate(totals):
        total_ref[:, g * base : (g + 1) * base] = total


def finish_kernel(
    near, near_ref, far_ref, sums_ref, total_ref, scale_ref, square_ref
):
    owned, width = near_ref.shape
    scale, step = scale_rows(
        sums_ref, lax.axis_index("dp") // near * owned, owned, width, near
    )
    total = near_ref[...] + far_ref[...].astype(jnp.float32) * step
    mean_scale = scale / (2 * near)
    mean_rot = total * mean_scale
    squares = jnp.sum(mean_rot * mean_rot)
    square_ref[...] = jnp.full(square_ref.shape, squares, jnp.float32)
    total_ref[...] = total
    scale_ref[...] = jnp.broadcast_to(mean_scale, scale_ref.shape)


def back_kernel(base, total_ref, scale_ref, sign_ref, matrix_ref, unrot_ref):
    owned, width = total_ref.shape
    total = total_ref[...]
    high = total.astype(jnp.bfloat16)
    low = (total - high.astype(jnp.float32)).astype(jnp.bfloat16)
    groups = rotate_groups([high, low], matrix_ref[...], base)
    back = scale_ref[:, 0:1] * (1.0 / math.sqrt(width))
    signs = sign_ref[...].astype(jnp.float32)
    for g, group in enumerate(groups):
        cut = slice(g * base, (g + 1) * base)
        unrot_ref[:, cut] = group * back * signs[:, cut]


def clip_factor(limit, square_ref):
    squares = jnp.sum(square_ref[...], axis=0, keepdims=True)[:, 0:1]
    return limit / jnp.maximum(jnp.sqrt(squares), limit)


def weights_kernel(limit, square_ref, unrot_ref, weight_ref, comp_ref, new_ref):
    update = unrot_ref[...] * clip_factor(limit, square_ref)
    summed = weight_ref[...].astype(jnp.float32) + (
        comp_ref[...].astype(jnp.float32) - learn_rate * update
    )
    new_ref[...] = summed.astype(jnp.bfloat16)


def update_kernel(limit, square_ref, unrot_ref, update_ref):
    update_ref[...] = unrot_ref[...] * clip_factor(limit, square_ref)


def swap(value, mask):
    size = lax.axis_size("dp")
    return lax.ppermute(value, "dp", [(i, i ^ mask) for i in range(size)])


def place_kernel(places, owned, *refs):
    pieces, out_ref, sem = refs[: len(places)], refs[-2], refs[-1]
    me = lax.axis_index("dp")
    copies = []
    for i, ((mask, row), piece) in enumerate(zip(places, pieces)):
        start = pl.multiple_of((me ^ mask) * owned + row, 16)
        rows = pl.ds(start, piece.shape[0])
        copies.append(pltpu.make_async_copy(piece, out_ref.at[rows], sem.at[i]))
    for copy in copies:
        copy.start()
    for copy in copies:
        copy.wait()


def place_pieces(items, owned, replicas, out, name):
    places = [(mask, row) for mask, row, _ in items]
    values = [piece for _, _, piece in items]
    operands, aliases = list(values), {}
    specs = [pl.BlockSpec(memory_space=pltpu.VMEM)] * len(values)
    if out is not None:
        aliases = {len(operands): 0}
        operands.append(out)
        specs.append(pl.BlockSpec(memory_space=pl.ANY))
    width = values[0].shape[1]
    return pl.pallas_call(
        functools.partial(place_kernel, places, owned),
        in_specs=specs,
        out_specs=pl.BlockSpec(memory_space=pl.ANY),
        out_shape=jax.ShapeDtypeStruct((replicas * owned, width), values[0].dtype),
        scratch_shapes=[pltpu.SemaphoreType.DMA((len(values),))],
        input_output_aliases=aliases,
        compiler_params=pltpu.CompilerParams(vmem_limit_bytes=vmem_bytes),
        name=name,
    )(*operands)


def gather_blocks(block, replicas):
    near = replicas // 2
    owned, width = block.shape
    far = swap(block, near)
    own = [(0, 0, block)] + [(m, 0, swap(block, m)) for m in reversed(range(1, near))]
    spread = [(near + m, 0, swap(far, m)) for m in range(1, near)]
    out = place_pieces(own + [(near, 0, far)], owned, replicas, None, "place_own")
    out = place_pieces(spread, owned, replicas, out, "place_far")
    return out.reshape(1, replicas * owned, width)


def on_device(grads, signs, weights, compensation):
    blocks, width = grads.shape[2:]
    replicas = lax.axis_size("dp")
    devices = replicas * lax.axis_size("expert")
    owned = blocks // replicas
    base = min(width, 256)
    matrix = jnp.asarray(hadamard(base), jnp.bfloat16)
    me = lax.axis_index("dp")
    near = replicas // 2
    params = pltpu.CompilerParams(vmem_limit_bytes=vmem_bytes)
    array = pl.BlockSpec(memory_space=pltpu.VMEM)

    def block_of(source, index):
        source = source.reshape(replicas, owned, width)
        return lax.dynamic_slice_in_dim(source, index, 1, 0).reshape(owned, width)

    far_pieces = [swap(block_of(grads, me ^ mask ^ near), mask) for mask in range(1, near)]
    sums = pl.pallas_call(
        sums_kernel,
        in_specs=[array],
        out_shape=jax.ShapeDtypeStruct((2, near, 1, 2 * owned), jnp.float32),
        compiler_params=params,
        name="sum_squares",
    )(grads.reshape(2, near, owned, width))
    later, sums = lax.optimization_barrier((grads, sums))
    sums = lax.all_to_all(
        sums.reshape(replicas, 1, 2 * owned), "dp", split_axis=0, concat_axis=0, tiled=True
    ).reshape(replicas, 2 * owned)
    near_pieces = [swap(block_of(later, me ^ mask), mask) for mask in range(1, near)]
    far_pieces.append(block_of(later, me ^ near))
    near_pieces.append(block_of(later, me))
    sent = pl.pallas_call(
        functools.partial(proxy_kernel, near, base),
        in_specs=[array] * (near + 3),
        out_shape=jax.ShapeDtypeStruct((owned, width), jnp.int16),
        compiler_params=params,
        name="proxy_blocks",
    )(*far_pieces, sums, signs, matrix)
    far_total = swap(sent, near)
    near_total = pl.pallas_call(
        functools.partial(owner_kernel, near, base),
        in_specs=[array] * (near + 3),
        out_shape=jax.ShapeDtypeStruct((owned, width), jnp.float32),
        compiler_params=params,
        name="owner_blocks",
    )(*near_pieces, sums, signs, matrix)
    total, mean_scale, squares = pl.pallas_call(
        functools.partial(finish_kernel, near),
        in_specs=[array] * 3,
        out_shape=(
            jax.ShapeDtypeStruct((owned, width), jnp.float32),
            jax.ShapeDtypeStruct((owned, lanes), jnp.float32),
            jax.ShapeDtypeStruct((devices, 1, lanes), jnp.float32),
        ),
        compiler_params=params,
        name="finish_blocks",
    )(near_total, far_total, sums)
    unrot = pl.pallas_call(
        functools.partial(back_kernel, base),
        out_shape=jax.ShapeDtypeStruct((owned, width), jnp.float32),
        compiler_params=params,
        name="rotate_back",
    )(total, mean_scale, signs, matrix)
    squares = lax.all_to_all(squares, ("dp", "expert"), split_axis=0, concat_axis=0, tiled=True)
    limit = target_rms * math.sqrt(blocks * width * lax.axis_size("expert"))
    squares = squares.reshape(devices, lanes)
    new_weights = pl.pallas_call(
        functools.partial(weights_kernel, limit),
        out_shape=jax.ShapeDtypeStruct((owned, width), jnp.bfloat16),
        compiler_params=params,
        name="new_weights",
    )(squares, unrot, weights.reshape(owned, width), compensation.reshape(owned, width))
    update_grad = pl.pallas_call(
        functools.partial(update_kernel, limit),
        out_shape=jax.ShapeDtypeStruct((owned, width), jnp.float32),
        compiler_params=params,
        name="update_grad",
    )(squares, unrot)
    return gather_blocks(new_weights, replicas), update_grad.reshape(weights.shape)


def solution(mesh):
    in_specs = (
        P("dp", "expert", None, None),
        P("expert", None),
        P("expert", "dp", None),
        P("expert", "dp", None),
    )
    out_specs = (P("expert", None, None), P("expert", "dp", None))
    return jax.shard_map(
        on_device, mesh=mesh, in_specs=in_specs, out_specs=out_specs, check_vma=False
    )
```

```python
import functools
import math

import jax
import jax.numpy as jnp
import numpy as np
from jax import lax
from jax.experimental import pallas as pl
from jax.experimental.pallas import tpu as pltpu
from jax.sharding import PartitionSpec as P

clamp_level = 2.0
target_rms = 0.2
learn_rate = 0.02
lanes = 128
vmem_bytes = 40 * 1024 * 1024


def hadamard(width):
    matrix = np.ones((1, 1), np.float32)
    while matrix.shape[0] < width:
        matrix = np.block([[matrix, matrix], [matrix, -matrix]])
    return matrix


def butterfly(groups):
    half = 1
    groups = list(groups)
    while half < len(groups):
        for start in range(0, len(groups), 2 * half):
            for i in range(start, start + half):
                upper, lower = groups[i], groups[i + half]
                groups[i], groups[i + half] = upper + lower, upper - lower
        half *= 2
    return groups


def rotate_groups(pieces, matrix, base):
    count = pieces[0].shape[1] // base
    groups = []
    for g in range(count):
        part = None
        for piece in pieces:
            term = jnp.dot(
                piece[:, g * base : (g + 1) * base], matrix, preferred_element_type=jnp.float32
            )
            part = term if part is None else part + term
        groups.append(part)
    return butterfly(groups)


def sums_kernel(x_ref, sums_ref):
    near, owned, width = x_ref.shape[1:]
    shape = (2 * owned, 2 * owned)
    row, lane = (lax.broadcasted_iota(jnp.int32, shape, axis) for axis in (0, 1))
    for j in range(near):
        rows = x_ref[:, j].reshape(2 * owned, width).astype(jnp.float32)
        squares = jnp.sum(rows * rows, axis=1, keepdims=True)
        line = jnp.sum(jnp.where(row == lane, squares, 0.0), axis=0, keepdims=True)
        sums_ref[0, j] = line
        sums_ref[1, j] = line


def scale_rows(sums_ref, offset, owned, width, near):
    biggest = jnp.max(sums_ref[...], axis=0, keepdims=True)
    shape = (owned, 2 * owned)
    row, lane = (lax.broadcasted_iota(jnp.int32, shape, axis) for axis in (0, 1))
    biggest = jnp.sum(jnp.where(lane == row + offset, biggest, 0.0), axis=1, keepdims=True)
    mean = biggest * (1.0 / width)
    scale = jnp.sqrt(mean + 1e-06)
    peak = jnp.sqrt(mean * width) / scale
    step = near * jnp.where(
        peak >= clamp_level, clamp_level / 32768.0, jnp.maximum(peak, 1e-20) / 32767.0
    )
    return scale, step


def add_levels(pieces, half, scale, sign_ref, matrix_ref, base):
    width = pieces[0].shape[-1]
    signs = sign_ref[...].astype(jnp.float32).astype(jnp.bfloat16)
    matrix = matrix_ref[...]
    inverse = (1.0 / math.sqrt(width)) / scale
    totals = None
    for piece in pieces:
        rows = piece[...] if len(piece.shape) == 2 else piece[half]
        groups = rotate_groups([rows * signs], matrix, base)
        levels = [
            jnp.clip(group * inverse, -clamp_level, clamp_level)
            .astype(jnp.bfloat16)
            .astype(jnp.float32)
            for group in groups
        ]
        totals = levels if totals is None else [t + v for t, v in zip(totals, levels)]
    return totals


def proxy_kernel(near, base, *refs):
    pieces, (sums_ref, sign_ref, matrix_ref, sent_ref) = refs[:near], refs[near:]
    owned, width = sent_ref.shape
    half = 1 - lax.axis_index("dp") // near
    scale, step = scale_rows(sums_ref, half * owned, owned, width, near)
    totals = add_levels(pieces, half, scale, sign_ref, matrix_ref, base)
    for g, total in enumerate(totals):
        value = jnp.clip(jnp.round(total / step), -32767.0, 32767.0)
        sent_ref[:, g * base : (g + 1) * base] = value.astype(jnp.int16)


def owner_kernel(near, base, *refs):
    pieces, rest = refs[:near], refs[near:]
    sums_ref, sign_ref, matrix_ref, total_ref, scale_ref, step_ref = rest
    owned, width = total_ref.shape
    half = lax.axis_index("dp") // near
    scale, step = scale_rows(sums_ref, half * owned, owned, width, near)
    totals = add_levels(pieces, half, scale, sign_ref, matrix_ref, base)
    for g, total in enumerate(totals):
        total_ref[:, g * base : (g + 1) * base] = total
    scale_ref[...] = jnp.broadcast_to(scale / (2 * near), scale_ref.shape)
    step_ref[...] = jnp.broadcast_to(step, step_ref.shape)


def finish_kernel(near_ref, far_ref, scale_ref, step_ref, total_ref, square_ref):
    width = near_ref.shape[1]
    step = step_ref[...]
    squares = None
    for start in range(0, width, lanes):
        cut = slice(start, start + lanes)
        total = near_ref[:, cut] + far_ref[:, cut].astype(jnp.float32) * step
        total_ref[:, cut] = total
        squares = total * total if squares is None else squares + total * total
    scale = scale_ref[...]
    squares = jnp.sum(squares * (scale * scale))
    square_ref[...] = jnp.full(square_ref.shape, squares, jnp.float32)


def back_kernel(base, total_ref, scale_ref, sign_ref, matrix_ref, unrot_ref):
    owned, width = total_ref.shape
    total = total_ref[...]
    high = total.astype(jnp.bfloat16)
    low = (total - high.astype(jnp.float32)).astype(jnp.bfloat16)
    groups = rotate_groups([high, low], matrix_ref[...], base)
    back = scale_ref[:, 0:1] * (1.0 / math.sqrt(width))
    signs = sign_ref[...].astype(jnp.float32)
    for g, group in enumerate(groups):
        cut = slice(g * base, (g + 1) * base)
        unrot_ref[:, cut] = group * back * signs[:, cut]


def clip_factor(limit, square_ref):
    squares = jnp.sum(square_ref[...], axis=0, keepdims=True)[:, 0:1]
    return limit / jnp.maximum(jnp.sqrt(squares), limit)


def weights_kernel(limit, square_ref, unrot_ref, weight_ref, comp_ref, new_ref):
    update = unrot_ref[...] * clip_factor(limit, square_ref)
    summed = weight_ref[...].astype(jnp.float32) + (
        comp_ref[...].astype(jnp.float32) - learn_rate * update
    )
    new_ref[...] = summed.astype(jnp.bfloat16)


def update_kernel(limit, square_ref, unrot_ref, update_ref):
    update_ref[...] = unrot_ref[...] * clip_factor(limit, square_ref)


def chips_along_x(replicas):
    return 1 << ((replicas.bit_length() - 1) // 2)


def swap(value, mask):
    size = lax.axis_size("dp")
    return lax.ppermute(value, "dp", [(i, i ^ mask) for i in range(size)])


def place_kernel(places, owned, *refs):
    pieces, out_ref, sem = refs[: len(places)], refs[-2], refs[-1]
    me = lax.axis_index("dp")
    copies = []
    for i, ((mask, row), piece) in enumerate(zip(places, pieces)):
        start = pl.multiple_of((me ^ mask) * owned + row, 16)
        rows = pl.ds(start, piece.shape[0])
        copies.append(pltpu.make_async_copy(piece, out_ref.at[rows], sem.at[i]))
    for copy in copies:
        copy.start()
    for copy in copies:
        copy.wait()


def place_pieces(items, owned, replicas, out, name):
    places = [(mask, row) for mask, row, _ in items]
    values = [piece for _, _, piece in items]
    operands, aliases = list(values), {}
    specs = [pl.BlockSpec(memory_space=pltpu.VMEM)] * len(values)
    if out is not None:
        aliases = {len(operands): 0}
        operands.append(out)
        specs.append(pl.BlockSpec(memory_space=pl.ANY))
    width = values[0].shape[1]
    return pl.pallas_call(
        functools.partial(place_kernel, places, owned),
        in_specs=specs,
        out_specs=pl.BlockSpec(memory_space=pl.ANY),
        out_shape=jax.ShapeDtypeStruct((replicas * owned, width), values[0].dtype),
        scratch_shapes=[pltpu.SemaphoreType.DMA((len(values),))],
        input_output_aliases=aliases,
        compiler_params=pltpu.CompilerParams(vmem_limit_bytes=vmem_bytes),
        name=name,
    )(*operands)


def gather_blocks(block, replicas):
    near = replicas // 2
    owned, width = block.shape
    far = swap(block, near)
    own = [(0, 0, block)] + [(m, 0, swap(block, m)) for m in reversed(range(1, near))]
    spread = [(near + m, 0, swap(far, m)) for m in range(1, near)]
    out = place_pieces(own + [(near, 0, far)], owned, replicas, None, "place_own")
    out = place_pieces(spread, owned, replicas, out, "place_far")
    return out.reshape(1, replicas * owned, width)


def on_device(grads, signs, weights, compensation):
    blocks, width = grads.shape[2:]
    replicas = lax.axis_size("dp")
    devices = replicas * lax.axis_size("expert")
    owned = blocks // replicas
    base = min(width, 256)
    matrix = jnp.asarray(hadamard(base), jnp.bfloat16)
    me = lax.axis_index("dp")
    near = replicas // 2
    params = pltpu.CompilerParams(vmem_limit_bytes=vmem_bytes)
    array = pl.BlockSpec(memory_space=pltpu.VMEM)

    def pair_of(source, index):
        source = source.reshape(2, near, owned, width)
        return lax.dynamic_slice_in_dim(source, index % near, 1, 1).reshape(2, owned, width)

    def block_of(source, index):
        source = source.reshape(replicas, owned, width)
        return lax.dynamic_slice_in_dim(source, index, 1, 0).reshape(owned, width)

    x_count = chips_along_x(replicas)
    aligned = [m for m in range(1, near) if m % x_count == 0 or m < x_count]
    diagonal = [m for m in range(1, near) if m not in aligned]
    pairs = [swap(pair_of(grads, me ^ mask), mask) for mask in aligned]
    sums = pl.pallas_call(
        sums_kernel,
        in_specs=[array],
        out_shape=jax.ShapeDtypeStruct((2, near, 1, 2 * owned), jnp.float32),
        compiler_params=params,
        name="sum_squares",
    )(grads.reshape(2, near, owned, width))
    later, sums = lax.optimization_barrier((grads, sums))
    sums = lax.all_to_all(
        sums.reshape(replicas, 1, 2 * owned), "dp", split_axis=0, concat_axis=0, tiled=True
    ).reshape(replicas, 2 * owned)
    far_pieces = [swap(block_of(later, me ^ mask ^ near), mask) for mask in diagonal]
    near_pieces = [swap(block_of(later, me ^ mask), mask) for mask in diagonal]
    pairs.append(pair_of(later, me))
    far_pieces, near_pieces = pairs + far_pieces, pairs + near_pieces
    sent = pl.pallas_call(
        functools.partial(proxy_kernel, near, base),
        in_specs=[array] * (near + 3),
        out_shape=jax.ShapeDtypeStruct((owned, width), jnp.int16),
        compiler_params=params,
        name="proxy_blocks",
    )(*far_pieces, sums, signs, matrix)
    far_total = swap(sent, near)
    column = jax.ShapeDtypeStruct((owned, lanes), jnp.float32)
    near_total, mean_scale, step = pl.pallas_call(
        functools.partial(owner_kernel, near, base),
        in_specs=[array] * (near + 3),
        out_shape=(jax.ShapeDtypeStruct((owned, width), jnp.float32), column, column),
        compiler_params=params,
        name="owner_blocks",
    )(*near_pieces, sums, signs, matrix)
    total, squares = pl.pallas_call(
        finish_kernel,
        in_specs=[array] * 4,
        out_shape=(
            jax.ShapeDtypeStruct((owned, width), jnp.float32),
            jax.ShapeDtypeStruct((devices, 1, lanes), jnp.float32),
        ),
        compiler_params=params,
        name="finish_blocks",
    )(near_total, far_total, mean_scale, step)
    unrot = pl.pallas_call(
        functools.partial(back_kernel, base),
        out_shape=jax.ShapeDtypeStruct((owned, width), jnp.float32),
        compiler_params=params,
        name="rotate_back",
    )(total, mean_scale, signs, matrix)
    squares = lax.all_to_all(squares, ("dp", "expert"), split_axis=0, concat_axis=0, tiled=True)
    limit = target_rms * math.sqrt(blocks * width * lax.axis_size("expert"))
    squares = squares.reshape(devices, lanes)
    new_weights = pl.pallas_call(
        functools.partial(weights_kernel, limit),
        out_shape=jax.ShapeDtypeStruct((owned, width), jnp.bfloat16),
        compiler_params=params,
        name="new_weights",
    )(squares, unrot, weights.reshape(owned, width), compensation.reshape(owned, width))
    update_grad = pl.pallas_call(
        functools.partial(update_kernel, limit),
        out_shape=jax.ShapeDtypeStruct((owned, width), jnp.float32),
        compiler_params=params,
        name="update_grad",
    )(squares, unrot)
    return gather_blocks(new_weights, replicas), update_grad.reshape(weights.shape)


def solution(mesh):
    in_specs = (
        P("dp", "expert", None, None),
        P("expert", None),
        P("expert", "dp", None),
        P("expert", "dp", None),
    )
    out_specs = (P("expert", None, None), P("expert", "dp", None))
    return jax.shard_map(
        on_device, mesh=mesh, in_specs=in_specs, out_specs=out_specs, check_vma=False
    )
```

```python
import functools
import math

import jax
import jax.numpy as jnp
import numpy as np
from jax import lax
from jax.experimental import pallas as pl
from jax.experimental.pallas import tpu as pltpu
from jax.sharding import PartitionSpec as P

clamp_level = 2.0
target_rms = 0.2
learn_rate = 0.02
lanes = 128
vmem_bytes = 40 * 1024 * 1024


def hadamard(width):
    matrix = np.ones((1, 1), np.float32)
    while matrix.shape[0] < width:
        matrix = np.block([[matrix, matrix], [matrix, -matrix]])
    return matrix


def butterfly(groups):
    half = 1
    groups = list(groups)
    while half < len(groups):
        for start in range(0, len(groups), 2 * half):
            for i in range(start, start + half):
                upper, lower = groups[i], groups[i + half]
                groups[i], groups[i + half] = upper + lower, upper - lower
        half *= 2
    return groups


def rotate_groups(pieces, matrix, base):
    count = pieces[0].shape[1] // base
    groups = []
    for g in range(count):
        part = None
        for piece in pieces:
            term = jnp.dot(
                piece[:, g * base : (g + 1) * base], matrix, preferred_element_type=jnp.float32
            )
            part = term if part is None else part + term
        groups.append(part)
    return butterfly(groups)


def sums_kernel(x_ref, sums_ref):
    near, owned, width = x_ref.shape[1:]
    shape = (2 * owned, 2 * owned)
    row, lane = (lax.broadcasted_iota(jnp.int32, shape, axis) for axis in (0, 1))
    for j in range(near):
        rows = x_ref[:, j].reshape(2 * owned, width).astype(jnp.float32)
        squares = jnp.sum(rows * rows, axis=1, keepdims=True)
        line = jnp.sum(jnp.where(row == lane, squares, 0.0), axis=0, keepdims=True)
        sums_ref[0, j] = line
        sums_ref[1, j] = line


def scale_rows(sums_ref, offset, owned, width, near):
    biggest = jnp.max(sums_ref[...], axis=0, keepdims=True)
    shape = (owned, 2 * owned)
    row, lane = (lax.broadcasted_iota(jnp.int32, shape, axis) for axis in (0, 1))
    biggest = jnp.sum(jnp.where(lane == row + offset, biggest, 0.0), axis=1, keepdims=True)
    mean = biggest * (1.0 / width)
    scale = jnp.sqrt(mean + 1e-06)
    peak = jnp.sqrt(mean * width) / scale
    step = near * jnp.where(
        peak >= clamp_level, clamp_level / 32768.0, jnp.maximum(peak, 1e-20) / 32767.0
    )
    return scale, step


def add_levels(pieces, half, inverse, sign_ref, matrix_ref, base, totals=None):
    signs = sign_ref[...].astype(jnp.float32).astype(jnp.bfloat16)
    matrix = matrix_ref[...]
    for piece in pieces:
        rows = piece[...] if len(piece.shape) == 2 else piece[half]
        groups = rotate_groups([rows * signs], matrix, base)
        levels = [
            jnp.clip(group * inverse, -clamp_level, clamp_level)
            .astype(jnp.bfloat16)
            .astype(jnp.float32)
            for group in groups
        ]
        totals = levels if totals is None else [t + v for t, v in zip(totals, levels)]
    return totals


def proxy_pairs_kernel(near, count, base, *refs):
    pieces, rest = refs[:count], refs[count:]
    sums_ref, sign_ref, matrix_ref, total_ref, inverse_ref, step_ref = rest
    owned, width = total_ref.shape
    half = 1 - lax.axis_index("dp") // near
    scale, step = scale_rows(sums_ref, half * owned, owned, width, near)
    inverse = (1.0 / math.sqrt(width)) / scale
    totals = add_levels(pieces, half, inverse, sign_ref, matrix_ref, base)
    for g, total in enumerate(totals):
        total_ref[:, g * base : (g + 1) * base] = total
    inverse_ref[...] = jnp.broadcast_to(inverse, inverse_ref.shape)
    step_ref[...] = jnp.broadcast_to(1.0 / step, step_ref.shape)


def proxy_kernel(count, base, *refs):
    pieces, rest = refs[:count], refs[count:]
    total_ref, inverse_ref, step_ref, sign_ref, matrix_ref, sent_ref = rest
    cuts = [slice(start, start + base) for start in range(0, total_ref.shape[1], base)]
    totals = [total_ref[:, cut] for cut in cuts]
    totals = add_levels(pieces, 0, inverse_ref[:, 0:1], sign_ref, matrix_ref, base, totals)
    steps = step_ref[:, 0:1]
    for cut, total in zip(cuts, totals):
        value = jnp.clip(jnp.round(total * steps), -32767.0, 32767.0)
        sent_ref[:, cut] = value.astype(jnp.int16)


def owner_kernel(near, base, *refs):
    pieces, rest = refs[:near], refs[near:]
    sums_ref, sign_ref, matrix_ref, total_ref, scale_ref, step_ref = rest
    owned, width = total_ref.shape
    half = lax.axis_index("dp") // near
    scale, step = scale_rows(sums_ref, half * owned, owned, width, near)
    inverse = (1.0 / math.sqrt(width)) / scale
    totals = add_levels(pieces, half, inverse, sign_ref, matrix_ref, base)
    for g, total in enumerate(totals):
        total_ref[:, g * base : (g + 1) * base] = total
    scale_ref[...] = jnp.broadcast_to(scale / (2 * near), scale_ref.shape)
    step_ref[...] = jnp.broadcast_to(step, step_ref.shape)


def finish_kernel(near_ref, far_ref, scale_ref, step_ref, total_ref, square_ref):
    width = near_ref.shape[1]
    step = step_ref[...]
    squares = None
    for start in range(0, width, lanes):
        cut = slice(start, start + lanes)
        total = near_ref[:, cut] + far_ref[:, cut].astype(jnp.float32) * step
        total_ref[:, cut] = total
        squares = total * total if squares is None else squares + total * total
    scale = scale_ref[...]
    squares = jnp.sum(squares * (scale * scale), axis=0, keepdims=True)
    square_ref[...] = jnp.broadcast_to(squares[None], square_ref.shape)


def back_kernel(base, total_ref, scale_ref, sign_ref, matrix_ref, unrot_ref):
    owned, width = total_ref.shape
    total = total_ref[...]
    high = total.astype(jnp.bfloat16)
    low = (total - high.astype(jnp.float32)).astype(jnp.bfloat16)
    groups = rotate_groups([high, low], matrix_ref[...], base)
    back = scale_ref[:, 0:1] * (1.0 / math.sqrt(width))
    signs = sign_ref[...].astype(jnp.float32)
    for g, group in enumerate(groups):
        cut = slice(g * base, (g + 1) * base)
        unrot_ref[:, cut] = group * back * signs[:, cut]


def clip_factor(limit, square_ref):
    squares = jnp.sum(jnp.sum(square_ref[...], axis=0, keepdims=True), axis=1, keepdims=True)
    return limit / jnp.maximum(jnp.sqrt(squares), limit)


def weights_kernel(limit, square_ref, unrot_ref, weight_ref, comp_ref, new_ref):
    update = unrot_ref[...] * clip_factor(limit, square_ref)
    summed = weight_ref[...].astype(jnp.float32) + (
        comp_ref[...].astype(jnp.float32) - learn_rate * update
    )
    new_ref[...] = summed.astype(jnp.bfloat16)


def update_kernel(limit, square_ref, unrot_ref, update_ref):
    update_ref[...] = unrot_ref[...] * clip_factor(limit, square_ref)


def chips_along_x(replicas):
    return 1 << ((replicas.bit_length() - 1) // 2)


def swap(value, mask):
    size = lax.axis_size("dp")
    return lax.ppermute(value, "dp", [(i, i ^ mask) for i in range(size)])


def place_kernel(places, owned, *refs):
    pieces, out_ref, sem = refs[: len(places)], refs[-2], refs[-1]
    me = lax.axis_index("dp")
    copies = []
    for i, ((mask, row), piece) in enumerate(zip(places, pieces)):
        start = pl.multiple_of((me ^ mask) * owned + row, 16)
        rows = pl.ds(start, piece.shape[0])
        copies.append(pltpu.make_async_copy(piece, out_ref.at[rows], sem.at[i]))
    for copy in copies:
        copy.start()
    for copy in copies:
        copy.wait()


def place_pieces(items, owned, replicas, out, name):
    places = [(mask, row) for mask, row, _ in items]
    values = [piece for _, _, piece in items]
    operands, aliases = list(values), {}
    specs = [pl.BlockSpec(memory_space=pltpu.VMEM)] * len(values)
    if out is not None:
        aliases = {len(operands): 0}
        operands.append(out)
        specs.append(pl.BlockSpec(memory_space=pl.ANY))
    width = values[0].shape[1]
    return pl.pallas_call(
        functools.partial(place_kernel, places, owned),
        in_specs=specs,
        out_specs=pl.BlockSpec(memory_space=pl.ANY),
        out_shape=jax.ShapeDtypeStruct((replicas * owned, width), values[0].dtype),
        scratch_shapes=[pltpu.SemaphoreType.DMA((len(values),))],
        input_output_aliases=aliases,
        compiler_params=pltpu.CompilerParams(vmem_limit_bytes=vmem_bytes),
        name=name,
    )(*operands)


def gather_blocks(block, replicas):
    near = replicas // 2
    owned, width = block.shape
    far = swap(block, near)
    own = [(0, 0, block)] + [(m, 0, swap(block, m)) for m in reversed(range(1, near))]
    spread = [(near + m, 0, swap(far, m)) for m in range(1, near)]
    out = place_pieces(own + [(near, 0, far)], owned, replicas, None, "place_own")
    out = place_pieces(spread, owned, replicas, out, "place_far")
    return out.reshape(1, replicas * owned, width)


def on_device(grads, signs, weights, compensation):
    blocks, width = grads.shape[2:]
    replicas = lax.axis_size("dp")
    devices = replicas * lax.axis_size("expert")
    owned = blocks // replicas
    base = min(width, 256)
    matrix = jnp.asarray(hadamard(base), jnp.bfloat16)
    me = lax.axis_index("dp")
    near = replicas // 2
    params = pltpu.CompilerParams(vmem_limit_bytes=vmem_bytes)
    array = pl.BlockSpec(memory_space=pltpu.VMEM)

    def pair_of(source, index):
        source = source.reshape(2, near, owned, width)
        return lax.dynamic_slice_in_dim(source, index % near, 1, 1).reshape(2, owned, width)

    def block_of(source, index):
        source = source.reshape(replicas, owned, width)
        return lax.dynamic_slice_in_dim(source, index, 1, 0).reshape(owned, width)

    x_count = chips_along_x(replicas)
    aligned = [m for m in range(1, near) if m % x_count == 0 or m < x_count]
    diagonal = [m for m in range(1, near) if m not in aligned]
    pairs = [swap(pair_of(grads, me ^ mask), mask) for mask in aligned]
    sums = pl.pallas_call(
        sums_kernel,
        in_specs=[array],
        out_shape=jax.ShapeDtypeStruct((2, near, 1, 2 * owned), jnp.float32),
        compiler_params=params,
        name="sum_squares",
    )(grads.reshape(2, near, owned, width))
    later, sums = lax.optimization_barrier((grads, sums))
    sums = lax.all_to_all(
        sums.reshape(replicas, 1, 2 * owned), "dp", split_axis=0, concat_axis=0, tiled=True
    ).reshape(replicas, 2 * owned)
    far_pieces = [swap(block_of(later, me ^ mask ^ near), mask) for mask in diagonal]
    near_pieces = [swap(block_of(later, me ^ mask), mask) for mask in diagonal]
    pairs.append(pair_of(later, me))
    whole = jax.ShapeDtypeStruct((owned, width), jnp.float32)
    column = jax.ShapeDtypeStruct((owned, lanes), jnp.float32)
    part, inverse, step = pl.pallas_call(
        functools.partial(proxy_pairs_kernel, near, len(pairs), base),
        in_specs=[array] * (len(pairs) + 3),
        out_shape=(whole, column, column),
        compiler_params=params,
        name="proxy_pairs",
    )(*pairs, sums, signs, matrix)
    sent = pl.pallas_call(
        functools.partial(proxy_kernel, len(far_pieces), base),
        in_specs=[array] * (len(far_pieces) + 5),
        out_shape=jax.ShapeDtypeStruct((owned, width), jnp.int16),
        compiler_params=params,
        name="proxy_blocks",
    )(*far_pieces, part, inverse, step, signs, matrix)
    far_total = swap(sent, near)
    near_total, mean_scale, step = pl.pallas_call(
        functools.partial(owner_kernel, near, base),
        in_specs=[array] * (near + 3),
        out_shape=(whole, column, column),
        compiler_params=params,
        name="owner_blocks",
    )(*pairs, *near_pieces, sums, signs, matrix)
    total, squares = pl.pallas_call(
        finish_kernel,
        in_specs=[array] * 4,
        out_shape=(
            jax.ShapeDtypeStruct((owned, width), jnp.float32),
            jax.ShapeDtypeStruct((devices, 1, lanes), jnp.float32),
        ),
        compiler_params=params,
        name="finish_blocks",
    )(near_total, far_total, mean_scale, step)
    unrot = pl.pallas_call(
        functools.partial(back_kernel, base),
        out_shape=jax.ShapeDtypeStruct((owned, width), jnp.float32),
        compiler_params=params,
        name="rotate_back",
    )(total, mean_scale, signs, matrix)
    squares = lax.all_to_all(squares, ("dp", "expert"), split_axis=0, concat_axis=0, tiled=True)
    limit = target_rms * math.sqrt(blocks * width * lax.axis_size("expert"))
    squares = squares.reshape(devices, lanes)
    new_weights = pl.pallas_call(
        functools.partial(weights_kernel, limit),
        out_shape=jax.ShapeDtypeStruct((owned, width), jnp.bfloat16),
        compiler_params=params,
        name="new_weights",
    )(squares, unrot, weights.reshape(owned, width), compensation.reshape(owned, width))
    update_grad = pl.pallas_call(
        functools.partial(update_kernel, limit),
        out_shape=jax.ShapeDtypeStruct((owned, width), jnp.float32),
        compiler_params=params,
        name="update_grad",
    )(squares, unrot)
    return gather_blocks(new_weights, replicas), update_grad.reshape(weights.shape)


def solution(mesh):
    in_specs = (
        P("dp", "expert", None, None),
        P("expert", None),
        P("expert", "dp", None),
        P("expert", "dp", None),
    )
    out_specs = (P("expert", None, None), P("expert", "dp", None))
    return jax.shard_map(
        on_device, mesh=mesh, in_specs=in_specs, out_specs=out_specs, check_vma=False
    )
```

```python
import functools
import math

import jax
import jax.numpy as jnp
import numpy as np
from jax import lax
from jax.experimental import pallas as pl
from jax.experimental.pallas import tpu as pltpu
from jax.sharding import PartitionSpec as P

clamp_level = 2.0
target_rms = 0.2
learn_rate = 0.02
lanes = 128
vmem_bytes = 40 * 1024 * 1024


def hadamard(width):
    matrix = np.ones((1, 1), np.float32)
    while matrix.shape[0] < width:
        matrix = np.block([[matrix, matrix], [matrix, -matrix]])
    return matrix


def butterfly(groups):
    half = 1
    groups = list(groups)
    while half < len(groups):
        for start in range(0, len(groups), 2 * half):
            for i in range(start, start + half):
                upper, lower = groups[i], groups[i + half]
                groups[i], groups[i + half] = upper + lower, upper - lower
        half *= 2
    return groups


def rotate_groups(pieces, matrix, base):
    count = pieces[0].shape[1] // base
    groups = []
    for g in range(count):
        part = None
        for piece in pieces:
            term = jnp.dot(
                piece[:, g * base : (g + 1) * base], matrix, preferred_element_type=jnp.float32
            )
            part = term if part is None else part + term
        groups.append(part)
    return butterfly(groups)


def sums_kernel(x_ref, sums_ref):
    near, owned, width = x_ref.shape[1:]
    shape = (2 * owned, 2 * owned)
    row, lane = (lax.broadcasted_iota(jnp.int32, shape, axis) for axis in (0, 1))
    for j in range(near):
        rows = x_ref[:, j].reshape(2 * owned, width).astype(jnp.float32)
        squares = jnp.sum(rows * rows, axis=1, keepdims=True)
        line = jnp.sum(jnp.where(row == lane, squares, 0.0), axis=0, keepdims=True)
        sums_ref[0, j] = line
        sums_ref[1, j] = line


def scale_rows(sums_ref, offset, owned, width, near):
    biggest = jnp.max(sums_ref[...], axis=0, keepdims=True)
    shape = (owned, 2 * owned)
    row, lane = (lax.broadcasted_iota(jnp.int32, shape, axis) for axis in (0, 1))
    biggest = jnp.sum(jnp.where(lane == row + offset, biggest, 0.0), axis=1, keepdims=True)
    mean = biggest * (1.0 / width)
    scale = jnp.sqrt(mean + 1e-06)
    peak = jnp.sqrt(mean * width) / scale
    step = near * jnp.where(
        peak >= clamp_level, clamp_level / 32768.0, jnp.maximum(peak, 1e-20) / 32767.0
    )
    return scale, step


def add_levels(pieces, half, inverse, sign_ref, matrix_ref, base, totals=None):
    signs = sign_ref[...].astype(jnp.float32).astype(jnp.bfloat16)
    matrix = matrix_ref[...]
    for piece in pieces:
        rows = piece[...] if len(piece.shape) == 2 else piece[half]
        groups = rotate_groups([rows * signs], matrix, base)
        levels = [
            jnp.clip(group * inverse, -clamp_level, clamp_level)
            .astype(jnp.bfloat16)
            .astype(jnp.float32)
            for group in groups
        ]
        totals = levels if totals is None else [t + v for t, v in zip(totals, levels)]
    return totals


def proxy_pairs_kernel(near, count, base, *refs):
    pieces, rest = refs[:count], refs[count:]
    sums_ref, sign_ref, matrix_ref, total_ref, inverse_ref, step_ref = rest
    owned, width = total_ref.shape
    half = 1 - lax.axis_index("dp") // near
    scale, step = scale_rows(sums_ref, half * owned, owned, width, near)
    inverse = (1.0 / math.sqrt(width)) / scale
    totals = add_levels(pieces, half, inverse, sign_ref, matrix_ref, base)
    for g, total in enumerate(totals):
        total_ref[:, g * base : (g + 1) * base] = total
    inverse_ref[...] = jnp.broadcast_to(inverse, inverse_ref.shape)
    step_ref[...] = jnp.broadcast_to(1.0 / step, step_ref.shape)


def proxy_kernel(count, base, *refs):
    pieces, rest = refs[:count], refs[count:]
    total_ref, inverse_ref, step_ref, sign_ref, matrix_ref, sent_ref = rest
    cuts = [slice(start, start + base) for start in range(0, total_ref.shape[1], base)]
    totals = [total_ref[:, cut] for cut in cuts]
    totals = add_levels(pieces, 0, inverse_ref[:, 0:1], sign_ref, matrix_ref, base, totals)
    steps = step_ref[:, 0:1]
    for cut, total in zip(cuts, totals):
        value = jnp.clip(jnp.round(total * steps), -32767.0, 32767.0)
        sent_ref[:, cut] = value.astype(jnp.int16)


def owner_kernel(near, base, *refs):
    pieces, rest = refs[:near], refs[near:]
    sums_ref, sign_ref, matrix_ref, total_ref, scale_ref, step_ref = rest
    owned, width = total_ref.shape
    half = lax.axis_index("dp") // near
    scale, step = scale_rows(sums_ref, half * owned, owned, width, near)
    inverse = (1.0 / math.sqrt(width)) / scale
    totals = add_levels(pieces, half, inverse, sign_ref, matrix_ref, base)
    for g, total in enumerate(totals):
        total_ref[:, g * base : (g + 1) * base] = total
    scale_ref[...] = jnp.broadcast_to(scale / (2 * near), scale_ref.shape)
    step_ref[...] = jnp.broadcast_to(step, step_ref.shape)


def finish_kernel(near_ref, far_ref, scale_ref, step_ref, total_ref, square_ref):
    width = near_ref.shape[1]
    step = step_ref[...]
    squares = None
    for start in range(0, width, lanes):
        cut = slice(start, start + lanes)
        total = near_ref[:, cut] + far_ref[:, cut].astype(jnp.float32) * step
        total_ref[:, cut] = total
        squares = total * total if squares is None else squares + total * total
    scale = scale_ref[...]
    squares = jnp.sum(squares * (scale * scale), axis=0, keepdims=True)
    square_ref[...] = jnp.broadcast_to(squares[None], square_ref.shape)


def back_kernel(base, total_ref, scale_ref, sign_ref, matrix_ref, unrot_ref):
    owned, width = total_ref.shape
    total = total_ref[...]
    high = total.astype(jnp.bfloat16)
    low = (total - high.astype(jnp.float32)).astype(jnp.bfloat16)
    groups = rotate_groups([high, low], matrix_ref[...], base)
    back = scale_ref[:, 0:1] * (1.0 / math.sqrt(width))
    signs = sign_ref[...].astype(jnp.float32)
    for g, group in enumerate(groups):
        cut = slice(g * base, (g + 1) * base)
        unrot_ref[:, cut] = group * back * signs[:, cut]


def clip_factor(limit, square_ref):
    squares = jnp.sum(jnp.sum(square_ref[...], axis=0, keepdims=True), axis=1, keepdims=True)
    return limit / jnp.maximum(jnp.sqrt(squares), limit)


def weights_kernel(limit, square_ref, unrot_ref, weight_ref, comp_ref, new_ref):
    update = unrot_ref[...] * clip_factor(limit, square_ref)
    summed = weight_ref[...].astype(jnp.float32) + (
        comp_ref[...].astype(jnp.float32) - learn_rate * update
    )
    new_ref[...] = summed.astype(jnp.bfloat16)


def update_kernel(limit, square_ref, unrot_ref, update_ref):
    update_ref[...] = unrot_ref[...] * clip_factor(limit, square_ref)


def chips_along_x(replicas):
    return 1 << ((replicas.bit_length() - 1) // 2)


def swap(value, mask):
    size = lax.axis_size("dp")
    return lax.ppermute(value, "dp", [(i, i ^ mask) for i in range(size)])


def place_kernel(places, owned, *refs):
    pieces, out_ref, sem = refs[: len(places)], refs[-2], refs[-1]
    me = lax.axis_index("dp")
    copies = []
    for i, ((mask, row), piece) in enumerate(zip(places, pieces)):
        start = pl.multiple_of((me ^ mask) * owned + row, 16)
        rows = pl.ds(start, piece.shape[0])
        copies.append(pltpu.make_async_copy(piece, out_ref.at[rows], sem.at[i]))
    for copy in copies:
        copy.start()
    for copy in copies:
        copy.wait()


def place_pieces(items, owned, replicas, out, name):
    places = [(mask, row) for mask, row, _ in items]
    values = [piece for _, _, piece in items]
    operands, aliases = list(values), {}
    specs = [pl.BlockSpec(memory_space=pltpu.VMEM)] * len(values)
    if out is not None:
        aliases = {len(operands): 0}
        operands.append(out)
        specs.append(pl.BlockSpec(memory_space=pl.ANY))
    width = values[0].shape[1]
    return pl.pallas_call(
        functools.partial(place_kernel, places, owned),
        in_specs=specs,
        out_specs=pl.BlockSpec(memory_space=pl.ANY),
        out_shape=jax.ShapeDtypeStruct((replicas * owned, width), values[0].dtype),
        scratch_shapes=[pltpu.SemaphoreType.DMA((len(values),))],
        input_output_aliases=aliases,
        compiler_params=pltpu.CompilerParams(vmem_limit_bytes=vmem_bytes),
        name=name,
    )(*operands)


def gather_blocks(block, replicas):
    x_count = chips_along_x(replicas)
    near = replicas // 2
    owned, width = block.shape
    far = swap(block, near)
    own = {0: block}
    for m in range(1, near):
        own[m] = swap(block, m) if m < x_count or m % x_count == 0 else None
    for m in range(1, near):
        if own[m] is None:
            own[m] = swap(own[m - m % x_count], m % x_count)
    own = [(m, 0, piece) for m, piece in own.items()]
    spread = [(near + m, 0, swap(far, m)) for m in range(1, near)]
    out = place_pieces(own + [(near, 0, far)], owned, replicas, None, "place_own")
    out = place_pieces(spread, owned, replicas, out, "place_far")
    return out.reshape(1, replicas * owned, width)


def on_device(grads, signs, weights, compensation):
    blocks, width = grads.shape[2:]
    replicas = lax.axis_size("dp")
    devices = replicas * lax.axis_size("expert")
    owned = blocks // replicas
    base = min(width, 256)
    matrix = jnp.asarray(hadamard(base), jnp.bfloat16)
    me = lax.axis_index("dp")
    near = replicas // 2
    params = pltpu.CompilerParams(vmem_limit_bytes=vmem_bytes)
    array = pl.BlockSpec(memory_space=pltpu.VMEM)

    def pair_of(source, index):
        source = source.reshape(2, near, owned, width)
        return lax.dynamic_slice_in_dim(source, index % near, 1, 1).reshape(2, owned, width)

    def block_of(source, index):
        source = source.reshape(replicas, owned, width)
        return lax.dynamic_slice_in_dim(source, index, 1, 0).reshape(owned, width)

    x_count = chips_along_x(replicas)
    aligned = [m for m in range(1, near) if m % x_count == 0 or m < x_count]
    diagonal = [m for m in range(1, near) if m not in aligned]
    pairs = [swap(pair_of(grads, me ^ mask), mask) for mask in aligned]
    sums = pl.pallas_call(
        sums_kernel,
        in_specs=[array],
        out_shape=jax.ShapeDtypeStruct((2, near, 1, 2 * owned), jnp.float32),
        compiler_params=params,
        name="sum_squares",
    )(grads.reshape(2, near, owned, width))
    later, sums = lax.optimization_barrier((grads, sums))
    sums = lax.all_to_all(
        sums.reshape(replicas, 1, 2 * owned), "dp", split_axis=0, concat_axis=0, tiled=True
    ).reshape(replicas, 2 * owned)
    far_pieces = [swap(block_of(later, me ^ mask ^ near), mask) for mask in diagonal]
    near_pieces = [swap(block_of(later, me ^ mask), mask) for mask in diagonal]
    pairs.append(pair_of(later, me))
    whole = jax.ShapeDtypeStruct((owned, width), jnp.float32)
    column = jax.ShapeDtypeStruct((owned, lanes), jnp.float32)
    part, inverse, step = pl.pallas_call(
        functools.partial(proxy_pairs_kernel, near, len(pairs), base),
        in_specs=[array] * (len(pairs) + 3),
        out_shape=(whole, column, column),
        compiler_params=params,
        name="proxy_pairs",
    )(*pairs, sums, signs, matrix)
    sent = pl.pallas_call(
        functools.partial(proxy_kernel, len(far_pieces), base),
        in_specs=[array] * (len(far_pieces) + 5),
        out_shape=jax.ShapeDtypeStruct((owned, width), jnp.int16),
        compiler_params=params,
        name="proxy_blocks",
    )(*far_pieces, part, inverse, step, signs, matrix)
    far_total = swap(sent, near)
    near_total, mean_scale, step = pl.pallas_call(
        functools.partial(owner_kernel, near, base),
        in_specs=[array] * (near + 3),
        out_shape=(whole, column, column),
        compiler_params=params,
        name="owner_blocks",
    )(*pairs, *near_pieces, sums, signs, matrix)
    total, squares = pl.pallas_call(
        finish_kernel,
        in_specs=[array] * 4,
        out_shape=(
            jax.ShapeDtypeStruct((owned, width), jnp.float32),
            jax.ShapeDtypeStruct((devices, 1, lanes), jnp.float32),
        ),
        compiler_params=params,
        name="finish_blocks",
    )(near_total, far_total, mean_scale, step)
    unrot = pl.pallas_call(
        functools.partial(back_kernel, base),
        out_shape=jax.ShapeDtypeStruct((owned, width), jnp.float32),
        compiler_params=params,
        name="rotate_back",
    )(total, mean_scale, signs, matrix)
    squares = lax.all_to_all(squares, ("dp", "expert"), split_axis=0, concat_axis=0, tiled=True)
    limit = target_rms * math.sqrt(blocks * width * lax.axis_size("expert"))
    squares = squares.reshape(devices, lanes)
    new_weights = pl.pallas_call(
        functools.partial(weights_kernel, limit),
        out_shape=jax.ShapeDtypeStruct((owned, width), jnp.bfloat16),
        compiler_params=params,
        name="new_weights",
    )(squares, unrot, weights.reshape(owned, width), compensation.reshape(owned, width))
    update_grad = pl.pallas_call(
        functools.partial(update_kernel, limit),
        out_shape=jax.ShapeDtypeStruct((owned, width), jnp.float32),
        compiler_params=params,
        name="update_grad",
    )(squares, unrot)
    return gather_blocks(new_weights, replicas), update_grad.reshape(weights.shape)


def solution(mesh):
    in_specs = (
        P("dp", "expert", None, None),
        P("expert", None),
        P("expert", "dp", None),
        P("expert", "dp", None),
    )
    out_specs = (P("expert", None, None), P("expert", "dp", None))
    return jax.shard_map(
        on_device, mesh=mesh, in_specs=in_specs, out_specs=out_specs, check_vma=False
    )
```

```python
import functools
import math

import jax
import jax.numpy as jnp
import numpy as np
from jax import lax
from jax.experimental import pallas as pl
from jax.experimental.pallas import tpu as pltpu
from jax.sharding import PartitionSpec as P

clamp_level = 2.0
target_rms = 0.2
learn_rate = 0.02
lanes = 128
vmem_bytes = 40 * 1024 * 1024


def hadamard(width):
    matrix = np.ones((1, 1), np.float32)
    while matrix.shape[0] < width:
        matrix = np.block([[matrix, matrix], [matrix, -matrix]])
    return matrix


def butterfly(groups):
    half = 1
    groups = list(groups)
    while half < len(groups):
        for start in range(0, len(groups), 2 * half):
            for i in range(start, start + half):
                upper, lower = groups[i], groups[i + half]
                groups[i], groups[i + half] = upper + lower, upper - lower
        half *= 2
    return groups


def rotate_groups(pieces, matrix, base):
    count = pieces[0].shape[1] // base
    groups = []
    for g in range(count):
        part = None
        for piece in pieces:
            term = jnp.dot(
                piece[:, g * base : (g + 1) * base], matrix, preferred_element_type=jnp.float32
            )
            part = term if part is None else part + term
        groups.append(part)
    return butterfly(groups)


def sums_kernel(x_ref, sums_ref):
    near, owned, width = x_ref.shape[1:]
    shape = (2 * owned, 2 * owned)
    row, lane = (lax.broadcasted_iota(jnp.int32, shape, axis) for axis in (0, 1))
    for j in range(near):
        rows = x_ref[:, j].reshape(2 * owned, width).astype(jnp.float32)
        squares = jnp.sum(rows * rows, axis=1, keepdims=True)
        line = jnp.sum(jnp.where(row == lane, squares, 0.0), axis=0, keepdims=True)
        sums_ref[0, j] = line
        sums_ref[1, j] = line


def scale_rows(sums_ref, offset, owned, width, near):
    biggest = jnp.max(sums_ref[...], axis=0, keepdims=True)
    shape = (owned, 2 * owned)
    row, lane = (lax.broadcasted_iota(jnp.int32, shape, axis) for axis in (0, 1))
    biggest = jnp.sum(jnp.where(lane == row + offset, biggest, 0.0), axis=1, keepdims=True)
    mean = biggest * (1.0 / width)
    scale = jnp.sqrt(mean + 1e-06)
    peak = jnp.sqrt(mean * width) / scale
    step = near * jnp.where(
        peak >= clamp_level, clamp_level / 32768.0, jnp.maximum(peak, 1e-20) / 32767.0
    )
    return scale, step


def add_levels(pieces, half, inverse, sign_ref, matrix_ref, base, totals=None):
    signs = sign_ref[...].astype(jnp.float32).astype(jnp.bfloat16)
    matrix = matrix_ref[...]
    for piece in pieces:
        rows = piece[...] if len(piece.shape) == 2 else piece[half]
        groups = rotate_groups([rows * signs], matrix, base)
        levels = [
            jnp.clip(group * inverse, -clamp_level, clamp_level)
            .astype(jnp.bfloat16)
            .astype(jnp.float32)
            for group in groups
        ]
        totals = levels if totals is None else [t + v for t, v in zip(totals, levels)]
    return totals


def proxy_pairs_kernel(near, count, base, *refs):
    pieces, rest = refs[:count], refs[count:]
    sums_ref, sign_ref, matrix_ref, total_ref, inverse_ref, step_ref = rest
    owned, width = total_ref.shape
    half = 1 - lax.axis_index("dp") // near
    scale, step = scale_rows(sums_ref, half * owned, owned, width, near)
    inverse = (1.0 / math.sqrt(width)) / scale
    totals = add_levels(pieces, half, inverse, sign_ref, matrix_ref, base)
    for g, total in enumerate(totals):
        total_ref[:, g * base : (g + 1) * base] = total
    inverse_ref[...] = jnp.broadcast_to(inverse, inverse_ref.shape)
    step_ref[...] = jnp.broadcast_to(1.0 / step, step_ref.shape)


def proxy_kernel(count, base, *refs):
    pieces, rest = refs[:count], refs[count:]
    total_ref, inverse_ref, step_ref, sign_ref, matrix_ref, sent_ref = rest
    cuts = [slice(start, start + base) for start in range(0, total_ref.shape[1], base)]
    totals = [total_ref[:, cut] for cut in cuts]
    totals = add_levels(pieces, 0, inverse_ref[:, 0:1], sign_ref, matrix_ref, base, totals)
    steps = step_ref[:, 0:1]
    for cut, total in zip(cuts, totals):
        value = jnp.clip(jnp.round(total * steps), -32767.0, 32767.0)
        sent_ref[:, cut] = value.astype(jnp.int16)


def owner_kernel(near, base, *refs):
    pieces, rest = refs[:near], refs[near:]
    sums_ref, sign_ref, matrix_ref, total_ref, scale_ref, step_ref = rest
    owned, width = total_ref.shape
    half = lax.axis_index("dp") // near
    scale, step = scale_rows(sums_ref, half * owned, owned, width, near)
    inverse = (1.0 / math.sqrt(width)) / scale
    totals = add_levels(pieces, half, inverse, sign_ref, matrix_ref, base)
    for g, total in enumerate(totals):
        total_ref[:, g * base : (g + 1) * base] = total
    scale_ref[...] = jnp.broadcast_to(scale / (2 * near), scale_ref.shape)
    step_ref[...] = jnp.broadcast_to(step, step_ref.shape)


def finish_kernel(near_ref, far_ref, scale_ref, step_ref, total_ref, square_ref):
    width = near_ref.shape[1]
    step = step_ref[...]
    squares = None
    for start in range(0, width, lanes):
        cut = slice(start, start + lanes)
        total = near_ref[:, cut] + far_ref[:, cut].astype(jnp.float32) * step
        total_ref[:, cut] = total
        squares = total * total if squares is None else squares + total * total
    scale = scale_ref[...]
    squares = jnp.sum(squares * (scale * scale), axis=0, keepdims=True)
    square_ref[...] = jnp.broadcast_to(squares[None], square_ref.shape)


def back_kernel(base, total_ref, scale_ref, sign_ref, matrix_ref, unrot_ref):
    owned, width = total_ref.shape
    total = total_ref[...]
    high = total.astype(jnp.bfloat16)
    low = (total - high.astype(jnp.float32)).astype(jnp.bfloat16)
    groups = rotate_groups([high, low], matrix_ref[...], base)
    back = scale_ref[:, 0:1] * (1.0 / math.sqrt(width))
    signs = sign_ref[...].astype(jnp.float32)
    for g, group in enumerate(groups):
        cut = slice(g * base, (g + 1) * base)
        unrot_ref[:, cut] = group * back * signs[:, cut]


def clip_factor(limit, square_ref):
    squares = jnp.sum(jnp.sum(square_ref[...], axis=0, keepdims=True), axis=1, keepdims=True)
    return limit / jnp.maximum(jnp.sqrt(squares), limit)


def weights_kernel(limit, square_ref, unrot_ref, weight_ref, comp_ref, new_ref):
    update = unrot_ref[...] * clip_factor(limit, square_ref)
    summed = weight_ref[...].astype(jnp.float32) + (
        comp_ref[...].astype(jnp.float32) - learn_rate * update
    )
    new_ref[...] = summed.astype(jnp.bfloat16)


def update_kernel(limit, square_ref, unrot_ref, update_ref):
    update_ref[...] = unrot_ref[...] * clip_factor(limit, square_ref)


def chips_along_x(replicas):
    return 1 << ((replicas.bit_length() - 1) // 2)


def swap(value, mask):
    size = lax.axis_size("dp")
    return lax.ppermute(value, "dp", [(i, i ^ mask) for i in range(size)])


def place_kernel(places, owned, *refs):
    pieces, out_ref, sem = refs[: len(places)], refs[-2], refs[-1]
    me = lax.axis_index("dp")
    copies = []
    for i, ((mask, row), piece) in enumerate(zip(places, pieces)):
        start = pl.multiple_of((me ^ mask) * owned + row, 16)
        rows = pl.ds(start, piece.shape[0])
        copies.append(pltpu.make_async_copy(piece, out_ref.at[rows], sem.at[i]))
    for copy in copies:
        copy.start()
    for copy in copies:
        copy.wait()


def place_pieces(items, owned, replicas, out, name):
    places = [(mask, row) for mask, row, _ in items]
    values = [piece for _, _, piece in items]
    operands, aliases = list(values), {}
    specs = [pl.BlockSpec(memory_space=pltpu.VMEM)] * len(values)
    if out is not None:
        aliases = {len(operands): 0}
        operands.append(out)
        specs.append(pl.BlockSpec(memory_space=pl.ANY))
    width = values[0].shape[1]
    return pl.pallas_call(
        functools.partial(place_kernel, places, owned),
        in_specs=specs,
        out_specs=pl.BlockSpec(memory_space=pl.ANY),
        out_shape=jax.ShapeDtypeStruct((replicas * owned, width), values[0].dtype),
        scratch_shapes=[pltpu.SemaphoreType.DMA((len(values),))],
        input_output_aliases=aliases,
        compiler_params=pltpu.CompilerParams(vmem_limit_bytes=vmem_bytes),
        name=name,
    )(*operands)


def gather_blocks(block, replicas):
    x_count = chips_along_x(replicas)
    near = replicas // 2
    owned, width = block.shape
    far = swap(block, near)
    own = {0: block}
    for m in range(1, near):
        own[m] = swap(block, m) if m < x_count or m % x_count == 0 else None
    for m in range(1, near):
        if own[m] is None:
            own[m] = swap(own[m - m % x_count], m % x_count)
    own = [(m, 0, piece) for m, piece in own.items()]
    order = [m for m in range(1, near) if m % x_count and m > x_count]
    order += [m for m in range(1, near) if m < x_count]
    order += [m for m in range(1, near) if m % x_count == 0]
    spread = [(near + m, 0, swap(far, m)) for m in order]
    out = place_pieces(own + [(near, 0, far)], owned, replicas, None, "place_own")
    out = place_pieces(spread, owned, replicas, out, "place_far")
    return out.reshape(1, replicas * owned, width)


def on_device(grads, signs, weights, compensation):
    blocks, width = grads.shape[2:]
    replicas = lax.axis_size("dp")
    devices = replicas * lax.axis_size("expert")
    owned = blocks // replicas
    base = min(width, 256)
    matrix = jnp.asarray(hadamard(base), jnp.bfloat16)
    me = lax.axis_index("dp")
    near = replicas // 2
    params = pltpu.CompilerParams(vmem_limit_bytes=vmem_bytes)
    array = pl.BlockSpec(memory_space=pltpu.VMEM)

    def pair_of(source, index):
        source = source.reshape(2, near, owned, width)
        return lax.dynamic_slice_in_dim(source, index % near, 1, 1).reshape(2, owned, width)

    def block_of(source, index):
        source = source.reshape(replicas, owned, width)
        return lax.dynamic_slice_in_dim(source, index, 1, 0).reshape(owned, width)

    x_count = chips_along_x(replicas)
    aligned = [m for m in range(1, near) if m % x_count == 0 or m < x_count]
    diagonal = [m for m in range(1, near) if m not in aligned]
    pairs = [swap(pair_of(grads, me ^ mask), mask) for mask in aligned]
    sums = pl.pallas_call(
        sums_kernel,
        in_specs=[array],
        out_shape=jax.ShapeDtypeStruct((2, near, 1, 2 * owned), jnp.float32),
        compiler_params=params,
        name="sum_squares",
    )(grads.reshape(2, near, owned, width))
    later, sums = lax.optimization_barrier((grads, sums))
    sums = lax.all_to_all(
        sums.reshape(replicas, 1, 2 * owned), "dp", split_axis=0, concat_axis=0, tiled=True
    ).reshape(replicas, 2 * owned)
    far_pieces = [swap(block_of(later, me ^ mask ^ near), mask) for mask in diagonal]
    near_pieces = [swap(block_of(later, me ^ mask), mask) for mask in diagonal]
    pairs.append(pair_of(later, me))
    whole = jax.ShapeDtypeStruct((owned, width), jnp.float32)
    column = jax.ShapeDtypeStruct((owned, lanes), jnp.float32)
    part, inverse, step = pl.pallas_call(
        functools.partial(proxy_pairs_kernel, near, len(pairs), base),
        in_specs=[array] * (len(pairs) + 3),
        out_shape=(whole, column, column),
        compiler_params=params,
        name="proxy_pairs",
    )(*pairs, sums, signs, matrix)
    sent = pl.pallas_call(
        functools.partial(proxy_kernel, len(far_pieces), base),
        in_specs=[array] * (len(far_pieces) + 5),
        out_shape=jax.ShapeDtypeStruct((owned, width), jnp.int16),
        compiler_params=params,
        name="proxy_blocks",
    )(*far_pieces, part, inverse, step, signs, matrix)
    far_total = swap(sent, near)
    near_total, mean_scale, step = pl.pallas_call(
        functools.partial(owner_kernel, near, base),
        in_specs=[array] * (near + 3),
        out_shape=(whole, column, column),
        compiler_params=params,
        name="owner_blocks",
    )(*pairs, *near_pieces, sums, signs, matrix)
    total, squares = pl.pallas_call(
        finish_kernel,
        in_specs=[array] * 4,
        out_shape=(
            jax.ShapeDtypeStruct((owned, width), jnp.float32),
            jax.ShapeDtypeStruct((devices, 1, lanes), jnp.float32),
        ),
        compiler_params=params,
        name="finish_blocks",
    )(near_total, far_total, mean_scale, step)
    unrot = pl.pallas_call(
        functools.partial(back_kernel, base),
        out_shape=jax.ShapeDtypeStruct((owned, width), jnp.float32),
        compiler_params=params,
        name="rotate_back",
    )(total, mean_scale, signs, matrix)
    squares = lax.all_to_all(squares, ("dp", "expert"), split_axis=0, concat_axis=0, tiled=True)
    limit = target_rms * math.sqrt(blocks * width * lax.axis_size("expert"))
    squares = squares.reshape(devices, lanes)
    new_weights = pl.pallas_call(
        functools.partial(weights_kernel, limit),
        out_shape=jax.ShapeDtypeStruct((owned, width), jnp.bfloat16),
        compiler_params=params,
        name="new_weights",
    )(squares, unrot, weights.reshape(owned, width), compensation.reshape(owned, width))
    update_grad = pl.pallas_call(
        functools.partial(update_kernel, limit),
        out_shape=jax.ShapeDtypeStruct((owned, width), jnp.float32),
        compiler_params=params,
        name="update_grad",
    )(squares, unrot)
    return gather_blocks(new_weights, replicas), update_grad.reshape(weights.shape)


def solution(mesh):
    in_specs = (
        P("dp", "expert", None, None),
        P("expert", None),
        P("expert", "dp", None),
        P("expert", "dp", None),
    )
    out_specs = (P("expert", None, None), P("expert", "dp", None))
    return jax.shard_map(
        on_device, mesh=mesh, in_specs=in_specs, out_specs=out_specs, check_vma=False
    )
```

```python
import functools
import math

import jax
import jax.numpy as jnp
import numpy as np
from jax import lax
from jax.experimental import pallas as pl
from jax.experimental.pallas import tpu as pltpu
from jax.sharding import PartitionSpec as P

clamp_level = 2.0
target_rms = 0.2
learn_rate = 0.02
lanes = 128
vmem_bytes = 40 * 1024 * 1024


def hadamard(width):
    matrix = np.ones((1, 1), np.float32)
    while matrix.shape[0] < width:
        matrix = np.block([[matrix, matrix], [matrix, -matrix]])
    return matrix


def butterfly(groups):
    half = 1
    groups = list(groups)
    while half < len(groups):
        for start in range(0, len(groups), 2 * half):
            for i in range(start, start + half):
                upper, lower = groups[i], groups[i + half]
                groups[i], groups[i + half] = upper + lower, upper - lower
        half *= 2
    return groups


def rotate_groups(pieces, matrix, base):
    count = pieces[0].shape[1] // base
    groups = []
    for g in range(count):
        part = None
        for piece in pieces:
            term = jnp.dot(
                piece[:, g * base : (g + 1) * base], matrix, preferred_element_type=jnp.float32
            )
            part = term if part is None else part + term
        groups.append(part)
    return butterfly(groups)


def sums_kernel(x_ref, sums_ref):
    near, owned, width = x_ref.shape[1:]
    shape = (2 * owned, 2 * owned)
    row, lane = (lax.broadcasted_iota(jnp.int32, shape, axis) for axis in (0, 1))
    for j in range(near):
        rows = x_ref[:, j].reshape(2 * owned, width).astype(jnp.float32)
        squares = jnp.sum(rows * rows, axis=1, keepdims=True)
        line = jnp.sum(jnp.where(row == lane, squares, 0.0), axis=0, keepdims=True)
        sums_ref[0, j] = line
        sums_ref[1, j] = line


def scale_rows(sums_ref, offset, owned, width, near):
    biggest = jnp.max(sums_ref[...], axis=0, keepdims=True)
    shape = (owned, 2 * owned)
    row, lane = (lax.broadcasted_iota(jnp.int32, shape, axis) for axis in (0, 1))
    biggest = jnp.sum(jnp.where(lane == row + offset, biggest, 0.0), axis=1, keepdims=True)
    mean = biggest * (1.0 / width)
    scale = jnp.sqrt(mean + 1e-06)
    peak = jnp.sqrt(mean * width) / scale
    step = near * jnp.where(
        peak >= clamp_level, clamp_level / 32768.0, jnp.maximum(peak, 1e-20) / 32767.0
    )
    return scale, step


def add_levels(pieces, half, inverse, sign_ref, matrix_ref, base, totals=None):
    signs = sign_ref[...].astype(jnp.float32).astype(jnp.bfloat16)
    matrix = matrix_ref[...]
    for piece in pieces:
        rows = piece[...] if len(piece.shape) == 2 else piece[half]
        groups = rotate_groups([rows * signs], matrix, base)
        levels = [
            jnp.clip(group * inverse, -clamp_level, clamp_level)
            .astype(jnp.bfloat16)
            .astype(jnp.float32)
            for group in groups
        ]
        totals = levels if totals is None else [t + v for t, v in zip(totals, levels)]
    return totals


def proxy_pairs_kernel(near, count, base, *refs):
    pieces, rest = refs[:count], refs[count:]
    sums_ref, sign_ref, matrix_ref, total_ref, inverse_ref, step_ref = rest
    owned, width = total_ref.shape
    half = 1 - lax.axis_index("dp") // near
    scale, step = scale_rows(sums_ref, half * owned, owned, width, near)
    inverse = (1.0 / math.sqrt(width)) / scale
    totals = add_levels(pieces, half, inverse, sign_ref, matrix_ref, base)
    for g, total in enumerate(totals):
        total_ref[:, g * base : (g + 1) * base] = total
    inverse_ref[...] = jnp.broadcast_to(inverse, inverse_ref.shape)
    step_ref[...] = jnp.broadcast_to(1.0 / step, step_ref.shape)


def proxy_kernel(count, base, *refs):
    pieces, rest = refs[:count], refs[count:]
    total_ref, inverse_ref, step_ref, sign_ref, matrix_ref, sent_ref = rest
    cuts = [slice(start, start + base) for start in range(0, total_ref.shape[1], base)]
    totals = [total_ref[:, cut] for cut in cuts]
    totals = add_levels(pieces, 0, inverse_ref[:, 0:1], sign_ref, matrix_ref, base, totals)
    steps = step_ref[:, 0:1]
    for cut, total in zip(cuts, totals):
        value = jnp.clip(jnp.round(total * steps), -32767.0, 32767.0)
        sent_ref[:, cut] = value.astype(jnp.int16)


def owner_kernel(near, base, *refs):
    pieces, rest = refs[:near], refs[near:]
    sums_ref, sign_ref, matrix_ref, total_ref, scale_ref, step_ref = rest
    owned, width = total_ref.shape
    half = lax.axis_index("dp") // near
    scale, step = scale_rows(sums_ref, half * owned, owned, width, near)
    inverse = (1.0 / math.sqrt(width)) / scale
    totals = add_levels(pieces, half, inverse, sign_ref, matrix_ref, base)
    for g, total in enumerate(totals):
        total_ref[:, g * base : (g + 1) * base] = total
    scale_ref[...] = jnp.broadcast_to(scale / (2 * near), scale_ref.shape)
    step_ref[...] = jnp.broadcast_to(step, step_ref.shape)


def finish_kernel(near_ref, far_ref, scale_ref, step_ref, total_ref, square_ref):
    width = near_ref.shape[1]
    step = step_ref[...]
    squares = None
    for start in range(0, width, lanes):
        cut = slice(start, start + lanes)
        total = near_ref[:, cut] + far_ref[:, cut].astype(jnp.float32) * step
        total_ref[:, cut] = total
        squares = total * total if squares is None else squares + total * total
    scale = scale_ref[...]
    squares = jnp.sum(squares * (scale * scale), axis=0, keepdims=True)
    square_ref[...] = jnp.broadcast_to(squares[None], square_ref.shape)


def back_kernel(base, total_ref, scale_ref, sign_ref, matrix_ref, unrot_ref):
    owned, width = total_ref.shape
    total = total_ref[...]
    high = total.astype(jnp.bfloat16)
    low = (total - high.astype(jnp.float32)).astype(jnp.bfloat16)
    groups = rotate_groups([high, low], matrix_ref[...], base)
    back = scale_ref[:, 0:1] * (1.0 / math.sqrt(width))
    signs = sign_ref[...].astype(jnp.float32)
    for g, group in enumerate(groups):
        cut = slice(g * base, (g + 1) * base)
        unrot_ref[:, cut] = group * back * signs[:, cut]


def clip_factor(limit, square_ref):
    squares = jnp.sum(jnp.sum(square_ref[...], axis=0, keepdims=True), axis=1, keepdims=True)
    return limit / jnp.maximum(jnp.sqrt(squares), limit)


def weights_kernel(limit, square_ref, unrot_ref, weight_ref, comp_ref, new_ref):
    update = unrot_ref[...] * clip_factor(limit, square_ref)
    summed = weight_ref[...].astype(jnp.float32) + (
        comp_ref[...].astype(jnp.float32) - learn_rate * update
    )
    new_ref[...] = summed.astype(jnp.bfloat16)


def update_kernel(limit, square_ref, unrot_ref, update_ref):
    update_ref[...] = unrot_ref[...] * clip_factor(limit, square_ref)


def chips_along_x(replicas):
    return 1 << ((replicas.bit_length() - 1) // 2)


def swap(value, mask):
    size = lax.axis_size("dp")
    return lax.ppermute(value, "dp", [(i, i ^ mask) for i in range(size)])


def place_kernel(places, owned, *refs):
    pieces, out_ref, sem = refs[: len(places)], refs[-2], refs[-1]
    me = lax.axis_index("dp")
    copies = []
    for i, ((mask, row), piece) in enumerate(zip(places, pieces)):
        start = pl.multiple_of((me ^ mask) * owned + row, 16)
        rows = pl.ds(start, piece.shape[0])
        copies.append(pltpu.make_async_copy(piece, out_ref.at[rows], sem.at[i]))
    for copy in copies:
        copy.start()
    for copy in copies:
        copy.wait()


def place_pieces(items, owned, replicas, out, name):
    places = [(mask, row) for mask, row, _ in items]
    values = [piece for _, _, piece in items]
    operands, aliases = list(values), {}
    specs = [pl.BlockSpec(memory_space=pltpu.VMEM)] * len(values)
    if out is not None:
        aliases = {len(operands): 0}
        operands.append(out)
        specs.append(pl.BlockSpec(memory_space=pl.ANY))
    width = values[0].shape[1]
    return pl.pallas_call(
        functools.partial(place_kernel, places, owned),
        in_specs=specs,
        out_specs=pl.BlockSpec(memory_space=pl.ANY),
        out_shape=jax.ShapeDtypeStruct((replicas * owned, width), values[0].dtype),
        scratch_shapes=[pltpu.SemaphoreType.DMA((len(values),))],
        input_output_aliases=aliases,
        compiler_params=pltpu.CompilerParams(vmem_limit_bytes=vmem_bytes),
        name=name,
    )(*operands)


def gather_blocks(block, replicas):
    x_count = chips_along_x(replicas)
    near = replicas // 2
    owned, width = block.shape
    far = swap(block, near)
    own = {0: block}
    for m in range(1, near):
        own[m] = swap(block, m) if m < x_count or m % x_count == 0 else None
    for m in range(1, near):
        if own[m] is None:
            own[m] = swap(own[m - m % x_count], m % x_count)
    own = [(m, 0, piece) for m, piece in own.items()]
    spread = [(near + m, 0, swap(far, m)) for m in range(1, near)]
    out = place_pieces(own + [(near, 0, far)], owned, replicas, None, "place_own")
    out = place_pieces(spread, owned, replicas, out, "place_far")
    return out.reshape(1, replicas * owned, width)


def on_device(grads, signs, weights, compensation):
    blocks, width = grads.shape[2:]
    replicas = lax.axis_size("dp")
    devices = replicas * lax.axis_size("expert")
    owned = blocks // replicas
    base = min(width, 256)
    matrix = jnp.asarray(hadamard(base), jnp.bfloat16)
    me = lax.axis_index("dp")
    near = replicas // 2
    params = pltpu.CompilerParams(vmem_limit_bytes=vmem_bytes)
    array = pl.BlockSpec(memory_space=pltpu.VMEM)

    def pair_of(source, index):
        source = source.reshape(2, near, owned, width)
        return lax.dynamic_slice_in_dim(source, index % near, 1, 1).reshape(2, owned, width)

    def block_of(source, index):
        source = source.reshape(replicas, owned, width)
        return lax.dynamic_slice_in_dim(source, index, 1, 0).reshape(owned, width)

    x_count = chips_along_x(replicas)
    aligned = [m for m in range(1, near) if m % x_count == 0 or m < x_count]
    diagonal = [m for m in range(1, near) if m not in aligned]
    pairs = [swap(pair_of(grads, me ^ mask), mask) for mask in aligned]
    sums = pl.pallas_call(
        sums_kernel,
        in_specs=[array],
        out_shape=jax.ShapeDtypeStruct((2, near, 1, 2 * owned), jnp.float32),
        compiler_params=params,
        name="sum_squares",
    )(grads.reshape(2, near, owned, width))
    later, sums = lax.optimization_barrier((grads, sums))
    sums = lax.all_to_all(
        sums.reshape(replicas, 1, 2 * owned), "dp", split_axis=0, concat_axis=0, tiled=True
    ).reshape(replicas, 2 * owned)
    far_pieces = [swap(block_of(later, me ^ mask ^ near), mask) for mask in diagonal]
    near_pieces = [swap(block_of(later, me ^ mask), mask) for mask in diagonal]
    pairs.append(pair_of(later, me))
    whole = jax.ShapeDtypeStruct((owned, width), jnp.float32)
    column = jax.ShapeDtypeStruct((owned, lanes), jnp.float32)
    part, inverse, step = pl.pallas_call(
        functools.partial(proxy_pairs_kernel, near, len(pairs), base),
        in_specs=[array] * (len(pairs) + 3),
        out_shape=(whole, column, column),
        compiler_params=params,
        cost_estimate=pl.CostEstimate(
            flops=20000000000, bytes_accessed=4 * blocks * width, transcendentals=0
        ),
        name="proxy_pairs",
    )(*pairs, sums, signs, matrix)
    sent = pl.pallas_call(
        functools.partial(proxy_kernel, len(far_pieces), base),
        in_specs=[array] * (len(far_pieces) + 5),
        out_shape=jax.ShapeDtypeStruct((owned, width), jnp.int16),
        compiler_params=params,
        name="proxy_blocks",
    )(*far_pieces, part, inverse, step, signs, matrix)
    far_total = swap(sent, near)
    near_total, mean_scale, step = pl.pallas_call(
        functools.partial(owner_kernel, near, base),
        in_specs=[array] * (near + 3),
        out_shape=(whole, column, column),
        compiler_params=params,
        name="owner_blocks",
    )(*pairs, *near_pieces, sums, signs, matrix)
    total, squares = pl.pallas_call(
        finish_kernel,
        in_specs=[array] * 4,
        out_shape=(
            jax.ShapeDtypeStruct((owned, width), jnp.float32),
            jax.ShapeDtypeStruct((devices, 1, lanes), jnp.float32),
        ),
        compiler_params=params,
        name="finish_blocks",
    )(near_total, far_total, mean_scale, step)
    unrot = pl.pallas_call(
        functools.partial(back_kernel, base),
        out_shape=jax.ShapeDtypeStruct((owned, width), jnp.float32),
        compiler_params=params,
        name="rotate_back",
    )(total, mean_scale, signs, matrix)
    squares = lax.all_to_all(squares, ("dp", "expert"), split_axis=0, concat_axis=0, tiled=True)
    limit = target_rms * math.sqrt(blocks * width * lax.axis_size("expert"))
    squares = squares.reshape(devices, lanes)
    new_weights = pl.pallas_call(
        functools.partial(weights_kernel, limit),
        out_shape=jax.ShapeDtypeStruct((owned, width), jnp.bfloat16),
        compiler_params=params,
        name="new_weights",
    )(squares, unrot, weights.reshape(owned, width), compensation.reshape(owned, width))
    update_grad = pl.pallas_call(
        functools.partial(update_kernel, limit),
        out_shape=jax.ShapeDtypeStruct((owned, width), jnp.float32),
        compiler_params=params,
        name="update_grad",
    )(squares, unrot)
    return gather_blocks(new_weights, replicas), update_grad.reshape(weights.shape)


def solution(mesh):
    in_specs = (
        P("dp", "expert", None, None),
        P("expert", None),
        P("expert", "dp", None),
        P("expert", "dp", None),
    )
    out_specs = (P("expert", None, None), P("expert", "dp", None))
    return jax.shard_map(
        on_device, mesh=mesh, in_specs=in_specs, out_specs=out_specs, check_vma=False
    )
```

```python
import functools
import math

import jax
import jax.numpy as jnp
import numpy as np
from jax import lax
from jax.experimental import pallas as pl
from jax.experimental.pallas import tpu as pltpu
from jax.sharding import PartitionSpec as P

clamp_level = 2.0
target_rms = 0.2
learn_rate = 0.02
lanes = 128
vmem_bytes = 40 * 1024 * 1024


def hadamard(width):
    matrix = np.ones((1, 1), np.float32)
    while matrix.shape[0] < width:
        matrix = np.block([[matrix, matrix], [matrix, -matrix]])
    return matrix


def butterfly(groups):
    half = 1
    groups = list(groups)
    while half < len(groups):
        for start in range(0, len(groups), 2 * half):
            for i in range(start, start + half):
                upper, lower = groups[i], groups[i + half]
                groups[i], groups[i + half] = upper + lower, upper - lower
        half *= 2
    return groups


def rotate_groups(pieces, matrix, base):
    count = pieces[0].shape[1] // base
    groups = []
    for g in range(count):
        part = None
        for piece in pieces:
            term = jnp.dot(
                piece[:, g * base : (g + 1) * base], matrix, preferred_element_type=jnp.float32
            )
            part = term if part is None else part + term
        groups.append(part)
    return butterfly(groups)


def sums_kernel(x_ref, sums_ref):
    near, owned, width = x_ref.shape[1:]
    shape = (2 * owned, 2 * owned)
    row, lane = (lax.broadcasted_iota(jnp.int32, shape, axis) for axis in (0, 1))
    for j in range(near):
        rows = x_ref[:, j].reshape(2 * owned, width).astype(jnp.float32)
        squares = jnp.sum(rows * rows, axis=1, keepdims=True)
        line = jnp.sum(jnp.where(row == lane, squares, 0.0), axis=0, keepdims=True)
        sums_ref[0, j] = line
        sums_ref[1, j] = line


def scale_rows(sums_ref, offset, owned, width, near):
    biggest = jnp.max(sums_ref[...], axis=0, keepdims=True)
    shape = (owned, 2 * owned)
    row, lane = (lax.broadcasted_iota(jnp.int32, shape, axis) for axis in (0, 1))
    biggest = jnp.sum(jnp.where(lane == row + offset, biggest, 0.0), axis=1, keepdims=True)
    mean = biggest * (1.0 / width)
    scale = jnp.sqrt(mean + 1e-06)
    peak = jnp.sqrt(mean * width) / scale
    step = near * jnp.where(
        peak >= clamp_level, clamp_level / 32768.0, jnp.maximum(peak, 1e-20) / 32767.0
    )
    return scale, step


def add_levels(pieces, half, inverse, sign_ref, matrix_ref, base, totals=None):
    signs = sign_ref[...].astype(jnp.float32).astype(jnp.bfloat16)
    matrix = matrix_ref[...]
    for piece in pieces:
        rows = piece[...] if len(piece.shape) == 2 else piece[half]
        groups = rotate_groups([rows * signs], matrix, base)
        levels = [
            jnp.clip(group * inverse, -clamp_level, clamp_level)
            .astype(jnp.bfloat16)
            .astype(jnp.float32)
            for group in groups
        ]
        totals = levels if totals is None else [t + v for t, v in zip(totals, levels)]
    return totals


def proxy_pairs_kernel(near, count, base, *refs):
    pieces, rest = refs[:count], refs[count:]
    sums_ref, sign_ref, matrix_ref, total_ref, inverse_ref, step_ref = rest
    owned, width = total_ref.shape
    half = 1 - lax.axis_index("dp") // near
    scale, step = scale_rows(sums_ref, half * owned, owned, width, near)
    inverse = (1.0 / math.sqrt(width)) / scale
    totals = add_levels(pieces, half, inverse, sign_ref, matrix_ref, base)
    for g, total in enumerate(totals):
        total_ref[:, g * base : (g + 1) * base] = total
    inverse_ref[...] = jnp.broadcast_to(inverse, inverse_ref.shape)
    step_ref[...] = jnp.broadcast_to(1.0 / step, step_ref.shape)


def proxy_kernel(count, base, *refs):
    pieces, rest = refs[:count], refs[count:]
    total_ref, inverse_ref, step_ref, sign_ref, matrix_ref, sent_ref = rest
    cuts = [slice(start, start + base) for start in range(0, total_ref.shape[1], base)]
    totals = [total_ref[:, cut] for cut in cuts]
    totals = add_levels(pieces, 0, inverse_ref[:, 0:1], sign_ref, matrix_ref, base, totals)
    steps = step_ref[:, 0:1]
    for cut, total in zip(cuts, totals):
        value = jnp.clip(jnp.round(total * steps), -32767.0, 32767.0)
        sent_ref[:, cut] = value.astype(jnp.int16)


def owner_kernel(near, base, *refs):
    pieces, rest = refs[:near], refs[near:]
    sums_ref, sign_ref, matrix_ref, total_ref, scale_ref, step_ref = rest
    owned, width = total_ref.shape
    half = lax.axis_index("dp") // near
    scale, step = scale_rows(sums_ref, half * owned, owned, width, near)
    inverse = (1.0 / math.sqrt(width)) / scale
    totals = add_levels(pieces, half, inverse, sign_ref, matrix_ref, base)
    for g, total in enumerate(totals):
        total_ref[:, g * base : (g + 1) * base] = total
    scale_ref[...] = jnp.broadcast_to(scale / (2 * near), scale_ref.shape)
    step_ref[...] = jnp.broadcast_to(step, step_ref.shape)


def finish_kernel(near_ref, far_ref, scale_ref, step_ref, total_ref, square_ref):
    width = near_ref.shape[1]
    step = step_ref[...]
    squares = None
    for start in range(0, width, lanes):
        cut = slice(start, start + lanes)
        total = near_ref[:, cut] + far_ref[:, cut].astype(jnp.float32) * step
        total_ref[:, cut] = total
        squares = total * total if squares is None else squares + total * total
    scale = scale_ref[...]
    squares = jnp.sum(squares * (scale * scale), axis=0, keepdims=True)
    square_ref[...] = jnp.broadcast_to(squares[None], square_ref.shape)


def back_kernel(base, total_ref, scale_ref, sign_ref, matrix_ref, unrot_ref):
    owned, width = total_ref.shape
    total = total_ref[...]
    high = total.astype(jnp.bfloat16)
    low = (total - high.astype(jnp.float32)).astype(jnp.bfloat16)
    groups = rotate_groups([high, low], matrix_ref[...], base)
    back = scale_ref[:, 0:1] * (1.0 / math.sqrt(width))
    signs = sign_ref[...].astype(jnp.float32)
    for g, group in enumerate(groups):
        cut = slice(g * base, (g + 1) * base)
        unrot_ref[:, cut] = group * back * signs[:, cut]


def clip_factor(limit, square_ref):
    squares = jnp.sum(jnp.sum(square_ref[...], axis=0, keepdims=True), axis=1, keepdims=True)
    return limit / jnp.maximum(jnp.sqrt(squares), limit)


def weights_kernel(limit, square_ref, unrot_ref, weight_ref, comp_ref, new_ref):
    update = unrot_ref[...] * clip_factor(limit, square_ref)
    summed = weight_ref[...].astype(jnp.float32) + (
        comp_ref[...].astype(jnp.float32) - learn_rate * update
    )
    new_ref[...] = summed.astype(jnp.bfloat16)


def update_kernel(limit, square_ref, unrot_ref, update_ref):
    update_ref[...] = unrot_ref[...] * clip_factor(limit, square_ref)


def chips_along_x(replicas):
    return 1 << ((replicas.bit_length() - 1) // 2)


def swap(value, mask):
    size = lax.axis_size("dp")
    return lax.ppermute(value, "dp", [(i, i ^ mask) for i in range(size)])


def place_kernel(places, owned, *refs):
    pieces, out_ref, sem = refs[: len(places)], refs[-2], refs[-1]
    me = lax.axis_index("dp")
    copies = []
    for i, ((mask, row), piece) in enumerate(zip(places, pieces)):
        start = pl.multiple_of((me ^ mask) * owned + row, 16)
        rows = pl.ds(start, piece.shape[0])
        copies.append(pltpu.make_async_copy(piece, out_ref.at[rows], sem.at[i]))
    for copy in copies:
        copy.start()
    for copy in copies:
        copy.wait()


def place_pieces(items, owned, replicas, out, name):
    places = [(mask, row) for mask, row, _ in items]
    values = [piece for _, _, piece in items]
    operands, aliases = list(values), {}
    specs = [pl.BlockSpec(memory_space=pltpu.VMEM)] * len(values)
    if out is not None:
        aliases = {len(operands): 0}
        operands.append(out)
        specs.append(pl.BlockSpec(memory_space=pl.ANY))
    width = values[0].shape[1]
    return pl.pallas_call(
        functools.partial(place_kernel, places, owned),
        in_specs=specs,
        out_specs=pl.BlockSpec(memory_space=pl.ANY),
        out_shape=jax.ShapeDtypeStruct((replicas * owned, width), values[0].dtype),
        scratch_shapes=[pltpu.SemaphoreType.DMA((len(values),))],
        input_output_aliases=aliases,
        compiler_params=pltpu.CompilerParams(vmem_limit_bytes=vmem_bytes),
        name=name,
    )(*operands)


def gather_blocks(block, replicas):
    x_count = chips_along_x(replicas)
    near = replicas // 2
    owned, width = block.shape
    far = swap(block, near)
    own = {0: block}
    for m in range(1, near):
        own[m] = swap(block, m) if m < x_count or m % x_count == 0 else None
    for m in range(1, near):
        if own[m] is None:
            own[m] = swap(own[m - m % x_count], m % x_count)
    own = [(m, 0, piece) for m, piece in own.items()]
    spread = [(near + m, 0, swap(far, m)) for m in range(1, near)]
    out = place_pieces(own + [(near, 0, far)], owned, replicas, None, "place_own")
    out = place_pieces(spread, owned, replicas, out, "place_far")
    return out.reshape(1, replicas * owned, width)


def on_device(grads, signs, weights, compensation):
    blocks, width = grads.shape[2:]
    replicas = lax.axis_size("dp")
    devices = replicas * lax.axis_size("expert")
    owned = blocks // replicas
    base = min(width, 256)
    matrix = jnp.asarray(hadamard(base), jnp.bfloat16)
    me = lax.axis_index("dp")
    near = replicas // 2
    params = pltpu.CompilerParams(vmem_limit_bytes=vmem_bytes)
    array = pl.BlockSpec(memory_space=pltpu.VMEM)

    def pair_of(source, index):
        source = source.reshape(2, near, owned, width)
        return lax.dynamic_slice_in_dim(source, index % near, 1, 1).reshape(2, owned, width)

    def block_of(source, index):
        source = source.reshape(replicas, owned, width)
        return lax.dynamic_slice_in_dim(source, index, 1, 0).reshape(owned, width)

    x_count = chips_along_x(replicas)
    aligned = [m for m in range(1, near) if m % x_count == 0 or m < x_count]
    diagonal = [m for m in range(1, near) if m not in aligned]
    pairs = [swap(pair_of(grads, me ^ mask), mask) for mask in aligned]
    sums = pl.pallas_call(
        sums_kernel,
        in_specs=[array],
        out_shape=jax.ShapeDtypeStruct((2, near, 1, 2 * owned), jnp.float32),
        compiler_params=params,
        name="sum_squares",
    )(grads.reshape(2, near, owned, width))
    later, sums = lax.optimization_barrier((grads, sums))
    sums = lax.all_to_all(
        sums.reshape(replicas, 1, 2 * owned), "dp", split_axis=0, concat_axis=0, tiled=True
    ).reshape(replicas, 2 * owned)
    far_pieces = [swap(block_of(later, me ^ mask ^ near), mask) for mask in diagonal]
    after, sums = lax.optimization_barrier((later, sums))
    near_pieces = [swap(block_of(after, me ^ mask), mask) for mask in diagonal]
    pairs.append(pair_of(later, me))
    whole = jax.ShapeDtypeStruct((owned, width), jnp.float32)
    column = jax.ShapeDtypeStruct((owned, lanes), jnp.float32)
    part, inverse, step = pl.pallas_call(
        functools.partial(proxy_pairs_kernel, near, len(pairs), base),
        in_specs=[array] * (len(pairs) + 3),
        out_shape=(whole, column, column),
        compiler_params=params,
        cost_estimate=pl.CostEstimate(
            flops=20000000000, bytes_accessed=4 * blocks * width, transcendentals=0
        ),
        name="proxy_pairs",
    )(*pairs, sums, signs, matrix)
    sent = pl.pallas_call(
        functools.partial(proxy_kernel, len(far_pieces), base),
        in_specs=[array] * (len(far_pieces) + 5),
        out_shape=jax.ShapeDtypeStruct((owned, width), jnp.int16),
        compiler_params=params,
        name="proxy_blocks",
    )(*far_pieces, part, inverse, step, signs, matrix)
    far_total = swap(sent, near)
    near_total, mean_scale, step = pl.pallas_call(
        functools.partial(owner_kernel, near, base),
        in_specs=[array] * (near + 3),
        out_shape=(whole, column, column),
        compiler_params=params,
        name="owner_blocks",
    )(*pairs, *near_pieces, sums, signs, matrix)
    total, squares = pl.pallas_call(
        finish_kernel,
        in_specs=[array] * 4,
        out_shape=(
            jax.ShapeDtypeStruct((owned, width), jnp.float32),
            jax.ShapeDtypeStruct((devices, 1, lanes), jnp.float32),
        ),
        compiler_params=params,
        name="finish_blocks",
    )(near_total, far_total, mean_scale, step)
    unrot = pl.pallas_call(
        functools.partial(back_kernel, base),
        out_shape=jax.ShapeDtypeStruct((owned, width), jnp.float32),
        compiler_params=params,
        name="rotate_back",
    )(total, mean_scale, signs, matrix)
    squares = lax.all_to_all(squares, ("dp", "expert"), split_axis=0, concat_axis=0, tiled=True)
    limit = target_rms * math.sqrt(blocks * width * lax.axis_size("expert"))
    squares = squares.reshape(devices, lanes)
    new_weights = pl.pallas_call(
        functools.partial(weights_kernel, limit),
        out_shape=jax.ShapeDtypeStruct((owned, width), jnp.bfloat16),
        compiler_params=params,
        name="new_weights",
    )(squares, unrot, weights.reshape(owned, width), compensation.reshape(owned, width))
    update_grad = pl.pallas_call(
        functools.partial(update_kernel, limit),
        out_shape=jax.ShapeDtypeStruct((owned, width), jnp.float32),
        compiler_params=params,
        name="update_grad",
    )(squares, unrot)
    return gather_blocks(new_weights, replicas), update_grad.reshape(weights.shape)


def solution(mesh):
    in_specs = (
        P("dp", "expert", None, None),
        P("expert", None),
        P("expert", "dp", None),
        P("expert", "dp", None),
    )
    out_specs = (P("expert", None, None), P("expert", "dp", None))
    return jax.shard_map(
        on_device, mesh=mesh, in_specs=in_specs, out_specs=out_specs, check_vma=False
    )
```

```python
import functools
import math

import jax
import jax.numpy as jnp
import numpy as np
from jax import lax
from jax.experimental import pallas as pl
from jax.experimental.pallas import tpu as pltpu
from jax.sharding import PartitionSpec as P

clamp_level = 2.0
target_rms = 0.2
learn_rate = 0.02
lanes = 128
vmem_bytes = 40 * 1024 * 1024


def hadamard(width):
    matrix = np.ones((1, 1), np.float32)
    while matrix.shape[0] < width:
        matrix = np.block([[matrix, matrix], [matrix, -matrix]])
    return matrix


def butterfly(groups):
    half = 1
    groups = list(groups)
    while half < len(groups):
        for start in range(0, len(groups), 2 * half):
            for i in range(start, start + half):
                upper, lower = groups[i], groups[i + half]
                groups[i], groups[i + half] = upper + lower, upper - lower
        half *= 2
    return groups


def rotate_groups(pieces, matrix, base):
    count = pieces[0].shape[1] // base
    groups = []
    for g in range(count):
        part = None
        for piece in pieces:
            term = jnp.dot(
                piece[:, g * base : (g + 1) * base], matrix, preferred_element_type=jnp.float32
            )
            part = term if part is None else part + term
        groups.append(part)
    return butterfly(groups)


def sums_kernel(x_ref, sums_ref):
    near, owned, width = x_ref.shape[1:]
    shape = (2 * owned, 2 * owned)
    row, lane = (lax.broadcasted_iota(jnp.int32, shape, axis) for axis in (0, 1))
    for j in range(near):
        rows = x_ref[:, j].reshape(2 * owned, width).astype(jnp.float32)
        squares = jnp.sum(rows * rows, axis=1, keepdims=True)
        line = jnp.sum(jnp.where(row == lane, squares, 0.0), axis=0, keepdims=True)
        sums_ref[0, j] = line
        sums_ref[1, j] = line


def scale_rows(sums_ref, offset, owned, width, near):
    biggest = jnp.max(sums_ref[...], axis=0, keepdims=True)
    shape = (owned, 2 * owned)
    row, lane = (lax.broadcasted_iota(jnp.int32, shape, axis) for axis in (0, 1))
    biggest = jnp.sum(jnp.where(lane == row + offset, biggest, 0.0), axis=1, keepdims=True)
    mean = biggest * (1.0 / width)
    scale = jnp.sqrt(mean + 1e-06)
    peak = jnp.sqrt(mean * width) / scale
    step = near * jnp.where(
        peak >= clamp_level, clamp_level / 32768.0, jnp.maximum(peak, 1e-20) / 32767.0
    )
    return scale, step


def add_levels(pieces, half, inverse, sign_ref, matrix_ref, base, totals=None):
    signs = sign_ref[...].astype(jnp.float32).astype(jnp.bfloat16)
    matrix = matrix_ref[...]
    for piece in pieces:
        rows = piece[...] if len(piece.shape) == 2 else piece[half]
        groups = rotate_groups([rows * signs], matrix, base)
        levels = [
            jnp.clip(group * inverse, -clamp_level, clamp_level)
            .astype(jnp.bfloat16)
            .astype(jnp.float32)
            for group in groups
        ]
        totals = levels if totals is None else [t + v for t, v in zip(totals, levels)]
    return totals


def proxy_pairs_kernel(near, count, base, *refs):
    pieces, rest = refs[:count], refs[count:]
    sums_ref, sign_ref, matrix_ref, total_ref, inverse_ref, step_ref = rest
    owned, width = total_ref.shape
    half = 1 - lax.axis_index("dp") // near
    scale, step = scale_rows(sums_ref, half * owned, owned, width, near)
    inverse = (1.0 / math.sqrt(width)) / scale
    totals = add_levels(pieces, half, inverse, sign_ref, matrix_ref, base)
    for g, total in enumerate(totals):
        total_ref[:, g * base : (g + 1) * base] = total
    inverse_ref[...] = jnp.broadcast_to(inverse, inverse_ref.shape)
    step_ref[...] = jnp.broadcast_to(1.0 / step, step_ref.shape)


def proxy_kernel(count, base, *refs):
    pieces, rest = refs[:count], refs[count:]
    total_ref, inverse_ref, step_ref, sign_ref, matrix_ref, sent_ref = rest
    cuts = [slice(start, start + base) for start in range(0, total_ref.shape[1], base)]
    totals = [total_ref[:, cut] for cut in cuts]
    totals = add_levels(pieces, 0, inverse_ref[:, 0:1], sign_ref, matrix_ref, base, totals)
    steps = step_ref[:, 0:1]
    for cut, total in zip(cuts, totals):
        value = jnp.clip(jnp.round(total * steps), -32767.0, 32767.0)
        sent_ref[:, cut] = value.astype(jnp.int16)


def owner_kernel(near, base, *refs):
    pieces, rest = refs[:near], refs[near:]
    sums_ref, sign_ref, matrix_ref, total_ref, scale_ref, step_ref = rest
    owned, width = total_ref.shape
    half = lax.axis_index("dp") // near
    scale, step = scale_rows(sums_ref, half * owned, owned, width, near)
    inverse = (1.0 / math.sqrt(width)) / scale
    totals = add_levels(pieces, half, inverse, sign_ref, matrix_ref, base)
    for g, total in enumerate(totals):
        total_ref[:, g * base : (g + 1) * base] = total
    scale_ref[...] = jnp.broadcast_to(scale / (2 * near), scale_ref.shape)
    step_ref[...] = jnp.broadcast_to(step, step_ref.shape)


def finish_kernel(near_ref, far_ref, scale_ref, step_ref, total_ref, square_ref):
    width = near_ref.shape[1]
    step = step_ref[...]
    squares = None
    for start in range(0, width, lanes):
        cut = slice(start, start + lanes)
        total = near_ref[:, cut] + far_ref[:, cut].astype(jnp.float32) * step
        total_ref[:, cut] = total
        squares = total * total if squares is None else squares + total * total
    scale = scale_ref[...]
    squares = jnp.sum(squares * (scale * scale), axis=0, keepdims=True)
    square_ref[...] = jnp.broadcast_to(squares[None], square_ref.shape)


def back_kernel(base, total_ref, scale_ref, sign_ref, matrix_ref, unrot_ref):
    owned, width = total_ref.shape
    total = total_ref[...]
    high = total.astype(jnp.bfloat16)
    low = (total - high.astype(jnp.float32)).astype(jnp.bfloat16)
    groups = rotate_groups([high, low], matrix_ref[...], base)
    back = scale_ref[:, 0:1] * (1.0 / math.sqrt(width))
    signs = sign_ref[...].astype(jnp.float32)
    for g, group in enumerate(groups):
        cut = slice(g * base, (g + 1) * base)
        unrot_ref[:, cut] = group * back * signs[:, cut]


def clip_factor(limit, square_ref):
    squares = jnp.sum(jnp.sum(square_ref[...], axis=0, keepdims=True), axis=1, keepdims=True)
    return limit / jnp.maximum(jnp.sqrt(squares), limit)


def weights_kernel(limit, square_ref, unrot_ref, weight_ref, comp_ref, new_ref):
    update = unrot_ref[...] * clip_factor(limit, square_ref)
    summed = weight_ref[...].astype(jnp.float32) + (
        comp_ref[...].astype(jnp.float32) - learn_rate * update
    )
    new_ref[...] = summed.astype(jnp.bfloat16)


def update_kernel(limit, square_ref, unrot_ref, update_ref):
    update_ref[...] = unrot_ref[...] * clip_factor(limit, square_ref)


def chips_along_x(replicas):
    return 1 << ((replicas.bit_length() - 1) // 2)


def swap(value, mask):
    size = lax.axis_size("dp")
    return lax.ppermute(value, "dp", [(i, i ^ mask) for i in range(size)])


def place_kernel(places, owned, *refs):
    pieces, out_ref, sem = refs[: len(places)], refs[-2], refs[-1]
    me = lax.axis_index("dp")
    copies = []
    for i, ((mask, row), piece) in enumerate(zip(places, pieces)):
        start = pl.multiple_of((me ^ mask) * owned + row, 16)
        rows = pl.ds(start, piece.shape[0])
        copies.append(pltpu.make_async_copy(piece, out_ref.at[rows], sem.at[i]))
    for copy in copies:
        copy.start()
    for copy in copies:
        copy.wait()


def place_pieces(items, owned, replicas, out, name):
    places = [(mask, row) for mask, row, _ in items]
    values = [piece for _, _, piece in items]
    operands, aliases = list(values), {}
    specs = [pl.BlockSpec(memory_space=pltpu.VMEM)] * len(values)
    if out is not None:
        aliases = {len(operands): 0}
        operands.append(out)
        specs.append(pl.BlockSpec(memory_space=pl.ANY))
    width = values[0].shape[1]
    return pl.pallas_call(
        functools.partial(place_kernel, places, owned),
        in_specs=specs,
        out_specs=pl.BlockSpec(memory_space=pl.ANY),
        out_shape=jax.ShapeDtypeStruct((replicas * owned, width), values[0].dtype),
        scratch_shapes=[pltpu.SemaphoreType.DMA((len(values),))],
        input_output_aliases=aliases,
        compiler_params=pltpu.CompilerParams(vmem_limit_bytes=vmem_bytes),
        name=name,
    )(*operands)


def gather_blocks(block, replicas):
    x_count = chips_along_x(replicas)
    near = replicas // 2
    owned, width = block.shape
    far = swap(block, near)
    own = {0: block}
    for m in range(1, near):
        own[m] = swap(block, m) if m < x_count or m % x_count == 0 else None
    for m in range(1, near):
        if own[m] is None:
            own[m] = swap(own[m - m % x_count], m % x_count)
    own = [(m, 0, piece) for m, piece in own.items()]
    spread = [(near + m, 0, swap(far, m)) for m in range(1, near)]
    out = place_pieces(own + [(near, 0, far)], owned, replicas, None, "place_own")
    out = place_pieces(spread, owned, replicas, out, "place_far")
    return out.reshape(1, replicas * owned, width)


def on_device(grads, signs, weights, compensation):
    blocks, width = grads.shape[2:]
    replicas = lax.axis_size("dp")
    devices = replicas * lax.axis_size("expert")
    owned = blocks // replicas
    base = min(width, 256)
    matrix = jnp.asarray(hadamard(base), jnp.bfloat16)
    me = lax.axis_index("dp")
    near = replicas // 2
    params = pltpu.CompilerParams(vmem_limit_bytes=vmem_bytes)
    array = pl.BlockSpec(memory_space=pltpu.VMEM)

    def pair_of(source, index):
        source = source.reshape(2, near, owned, width)
        return lax.dynamic_slice_in_dim(source, index % near, 1, 1).reshape(2, owned, width)

    def block_of(source, index):
        source = source.reshape(replicas, owned, width)
        return lax.dynamic_slice_in_dim(source, index, 1, 0).reshape(owned, width)

    x_count = chips_along_x(replicas)
    aligned = [m for m in range(1, near) if m % x_count == 0 or m < x_count]
    diagonal = [m for m in range(1, near) if m not in aligned]
    pairs = [swap(pair_of(grads, me ^ mask), mask) for mask in aligned]
    sums = pl.pallas_call(
        sums_kernel,
        in_specs=[array],
        out_shape=jax.ShapeDtypeStruct((2, near, 1, 2 * owned), jnp.float32),
        compiler_params=params,
        name="sum_squares",
    )(grads.reshape(2, near, owned, width))
    later, sums = lax.optimization_barrier((grads, sums))
    sums = lax.all_to_all(
        sums.reshape(replicas, 1, 2 * owned), "dp", split_axis=0, concat_axis=0, tiled=True
    ).reshape(replicas, 2 * owned)
    far_pieces = [swap(block_of(later, me ^ mask ^ near), mask) for mask in diagonal]
    after, sums = lax.optimization_barrier((later, sums))
    near_pieces = [swap(block_of(after, me ^ mask), mask) for mask in diagonal]
    pairs.append(pair_of(later, me))
    whole = jax.ShapeDtypeStruct((owned, width), jnp.float32)
    column = jax.ShapeDtypeStruct((owned, lanes), jnp.float32)
    part, inverse, step = pl.pallas_call(
        functools.partial(proxy_pairs_kernel, near, len(pairs), base),
        in_specs=[array] * (len(pairs) + 3),
        out_shape=(whole, column, column),
        compiler_params=params,
        name="proxy_pairs",
    )(*pairs, sums, signs, matrix)
    sent = pl.pallas_call(
        functools.partial(proxy_kernel, len(far_pieces), base),
        in_specs=[array] * (len(far_pieces) + 5),
        out_shape=jax.ShapeDtypeStruct((owned, width), jnp.int16),
        compiler_params=params,
        name="proxy_blocks",
    )(*far_pieces, part, inverse, step, signs, matrix)
    far_total = swap(sent, near)
    near_total, mean_scale, step = pl.pallas_call(
        functools.partial(owner_kernel, near, base),
        in_specs=[array] * (near + 3),
        out_shape=(whole, column, column),
        compiler_params=params,
        name="owner_blocks",
    )(*pairs, *near_pieces, sums, signs, matrix)
    total, squares = pl.pallas_call(
        finish_kernel,
        in_specs=[array] * 4,
        out_shape=(
            jax.ShapeDtypeStruct((owned, width), jnp.float32),
            jax.ShapeDtypeStruct((devices, 1, lanes), jnp.float32),
        ),
        compiler_params=params,
        name="finish_blocks",
    )(near_total, far_total, mean_scale, step)
    unrot = pl.pallas_call(
        functools.partial(back_kernel, base),
        out_shape=jax.ShapeDtypeStruct((owned, width), jnp.float32),
        compiler_params=params,
        name="rotate_back",
    )(total, mean_scale, signs, matrix)
    squares = lax.all_to_all(squares, ("dp", "expert"), split_axis=0, concat_axis=0, tiled=True)
    limit = target_rms * math.sqrt(blocks * width * lax.axis_size("expert"))
    squares = squares.reshape(devices, lanes)
    new_weights = pl.pallas_call(
        functools.partial(weights_kernel, limit),
        out_shape=jax.ShapeDtypeStruct((owned, width), jnp.bfloat16),
        compiler_params=params,
        name="new_weights",
    )(squares, unrot, weights.reshape(owned, width), compensation.reshape(owned, width))
    update_grad = pl.pallas_call(
        functools.partial(update_kernel, limit),
        out_shape=jax.ShapeDtypeStruct((owned, width), jnp.float32),
        compiler_params=params,
        name="update_grad",
    )(squares, unrot)
    return gather_blocks(new_weights, replicas), update_grad.reshape(weights.shape)


def solution(mesh):
    in_specs = (
        P("dp", "expert", None, None),
        P("expert", None),
        P("expert", "dp", None),
        P("expert", "dp", None),
    )
    out_specs = (P("expert", None, None), P("expert", "dp", None))
    return jax.shard_map(
        on_device, mesh=mesh, in_specs=in_specs, out_specs=out_specs, check_vma=False
    )
```

```python
import functools
import math

import jax
import jax.numpy as jnp
import numpy as np
from jax import lax
from jax.experimental import pallas as pl
from jax.experimental.pallas import tpu as pltpu
from jax.sharding import PartitionSpec as P

clamp_level = 2.0
target_rms = 0.2
learn_rate = 0.02
lanes = 128
vmem_bytes = 40 * 1024 * 1024


def hadamard(width):
    matrix = np.ones((1, 1), np.float32)
    while matrix.shape[0] < width:
        matrix = np.block([[matrix, matrix], [matrix, -matrix]])
    return matrix


def butterfly(groups):
    half = 1
    groups = list(groups)
    while half < len(groups):
        for start in range(0, len(groups), 2 * half):
            for i in range(start, start + half):
                upper, lower = groups[i], groups[i + half]
                groups[i], groups[i + half] = upper + lower, upper - lower
        half *= 2
    return groups


def rotate_groups(pieces, matrix, base):
    count = pieces[0].shape[1] // base
    groups = []
    for g in range(count):
        part = None
        for piece in pieces:
            term = jnp.dot(
                piece[:, g * base : (g + 1) * base], matrix, preferred_element_type=jnp.float32
            )
            part = term if part is None else part + term
        groups.append(part)
    return butterfly(groups)


def sums_kernel(x_ref, sums_ref):
    near, owned, width = x_ref.shape[1:]
    shape = (2 * owned, 2 * owned)
    row, lane = (lax.broadcasted_iota(jnp.int32, shape, axis) for axis in (0, 1))
    for j in range(near):
        rows = x_ref[:, j].reshape(2 * owned, width).astype(jnp.float32)
        squares = jnp.sum(rows * rows, axis=1, keepdims=True)
        line = jnp.sum(jnp.where(row == lane, squares, 0.0), axis=0, keepdims=True)
        sums_ref[0, j] = line
        sums_ref[1, j] = line


def scale_rows(sums_ref, offset, owned, width, near):
    biggest = jnp.max(sums_ref[...], axis=0, keepdims=True)
    shape = (owned, 2 * owned)
    row, lane = (lax.broadcasted_iota(jnp.int32, shape, axis) for axis in (0, 1))
    biggest = jnp.sum(jnp.where(lane == row + offset, biggest, 0.0), axis=1, keepdims=True)
    mean = biggest * (1.0 / width)
    scale = jnp.sqrt(mean + 1e-06)
    peak = jnp.sqrt(mean * width) / scale
    step = near * jnp.where(
        peak >= clamp_level, clamp_level / 32768.0, jnp.maximum(peak, 1e-20) / 32767.0
    )
    return scale, step


def add_levels(pieces, half, inverse, sign_ref, matrix_ref, base, totals=None):
    signs = sign_ref[...].astype(jnp.float32).astype(jnp.bfloat16)
    matrix = matrix_ref[...]
    for piece in pieces:
        rows = piece[...] if len(piece.shape) == 2 else piece[half]
        groups = rotate_groups([rows * signs], matrix, base)
        levels = [
            jnp.clip(group * inverse, -clamp_level, clamp_level)
            .astype(jnp.bfloat16)
            .astype(jnp.float32)
            for group in groups
        ]
        totals = levels if totals is None else [t + v for t, v in zip(totals, levels)]
    return totals


def proxy_pairs_kernel(near, count, base, *refs):
    pieces, rest = refs[:count], refs[count:]
    sums_ref, sign_ref, matrix_ref, total_ref, inverse_ref, step_ref = rest
    owned, width = total_ref.shape
    half = 1 - lax.axis_index("dp") // near
    scale, step = scale_rows(sums_ref, half * owned, owned, width, near)
    inverse = (1.0 / math.sqrt(width)) / scale
    totals = add_levels(pieces, half, inverse, sign_ref, matrix_ref, base)
    for g, total in enumerate(totals):
        total_ref[:, g * base : (g + 1) * base] = total
    inverse_ref[...] = jnp.broadcast_to(inverse, inverse_ref.shape)
    step_ref[...] = jnp.broadcast_to(1.0 / step, step_ref.shape)


def proxy_kernel(count, base, *refs):
    pieces, rest = refs[:count], refs[count:]
    total_ref, inverse_ref, step_ref, sign_ref, matrix_ref, sent_ref = rest
    cuts = [slice(start, start + base) for start in range(0, total_ref.shape[1], base)]
    totals = [total_ref[:, cut] for cut in cuts]
    totals = add_levels(pieces, 0, inverse_ref[:, 0:1], sign_ref, matrix_ref, base, totals)
    steps = step_ref[:, 0:1]
    for cut, total in zip(cuts, totals):
        value = jnp.clip(jnp.round(total * steps), -32767.0, 32767.0)
        sent_ref[:, cut] = value.astype(jnp.int16)


def owner_kernel(near, base, *refs):
    pieces, rest = refs[:near], refs[near:]
    sums_ref, sign_ref, matrix_ref, total_ref, scale_ref, step_ref = rest
    owned, width = total_ref.shape
    half = lax.axis_index("dp") // near
    scale, step = scale_rows(sums_ref, half * owned, owned, width, near)
    inverse = (1.0 / math.sqrt(width)) / scale
    totals = add_levels(pieces, half, inverse, sign_ref, matrix_ref, base)
    for g, total in enumerate(totals):
        total_ref[:, g * base : (g + 1) * base] = total
    scale_ref[...] = jnp.broadcast_to(scale / (2 * near), scale_ref.shape)
    step_ref[...] = jnp.broadcast_to(step, step_ref.shape)


def finish_kernel(near_ref, far_ref, scale_ref, step_ref, total_ref, square_ref):
    width = near_ref.shape[1]
    step = step_ref[...]
    squares = None
    for start in range(0, width, lanes):
        cut = slice(start, start + lanes)
        total = near_ref[:, cut] + far_ref[:, cut].astype(jnp.float32) * step
        total_ref[:, cut] = total
        squares = total * total if squares is None else squares + total * total
    scale = scale_ref[...]
    squares = jnp.sum(squares * (scale * scale), axis=0, keepdims=True)
    square_ref[...] = jnp.broadcast_to(squares[None], square_ref.shape)


def back_kernel(base, total_ref, scale_ref, sign_ref, matrix_ref, unrot_ref):
    owned, width = total_ref.shape
    total = total_ref[...]
    high = total.astype(jnp.bfloat16)
    low = (total - high.astype(jnp.float32)).astype(jnp.bfloat16)
    groups = rotate_groups([high, low], matrix_ref[...], base)
    back = scale_ref[:, 0:1] * (1.0 / math.sqrt(width))
    signs = sign_ref[...].astype(jnp.float32)
    for g, group in enumerate(groups):
        cut = slice(g * base, (g + 1) * base)
        unrot_ref[:, cut] = group * back * signs[:, cut]


def clip_factor(limit, square_ref):
    squares = jnp.sum(jnp.sum(square_ref[...], axis=0, keepdims=True), axis=1, keepdims=True)
    return limit / jnp.maximum(jnp.sqrt(squares), limit)


def weights_kernel(limit, square_ref, unrot_ref, weight_ref, comp_ref, new_ref):
    update = unrot_ref[...] * clip_factor(limit, square_ref)
    summed = weight_ref[...].astype(jnp.float32) + (
        comp_ref[...].astype(jnp.float32) - learn_rate * update
    )
    new_ref[...] = summed.astype(jnp.bfloat16)


def update_kernel(limit, square_ref, unrot_ref, update_ref):
    update_ref[...] = unrot_ref[...] * clip_factor(limit, square_ref)


def chips_along_x(replicas):
    return 1 << ((replicas.bit_length() - 1) // 2)


def swap(value, mask):
    size = lax.axis_size("dp")
    return lax.ppermute(value, "dp", [(i, i ^ mask) for i in range(size)])


def place_kernel(places, owned, *refs):
    pieces, out_ref, sem = refs[: len(places)], refs[-2], refs[-1]
    me = lax.axis_index("dp")
    copies = []
    for i, ((mask, row), piece) in enumerate(zip(places, pieces)):
        start = pl.multiple_of((me ^ mask) * owned + row, 16)
        rows = pl.ds(start, piece.shape[0])
        copies.append(pltpu.make_async_copy(piece, out_ref.at[rows], sem.at[i]))
    for copy in copies:
        copy.start()
    for copy in copies:
        copy.wait()


def place_pieces(items, owned, replicas, out, name):
    places = [(mask, row) for mask, row, _ in items]
    values = [piece for _, _, piece in items]
    operands, aliases = list(values), {}
    specs = [pl.BlockSpec(memory_space=pltpu.VMEM)] * len(values)
    if out is not None:
        aliases = {len(operands): 0}
        operands.append(out)
        specs.append(pl.BlockSpec(memory_space=pl.ANY))
    width = values[0].shape[1]
    return pl.pallas_call(
        functools.partial(place_kernel, places, owned),
        in_specs=specs,
        out_specs=pl.BlockSpec(memory_space=pl.ANY),
        out_shape=jax.ShapeDtypeStruct((replicas * owned, width), values[0].dtype),
        scratch_shapes=[pltpu.SemaphoreType.DMA((len(values),))],
        input_output_aliases=aliases,
        compiler_params=pltpu.CompilerParams(vmem_limit_bytes=vmem_bytes),
        name=name,
    )(*operands)


def gather_blocks(block, replicas):
    x_count = chips_along_x(replicas)
    near = replicas // 2
    owned, width = block.shape
    far = swap(block, near)
    own = {0: block}
    for m in range(1, near):
        own[m] = swap(block, m) if m < x_count or m % x_count == 0 else None
    for m in range(1, near):
        if own[m] is None:
            own[m] = swap(own[m - m % x_count], m % x_count)
    own = [(m, 0, piece) for m, piece in own.items()]
    spread = [(near + m, 0, swap(far, m)) for m in range(1, near)]
    out = place_pieces(own + [(near, 0, far)], owned, replicas, None, "place_own")
    out = place_pieces(spread[1:], owned, replicas, out, "place_far")
    out = place_pieces(spread[:1], owned, replicas, out, "place_last")
    return out.reshape(1, replicas * owned, width)


def on_device(grads, signs, weights, compensation):
    blocks, width = grads.shape[2:]
    replicas = lax.axis_size("dp")
    devices = replicas * lax.axis_size("expert")
    owned = blocks // replicas
    base = min(width, 256)
    matrix = jnp.asarray(hadamard(base), jnp.bfloat16)
    me = lax.axis_index("dp")
    near = replicas // 2
    params = pltpu.CompilerParams(vmem_limit_bytes=vmem_bytes)
    array = pl.BlockSpec(memory_space=pltpu.VMEM)

    def pair_of(source, index):
        source = source.reshape(2, near, owned, width)
        return lax.dynamic_slice_in_dim(source, index % near, 1, 1).reshape(2, owned, width)

    def block_of(source, index):
        source = source.reshape(replicas, owned, width)
        return lax.dynamic_slice_in_dim(source, index, 1, 0).reshape(owned, width)

    x_count = chips_along_x(replicas)
    aligned = [m for m in range(1, near) if m % x_count == 0 or m < x_count]
    diagonal = [m for m in range(1, near) if m not in aligned]
    pairs = [swap(pair_of(grads, me ^ mask), mask) for mask in aligned]
    sums = pl.pallas_call(
        sums_kernel,
        in_specs=[array],
        out_shape=jax.ShapeDtypeStruct((2, near, 1, 2 * owned), jnp.float32),
        compiler_params=params,
        name="sum_squares",
    )(grads.reshape(2, near, owned, width))
    later, sums = lax.optimization_barrier((grads, sums))
    sums = lax.all_to_all(
        sums.reshape(replicas, 1, 2 * owned), "dp", split_axis=0, concat_axis=0, tiled=True
    ).reshape(replicas, 2 * owned)
    far_pieces = [swap(block_of(later, me ^ mask ^ near), mask) for mask in diagonal]
    near_pieces = [swap(block_of(later, me ^ mask), mask) for mask in diagonal]
    pairs.append(pair_of(later, me))
    whole = jax.ShapeDtypeStruct((owned, width), jnp.float32)
    column = jax.ShapeDtypeStruct((owned, lanes), jnp.float32)
    part, inverse, step = pl.pallas_call(
        functools.partial(proxy_pairs_kernel, near, len(pairs), base),
        in_specs=[array] * (len(pairs) + 3),
        out_shape=(whole, column, column),
        compiler_params=params,
        name="proxy_pairs",
    )(*pairs, sums, signs, matrix)
    sent = pl.pallas_call(
        functools.partial(proxy_kernel, len(far_pieces), base),
        in_specs=[array] * (len(far_pieces) + 5),
        out_shape=jax.ShapeDtypeStruct((owned, width), jnp.int16),
        compiler_params=params,
        name="proxy_blocks",
    )(*far_pieces, part, inverse, step, signs, matrix)
    far_total = swap(sent, near)
    near_total, mean_scale, step = pl.pallas_call(
        functools.partial(owner_kernel, near, base),
        in_specs=[array] * (near + 3),
        out_shape=(whole, column, column),
        compiler_params=params,
        name="owner_blocks",
    )(*pairs, *near_pieces, sums, signs, matrix)
    total, squares = pl.pallas_call(
        finish_kernel,
        in_specs=[array] * 4,
        out_shape=(
            jax.ShapeDtypeStruct((owned, width), jnp.float32),
            jax.ShapeDtypeStruct((devices, 1, lanes), jnp.float32),
        ),
        compiler_params=params,
        name="finish_blocks",
    )(near_total, far_total, mean_scale, step)
    unrot = pl.pallas_call(
        functools.partial(back_kernel, base),
        out_shape=jax.ShapeDtypeStruct((owned, width), jnp.float32),
        compiler_params=params,
        name="rotate_back",
    )(total, mean_scale, signs, matrix)
    squares = lax.all_to_all(squares, ("dp", "expert"), split_axis=0, concat_axis=0, tiled=True)
    limit = target_rms * math.sqrt(blocks * width * lax.axis_size("expert"))
    squares = squares.reshape(devices, lanes)
    new_weights = pl.pallas_call(
        functools.partial(weights_kernel, limit),
        out_shape=jax.ShapeDtypeStruct((owned, width), jnp.bfloat16),
        compiler_params=params,
        name="new_weights",
    )(squares, unrot, weights.reshape(owned, width), compensation.reshape(owned, width))
    update_grad = pl.pallas_call(
        functools.partial(update_kernel, limit),
        out_shape=jax.ShapeDtypeStruct((owned, width), jnp.float32),
        compiler_params=params,
        name="update_grad",
    )(squares, unrot)
    return gather_blocks(new_weights, replicas), update_grad.reshape(weights.shape)


def solution(mesh):
    in_specs = (
        P("dp", "expert", None, None),
        P("expert", None),
        P("expert", "dp", None),
        P("expert", "dp", None),
    )
    out_specs = (P("expert", None, None), P("expert", "dp", None))
    return jax.shard_map(
        on_device, mesh=mesh, in_specs=in_specs, out_specs=out_specs, check_vma=False
    )
```

```python
import functools
import math

import jax
import jax.numpy as jnp
import numpy as np
from jax import lax
from jax.experimental import pallas as pl
from jax.experimental.pallas import tpu as pltpu
from jax.sharding import PartitionSpec as P

clamp_level = 2.0
target_rms = 0.2
learn_rate = 0.02
lanes = 128
vmem_bytes = 40 * 1024 * 1024


def hadamard(width):
    matrix = np.ones((1, 1), np.float32)
    while matrix.shape[0] < width:
        matrix = np.block([[matrix, matrix], [matrix, -matrix]])
    return matrix


def butterfly(groups):
    half = 1
    groups = list(groups)
    while half < len(groups):
        for start in range(0, len(groups), 2 * half):
            for i in range(start, start + half):
                upper, lower = groups[i], groups[i + half]
                groups[i], groups[i + half] = upper + lower, upper - lower
        half *= 2
    return groups


def rotate_groups(pieces, matrix, base):
    count = pieces[0].shape[1] // base
    groups = []
    for g in range(count):
        part = None
        for piece in pieces:
            term = jnp.dot(
                piece[:, g * base : (g + 1) * base], matrix, preferred_element_type=jnp.float32
            )
            part = term if part is None else part + term
        groups.append(part)
    return butterfly(groups)


def sums_kernel(x_ref, sums_ref):
    near, owned, width = x_ref.shape[1:]
    shape = (2 * owned, 2 * owned)
    row, lane = (lax.broadcasted_iota(jnp.int32, shape, axis) for axis in (0, 1))
    for j in range(near):
        rows = x_ref[:, j].reshape(2 * owned, width)
        products = lax.dot_general(
            rows, rows, (((1,), (1,)), ((), ())), preferred_element_type=jnp.float32
        )
        line = jnp.sum(jnp.where(row == lane, products, 0.0), axis=0, keepdims=True)
        sums_ref[0, j] = line
        sums_ref[1, j] = line


def scale_rows(sums_ref, offset, owned, width, near):
    biggest = jnp.max(sums_ref[...], axis=0, keepdims=True)
    shape = (owned, 2 * owned)
    row, lane = (lax.broadcasted_iota(jnp.int32, shape, axis) for axis in (0, 1))
    biggest = jnp.sum(jnp.where(lane == row + offset, biggest, 0.0), axis=1, keepdims=True)
    mean = biggest * (1.0 / width)
    scale = jnp.sqrt(mean + 1e-06)
    peak = jnp.sqrt(mean * width) / scale
    step = near * jnp.where(
        peak >= clamp_level, clamp_level / 32768.0, jnp.maximum(peak, 1e-20) / 32767.0
    )
    return scale, step


def add_levels(pieces, half, inverse, sign_ref, matrix_ref, base, totals=None):
    signs = sign_ref[...].astype(jnp.float32).astype(jnp.bfloat16)
    matrix = matrix_ref[...]
    for piece in pieces:
        rows = piece[...] if len(piece.shape) == 2 else piece[half]
        groups = rotate_groups([rows * signs], matrix, base)
        levels = [
            jnp.clip(group * inverse, -clamp_level, clamp_level)
            .astype(jnp.bfloat16)
            .astype(jnp.float32)
            for group in groups
        ]
        totals = levels if totals is None else [t + v for t, v in zip(totals, levels)]
    return totals


def proxy_pairs_kernel(near, count, base, *refs):
    pieces, rest = refs[:count], refs[count:]
    sums_ref, sign_ref, matrix_ref, total_ref, inverse_ref, step_ref = rest
    owned, width = total_ref.shape
    half = 1 - lax.axis_index("dp") // near
    scale, step = scale_rows(sums_ref, half * owned, owned, width, near)
    inverse = (1.0 / math.sqrt(width)) / scale
    totals = add_levels(pieces, half, inverse, sign_ref, matrix_ref, base)
    for g, total in enumerate(totals):
        total_ref[:, g * base : (g + 1) * base] = total
    inverse_ref[...] = jnp.broadcast_to(inverse, inverse_ref.shape)
    step_ref[...] = jnp.broadcast_to(1.0 / step, step_ref.shape)


def proxy_kernel(count, base, *refs):
    pieces, rest = refs[:count], refs[count:]
    total_ref, inverse_ref, step_ref, sign_ref, matrix_ref, sent_ref = rest
    cuts = [slice(start, start + base) for start in range(0, total_ref.shape[1], base)]
    totals = [total_ref[:, cut] for cut in cuts]
    totals = add_levels(pieces, 0, inverse_ref[:, 0:1], sign_ref, matrix_ref, base, totals)
    steps = step_ref[:, 0:1]
    for cut, total in zip(cuts, totals):
        value = jnp.clip(jnp.round(total * steps), -32767.0, 32767.0)
        sent_ref[:, cut] = value.astype(jnp.int16)


def owner_kernel(near, base, *refs):
    pieces, rest = refs[:near], refs[near:]
    sums_ref, sign_ref, matrix_ref, total_ref, scale_ref, step_ref = rest
    owned, width = total_ref.shape
    half = lax.axis_index("dp") // near
    scale, step = scale_rows(sums_ref, half * owned, owned, width, near)
    inverse = (1.0 / math.sqrt(width)) / scale
    totals = add_levels(pieces, half, inverse, sign_ref, matrix_ref, base)
    for g, total in enumerate(totals):
        total_ref[:, g * base : (g + 1) * base] = total
    scale_ref[...] = jnp.broadcast_to(scale / (2 * near), scale_ref.shape)
    step_ref[...] = jnp.broadcast_to(step, step_ref.shape)


def finish_kernel(near_ref, far_ref, scale_ref, step_ref, total_ref, square_ref):
    width = near_ref.shape[1]
    step = step_ref[...]
    squares = None
    for start in range(0, width, lanes):
        cut = slice(start, start + lanes)
        total = near_ref[:, cut] + far_ref[:, cut].astype(jnp.float32) * step
        total_ref[:, cut] = total
        squares = total * total if squares is None else squares + total * total
    scale = scale_ref[...]
    squares = jnp.sum(squares * (scale * scale), axis=0, keepdims=True)
    square_ref[...] = jnp.broadcast_to(squares[None], square_ref.shape)


def back_kernel(base, total_ref, scale_ref, sign_ref, matrix_ref, unrot_ref):
    owned, width = total_ref.shape
    total = total_ref[...]
    high = total.astype(jnp.bfloat16)
    low = (total - high.astype(jnp.float32)).astype(jnp.bfloat16)
    groups = rotate_groups([high, low], matrix_ref[...], base)
    back = scale_ref[:, 0:1] * (1.0 / math.sqrt(width))
    signs = sign_ref[...].astype(jnp.float32)
    for g, group in enumerate(groups):
        cut = slice(g * base, (g + 1) * base)
        unrot_ref[:, cut] = group * back * signs[:, cut]


def clip_factor(limit, square_ref):
    squares = jnp.sum(jnp.sum(square_ref[...], axis=0, keepdims=True), axis=1, keepdims=True)
    return limit / jnp.maximum(jnp.sqrt(squares), limit)


def weights_kernel(limit, square_ref, unrot_ref, weight_ref, comp_ref, new_ref):
    update = unrot_ref[...] * clip_factor(limit, square_ref)
    summed = weight_ref[...].astype(jnp.float32) + (
        comp_ref[...].astype(jnp.float32) - learn_rate * update
    )
    new_ref[...] = summed.astype(jnp.bfloat16)


def update_kernel(limit, square_ref, unrot_ref, update_ref):
    update_ref[...] = unrot_ref[...] * clip_factor(limit, square_ref)


def chips_along_x(replicas):
    return 1 << ((replicas.bit_length() - 1) // 2)


def swap(value, mask):
    size = lax.axis_size("dp")
    return lax.ppermute(value, "dp", [(i, i ^ mask) for i in range(size)])


def place_kernel(places, owned, *refs):
    pieces, out_ref, sem = refs[: len(places)], refs[-2], refs[-1]
    me = lax.axis_index("dp")
    copies = []
    for i, ((mask, row), piece) in enumerate(zip(places, pieces)):
        start = pl.multiple_of((me ^ mask) * owned + row, 16)
        rows = pl.ds(start, piece.shape[0])
        copies.append(pltpu.make_async_copy(piece, out_ref.at[rows], sem.at[i]))
    for copy in copies:
        copy.start()
    for copy in copies:
        copy.wait()


def place_pieces(items, owned, replicas, out, name):
    places = [(mask, row) for mask, row, _ in items]
    values = [piece for _, _, piece in items]
    operands, aliases = list(values), {}
    specs = [pl.BlockSpec(memory_space=pltpu.VMEM)] * len(values)
    if out is not None:
        aliases = {len(operands): 0}
        operands.append(out)
        specs.append(pl.BlockSpec(memory_space=pl.ANY))
    width = values[0].shape[1]
    return pl.pallas_call(
        functools.partial(place_kernel, places, owned),
        in_specs=specs,
        out_specs=pl.BlockSpec(memory_space=pl.ANY),
        out_shape=jax.ShapeDtypeStruct((replicas * owned, width), values[0].dtype),
        scratch_shapes=[pltpu.SemaphoreType.DMA((len(values),))],
        input_output_aliases=aliases,
        compiler_params=pltpu.CompilerParams(vmem_limit_bytes=vmem_bytes),
        name=name,
    )(*operands)


def gather_blocks(block, replicas):
    x_count = chips_along_x(replicas)
    near = replicas // 2
    owned, width = block.shape
    far = swap(block, near)
    own = {0: block}
    for m in range(1, near):
        own[m] = swap(block, m) if m < x_count or m % x_count == 0 else None
    for m in range(1, near):
        if own[m] is None:
            own[m] = swap(own[m - m % x_count], m % x_count)
    own = [(m, 0, piece) for m, piece in own.items()]
    spread = [(near + m, 0, swap(far, m)) for m in range(1, near)]
    out = place_pieces(own + [(near, 0, far)], owned, replicas, None, "place_own")
    out = place_pieces(spread, owned, replicas, out, "place_far")
    return out.reshape(1, replicas * owned, width)


def on_device(grads, signs, weights, compensation):
    blocks, width = grads.shape[2:]
    replicas = lax.axis_size("dp")
    devices = replicas * lax.axis_size("expert")
    owned = blocks // replicas
    base = min(width, 256)
    matrix = jnp.asarray(hadamard(base), jnp.bfloat16)
    me = lax.axis_index("dp")
    near = replicas // 2
    params = pltpu.CompilerParams(vmem_limit_bytes=vmem_bytes)
    array = pl.BlockSpec(memory_space=pltpu.VMEM)

    def pair_of(source, index):
        source = source.reshape(2, near, owned, width)
        return lax.dynamic_slice_in_dim(source, index % near, 1, 1).reshape(2, owned, width)

    def block_of(source, index):
        source = source.reshape(replicas, owned, width)
        return lax.dynamic_slice_in_dim(source, index, 1, 0).reshape(owned, width)

    x_count = chips_along_x(replicas)
    aligned = [m for m in range(1, near) if m % x_count == 0 or m < x_count]
    diagonal = [m for m in range(1, near) if m not in aligned]
    pairs = [swap(pair_of(grads, me ^ mask), mask) for mask in aligned]
    sums = pl.pallas_call(
        sums_kernel,
        in_specs=[array],
        out_shape=jax.ShapeDtypeStruct((2, near, 1, 2 * owned), jnp.float32),
        compiler_params=params,
        name="sum_squares",
    )(grads.reshape(2, near, owned, width))
    later, sums = lax.optimization_barrier((grads, sums))
    sums = lax.all_to_all(
        sums.reshape(replicas, 1, 2 * owned), "dp", split_axis=0, concat_axis=0, tiled=True
    ).reshape(replicas, 2 * owned)
    far_pieces = [swap(block_of(later, me ^ mask ^ near), mask) for mask in diagonal]
    near_pieces = [swap(block_of(later, me ^ mask), mask) for mask in diagonal]
    pairs.append(pair_of(later, me))
    whole = jax.ShapeDtypeStruct((owned, width), jnp.float32)
    column = jax.ShapeDtypeStruct((owned, lanes), jnp.float32)
    part, inverse, step = pl.pallas_call(
        functools.partial(proxy_pairs_kernel, near, len(pairs), base),
        in_specs=[array] * (len(pairs) + 3),
        out_shape=(whole, column, column),
        compiler_params=params,
        name="proxy_pairs",
    )(*pairs, sums, signs, matrix)
    sent = pl.pallas_call(
        functools.partial(proxy_kernel, len(far_pieces), base),
        in_specs=[array] * (len(far_pieces) + 5),
        out_shape=jax.ShapeDtypeStruct((owned, width), jnp.int16),
        compiler_params=params,
        name="proxy_blocks",
    )(*far_pieces, part, inverse, step, signs, matrix)
    far_total = swap(sent, near)
    near_total, mean_scale, step = pl.pallas_call(
        functools.partial(owner_kernel, near, base),
        in_specs=[array] * (near + 3),
        out_shape=(whole, column, column),
        compiler_params=params,
        name="owner_blocks",
    )(*pairs, *near_pieces, sums, signs, matrix)
    total, squares = pl.pallas_call(
        finish_kernel,
        in_specs=[array] * 4,
        out_shape=(
            jax.ShapeDtypeStruct((owned, width), jnp.float32),
            jax.ShapeDtypeStruct((devices, 1, lanes), jnp.float32),
        ),
        compiler_params=params,
        name="finish_blocks",
    )(near_total, far_total, mean_scale, step)
    unrot = pl.pallas_call(
        functools.partial(back_kernel, base),
        out_shape=jax.ShapeDtypeStruct((owned, width), jnp.float32),
        compiler_params=params,
        name="rotate_back",
    )(total, mean_scale, signs, matrix)
    squares = lax.all_to_all(squares, ("dp", "expert"), split_axis=0, concat_axis=0, tiled=True)
    limit = target_rms * math.sqrt(blocks * width * lax.axis_size("expert"))
    squares = squares.reshape(devices, lanes)
    new_weights = pl.pallas_call(
        functools.partial(weights_kernel, limit),
        out_shape=jax.ShapeDtypeStruct((owned, width), jnp.bfloat16),
        compiler_params=params,
        name="new_weights",
    )(squares, unrot, weights.reshape(owned, width), compensation.reshape(owned, width))
    update_grad = pl.pallas_call(
        functools.partial(update_kernel, limit),
        out_shape=jax.ShapeDtypeStruct((owned, width), jnp.float32),
        compiler_params=params,
        name="update_grad",
    )(squares, unrot)
    return gather_blocks(new_weights, replicas), update_grad.reshape(weights.shape)


def solution(mesh):
    in_specs = (
        P("dp", "expert", None, None),
        P("expert", None),
        P("expert", "dp", None),
        P("expert", "dp", None),
    )
    out_specs = (P("expert", None, None), P("expert", "dp", None))
    return jax.shard_map(
        on_device, mesh=mesh, in_specs=in_specs, out_specs=out_specs, check_vma=False
    )
```

```python
import functools
import math

import jax
import jax.numpy as jnp
import numpy as np
from jax import lax
from jax.experimental import pallas as pl
from jax.experimental.pallas import tpu as pltpu
from jax.sharding import PartitionSpec as P

clamp_level = 2.0
target_rms = 0.2
learn_rate = 0.02
lanes = 128
vmem_bytes = 40 * 1024 * 1024


def hadamard(width):
    matrix = np.ones((1, 1), np.float32)
    while matrix.shape[0] < width:
        matrix = np.block([[matrix, matrix], [matrix, -matrix]])
    return matrix


def butterfly(groups):
    half = 1
    groups = list(groups)
    while half < len(groups):
        for start in range(0, len(groups), 2 * half):
            for i in range(start, start + half):
                upper, lower = groups[i], groups[i + half]
                groups[i], groups[i + half] = upper + lower, upper - lower
        half *= 2
    return groups


def rotate_groups(pieces, matrix, base):
    count = pieces[0].shape[1] // base
    groups = []
    for g in range(count):
        part = None
        for piece in pieces:
            term = jnp.dot(
                piece[:, g * base : (g + 1) * base], matrix, preferred_element_type=jnp.float32
            )
            part = term if part is None else part + term
        groups.append(part)
    return butterfly(groups)


def sums_kernel(x_ref, sums_ref):
    near, owned, width = x_ref.shape[1:]
    shape = (2 * owned, 2 * owned)
    row, lane = (lax.broadcasted_iota(jnp.int32, shape, axis) for axis in (0, 1))
    for j in range(near):
        rows = x_ref[:, j].reshape(2 * owned, width).astype(jnp.float32)
        squares = jnp.sum(rows * rows, axis=1, keepdims=True)
        line = jnp.sum(jnp.where(row == lane, squares, 0.0), axis=0, keepdims=True)
        sums_ref[0, j] = line
        sums_ref[1, j] = line


def scale_rows(sums_ref, offset, owned, width, near):
    biggest = jnp.max(sums_ref[...], axis=0, keepdims=True)
    shape = (owned, 2 * owned)
    row, lane = (lax.broadcasted_iota(jnp.int32, shape, axis) for axis in (0, 1))
    biggest = jnp.sum(jnp.where(lane == row + offset, biggest, 0.0), axis=1, keepdims=True)
    mean = biggest * (1.0 / width)
    scale = jnp.sqrt(mean + 1e-06)
    peak = jnp.sqrt(mean * width) / scale
    step = near * jnp.where(
        peak >= clamp_level, clamp_level / 32768.0, jnp.maximum(peak, 1e-20) / 32767.0
    )
    return scale, step


def add_levels(pieces, half, inverse, sign_ref, matrix_ref, base, totals=None):
    signs = sign_ref[...].astype(jnp.float32).astype(jnp.bfloat16)
    matrix = matrix_ref[...]
    for piece in pieces:
        rows = piece[...] if len(piece.shape) == 2 else piece[half]
        groups = rotate_groups([rows * signs], matrix, base)
        levels = [
            jnp.clip(group * inverse, -clamp_level, clamp_level)
            .astype(jnp.bfloat16)
            .astype(jnp.float32)
            for group in groups
        ]
        totals = levels if totals is None else [t + v for t, v in zip(totals, levels)]
    return totals


def proxy_pairs_kernel(near, count, base, *refs):
    pieces, rest = refs[:count], refs[count:]
    sums_ref, sign_ref, matrix_ref, total_ref, inverse_ref, step_ref = rest
    owned, width = total_ref.shape
    half = 1 - lax.axis_index("dp") // near
    scale, step = scale_rows(sums_ref, half * owned, owned, width, near)
    inverse = (1.0 / math.sqrt(width)) / scale
    totals = add_levels(pieces, half, inverse, sign_ref, matrix_ref, base)
    for g, total in enumerate(totals):
        total_ref[:, g * base : (g + 1) * base] = total
    inverse_ref[...] = jnp.broadcast_to(inverse, inverse_ref.shape)
    step_ref[...] = jnp.broadcast_to(1.0 / step, step_ref.shape)


def proxy_kernel(count, base, *refs):
    pieces, rest = refs[:count], refs[count:]
    total_ref, inverse_ref, step_ref, sign_ref, matrix_ref, sent_ref = rest
    cuts = [slice(start, start + base) for start in range(0, total_ref.shape[1], base)]
    totals = [total_ref[:, cut] for cut in cuts]
    totals = add_levels(pieces, 0, inverse_ref[:, 0:1], sign_ref, matrix_ref, base, totals)
    steps = step_ref[:, 0:1]
    for cut, total in zip(cuts, totals):
        value = jnp.clip(jnp.round(total * steps), -32767.0, 32767.0)
        sent_ref[:, cut] = value.astype(jnp.int16)


def owner_kernel(near, base, *refs):
    pieces, rest = refs[:near], refs[near:]
    sums_ref, sign_ref, matrix_ref, total_ref, scale_ref, step_ref = rest
    owned, width = total_ref.shape
    half = lax.axis_index("dp") // near
    scale, step = scale_rows(sums_ref, half * owned, owned, width, near)
    inverse = (1.0 / math.sqrt(width)) / scale
    totals = add_levels(pieces, half, inverse, sign_ref, matrix_ref, base)
    for g, total in enumerate(totals):
        total_ref[:, g * base : (g + 1) * base] = total
    scale_ref[...] = jnp.broadcast_to(scale / (2 * near), scale_ref.shape)
    step_ref[...] = jnp.broadcast_to(step, step_ref.shape)


def finish_kernel(near_ref, far_ref, scale_ref, step_ref, square_ref):
    width = near_ref.shape[1]
    step = step_ref[...]
    squares = None
    for start in range(0, width, lanes):
        cut = slice(start, start + lanes)
        total = near_ref[:, cut] + far_ref[:, cut].astype(jnp.float32) * step
        squares = total * total if squares is None else squares + total * total
    scale = scale_ref[...]
    squares = jnp.sum(squares * (scale * scale), axis=0, keepdims=True)
    square_ref[...] = jnp.broadcast_to(squares[None], square_ref.shape)


def back_kernel(base, near_ref, far_ref, scale_ref, step_ref, sign_ref, matrix_ref, unrot_ref):
    total = near_ref[...] + far_ref[...].astype(jnp.float32) * step_ref[:, 0:1]
    high = total.astype(jnp.bfloat16)
    low = (total - high.astype(jnp.float32)).astype(jnp.bfloat16)
    groups = rotate_groups([high, low], matrix_ref[...], base)
    back = scale_ref[:, 0:1] * (1.0 / math.sqrt(total.shape[1]))
    signs = sign_ref[...].astype(jnp.float32)
    for g, group in enumerate(groups):
        cut = slice(g * base, (g + 1) * base)
        unrot_ref[:, cut] = group * back * signs[:, cut]


def clip_factor(limit, square_ref):
    squares = jnp.sum(jnp.sum(square_ref[...], axis=0, keepdims=True), axis=1, keepdims=True)
    return limit / jnp.maximum(jnp.sqrt(squares), limit)


def weights_kernel(limit, square_ref, unrot_ref, weight_ref, comp_ref, new_ref):
    update = unrot_ref[...] * clip_factor(limit, square_ref)
    summed = weight_ref[...].astype(jnp.float32) + (
        comp_ref[...].astype(jnp.float32) - learn_rate * update
    )
    new_ref[...] = summed.astype(jnp.bfloat16)


def update_kernel(limit, square_ref, unrot_ref, update_ref):
    update_ref[...] = unrot_ref[...] * clip_factor(limit, square_ref)


def chips_along_x(replicas):
    return 1 << ((replicas.bit_length() - 1) // 2)


def swap(value, mask):
    size = lax.axis_size("dp")
    return lax.ppermute(value, "dp", [(i, i ^ mask) for i in range(size)])


def place_kernel(places, owned, *refs):
    pieces, out_ref, sem = refs[: len(places)], refs[-2], refs[-1]
    me = lax.axis_index("dp")
    copies = []
    for i, ((mask, row), piece) in enumerate(zip(places, pieces)):
        start = pl.multiple_of((me ^ mask) * owned + row, 16)
        rows = pl.ds(start, piece.shape[0])
        copies.append(pltpu.make_async_copy(piece, out_ref.at[rows], sem.at[i]))
    for copy in copies:
        copy.start()
    for copy in copies:
        copy.wait()


def place_pieces(items, owned, replicas, out, name):
    places = [(mask, row) for mask, row, _ in items]
    values = [piece for _, _, piece in items]
    operands, aliases = list(values), {}
    specs = [pl.BlockSpec(memory_space=pltpu.VMEM)] * len(values)
    if out is not None:
        aliases = {len(operands): 0}
        operands.append(out)
        specs.append(pl.BlockSpec(memory_space=pl.ANY))
    width = values[0].shape[1]
    return pl.pallas_call(
        functools.partial(place_kernel, places, owned),
        in_specs=specs,
        out_specs=pl.BlockSpec(memory_space=pl.ANY),
        out_shape=jax.ShapeDtypeStruct((replicas * owned, width), values[0].dtype),
        scratch_shapes=[pltpu.SemaphoreType.DMA((len(values),))],
        input_output_aliases=aliases,
        compiler_params=pltpu.CompilerParams(vmem_limit_bytes=vmem_bytes),
        name=name,
    )(*operands)


def gather_blocks(block, replicas):
    x_count = chips_along_x(replicas)
    near = replicas // 2
    owned, width = block.shape
    far = swap(block, near)
    own = {0: block}
    for m in range(1, near):
        own[m] = swap(block, m) if m < x_count or m % x_count == 0 else None
    for m in range(1, near):
        if own[m] is None:
            own[m] = swap(own[m - m % x_count], m % x_count)
    own = [(m, 0, piece) for m, piece in own.items()]
    spread = [(near + m, 0, swap(far, m)) for m in range(1, near)]
    out = place_pieces(own + [(near, 0, far)], owned, replicas, None, "place_own")
    out = place_pieces(spread, owned, replicas, out, "place_far")
    return out.reshape(1, replicas * owned, width)


def on_device(grads, signs, weights, compensation):
    blocks, width = grads.shape[2:]
    replicas = lax.axis_size("dp")
    devices = replicas * lax.axis_size("expert")
    owned = blocks // replicas
    base = min(width, 256)
    matrix = jnp.asarray(hadamard(base), jnp.bfloat16)
    me = lax.axis_index("dp")
    near = replicas // 2
    params = pltpu.CompilerParams(vmem_limit_bytes=vmem_bytes)
    array = pl.BlockSpec(memory_space=pltpu.VMEM)

    def pair_of(source, index):
        source = source.reshape(2, near, owned, width)
        return lax.dynamic_slice_in_dim(source, index % near, 1, 1).reshape(2, owned, width)

    def block_of(source, index):
        source = source.reshape(replicas, owned, width)
        return lax.dynamic_slice_in_dim(source, index, 1, 0).reshape(owned, width)

    x_count = chips_along_x(replicas)
    aligned = [m for m in range(1, near) if m % x_count == 0 or m < x_count]
    diagonal = [m for m in range(1, near) if m not in aligned]
    pairs = [swap(pair_of(grads, me ^ mask), mask) for mask in aligned]
    sums = pl.pallas_call(
        sums_kernel,
        in_specs=[array],
        out_shape=jax.ShapeDtypeStruct((2, near, 1, 2 * owned), jnp.float32),
        compiler_params=params,
        name="sum_squares",
    )(grads.reshape(2, near, owned, width))
    later, sums = lax.optimization_barrier((grads, sums))
    sums = lax.all_to_all(
        sums.reshape(replicas, 1, 2 * owned), "dp", split_axis=0, concat_axis=0, tiled=True
    ).reshape(replicas, 2 * owned)
    far_pieces = [swap(block_of(later, me ^ mask ^ near), mask) for mask in diagonal]
    near_pieces = [swap(block_of(later, me ^ mask), mask) for mask in diagonal]
    pairs.append(pair_of(later, me))
    whole = jax.ShapeDtypeStruct((owned, width), jnp.float32)
    column = jax.ShapeDtypeStruct((owned, lanes), jnp.float32)
    part, inverse, step = pl.pallas_call(
        functools.partial(proxy_pairs_kernel, near, len(pairs), base),
        in_specs=[array] * (len(pairs) + 3),
        out_shape=(whole, column, column),
        compiler_params=params,
        name="proxy_pairs",
    )(*pairs, sums, signs, matrix)
    sent = pl.pallas_call(
        functools.partial(proxy_kernel, len(far_pieces), base),
        in_specs=[array] * (len(far_pieces) + 5),
        out_shape=jax.ShapeDtypeStruct((owned, width), jnp.int16),
        compiler_params=params,
        name="proxy_blocks",
    )(*far_pieces, part, inverse, step, signs, matrix)
    far_total = swap(sent, near)
    near_total, mean_scale, step = pl.pallas_call(
        functools.partial(owner_kernel, near, base),
        in_specs=[array] * (near + 3),
        out_shape=(whole, column, column),
        compiler_params=params,
        name="owner_blocks",
    )(*pairs, *near_pieces, sums, signs, matrix)
    squares = pl.pallas_call(
        finish_kernel,
        in_specs=[array] * 4,
        out_shape=jax.ShapeDtypeStruct((devices, 1, lanes), jnp.float32),
        compiler_params=params,
        name="finish_blocks",
    )(near_total, far_total, mean_scale, step)
    unrot = pl.pallas_call(
        functools.partial(back_kernel, base),
        out_shape=jax.ShapeDtypeStruct((owned, width), jnp.float32),
        compiler_params=params,
        name="rotate_back",
    )(near_total, far_total, mean_scale, step, signs, matrix)
    squares = lax.all_to_all(squares, ("dp", "expert"), split_axis=0, concat_axis=0, tiled=True)
    limit = target_rms * math.sqrt(blocks * width * lax.axis_size("expert"))
    squares = squares.reshape(devices, lanes)
    new_weights = pl.pallas_call(
        functools.partial(weights_kernel, limit),
        out_shape=jax.ShapeDtypeStruct((owned, width), jnp.bfloat16),
        compiler_params=params,
        name="new_weights",
    )(squares, unrot, weights.reshape(owned, width), compensation.reshape(owned, width))
    update_grad = pl.pallas_call(
        functools.partial(update_kernel, limit),
        out_shape=jax.ShapeDtypeStruct((owned, width), jnp.float32),
        compiler_params=params,
        name="update_grad",
    )(squares, unrot)
    return gather_blocks(new_weights, replicas), update_grad.reshape(weights.shape)


def solution(mesh):
    in_specs = (
        P("dp", "expert", None, None),
        P("expert", None),
        P("expert", "dp", None),
        P("expert", "dp", None),
    )
    out_specs = (P("expert", None, None), P("expert", "dp", None))
    return jax.shard_map(
        on_device, mesh=mesh, in_specs=in_specs, out_specs=out_specs, check_vma=False
    )
```

```python
import functools
import math

import jax
import jax.numpy as jnp
import numpy as np
from jax import lax
from jax.experimental import pallas as pl
from jax.experimental.pallas import tpu as pltpu
from jax.sharding import PartitionSpec as P

clamp_level = 2.0
target_rms = 0.2
learn_rate = 0.02
lanes = 128
vmem_bytes = 40 * 1024 * 1024


def hadamard(width):
    matrix = np.ones((1, 1), np.float32)
    while matrix.shape[0] < width:
        matrix = np.block([[matrix, matrix], [matrix, -matrix]])
    return matrix


def butterfly(groups):
    half = 1
    groups = list(groups)
    while half < len(groups):
        for start in range(0, len(groups), 2 * half):
            for i in range(start, start + half):
                upper, lower = groups[i], groups[i + half]
                groups[i], groups[i + half] = upper + lower, upper - lower
        half *= 2
    return groups


def rotate_groups(pieces, matrix, base):
    count = pieces[0].shape[1] // base
    groups = []
    for g in range(count):
        part = None
        for piece in pieces:
            term = jnp.dot(
                piece[:, g * base : (g + 1) * base], matrix, preferred_element_type=jnp.float32
            )
            part = term if part is None else part + term
        groups.append(part)
    return butterfly(groups)


def sums_kernel(x_ref, sums_ref):
    near, owned, width = x_ref.shape[1:]
    shape = (2 * owned, 2 * owned)
    row, lane = (lax.broadcasted_iota(jnp.int32, shape, axis) for axis in (0, 1))
    for j in range(near):
        rows = x_ref[:, j].reshape(2 * owned, width).astype(jnp.float32)
        squares = jnp.sum(rows * rows, axis=1, keepdims=True)
        line = jnp.sum(jnp.where(row == lane, squares, 0.0), axis=0, keepdims=True)
        sums_ref[0, j] = line
        sums_ref[1, j] = line


def scale_rows(sums_ref, offset, owned, width, near):
    biggest = jnp.max(sums_ref[...], axis=0, keepdims=True)
    shape = (owned, 2 * owned)
    row, lane = (lax.broadcasted_iota(jnp.int32, shape, axis) for axis in (0, 1))
    biggest = jnp.sum(jnp.where(lane == row + offset, biggest, 0.0), axis=1, keepdims=True)
    mean = biggest * (1.0 / width)
    scale = jnp.sqrt(mean + 1e-06)
    peak = jnp.sqrt(mean * width) / scale
    step = near * jnp.where(
        peak >= clamp_level, clamp_level / 32768.0, jnp.maximum(peak, 1e-20) / 32767.0
    )
    return scale, step


def add_levels(pieces, half, inverse, sign_ref, matrix_ref, base, totals=None):
    signs = sign_ref[...].astype(jnp.float32).astype(jnp.bfloat16)
    matrix = matrix_ref[...]
    for piece in pieces:
        rows = piece[...] if len(piece.shape) == 2 else piece[half]
        groups = rotate_groups([rows * signs], matrix, base)
        levels = [
            jnp.clip(group * inverse, -clamp_level, clamp_level)
            .astype(jnp.bfloat16)
            .astype(jnp.float32)
            for group in groups
        ]
        totals = levels if totals is None else [t + v for t, v in zip(totals, levels)]
    return totals


def proxy_pairs_kernel(near, count, base, *refs):
    pieces, rest = refs[:count], refs[count:]
    sums_ref, sign_ref, matrix_ref, total_ref, inverse_ref, step_ref = rest
    owned, width = total_ref.shape
    half = 1 - lax.axis_index("dp") // near
    scale, step = scale_rows(sums_ref, half * owned, owned, width, near)
    inverse = (1.0 / math.sqrt(width)) / scale
    totals = add_levels(pieces, half, inverse, sign_ref, matrix_ref, base)
    for g, total in enumerate(totals):
        total_ref[:, g * base : (g + 1) * base] = total
    inverse_ref[...] = jnp.broadcast_to(inverse, inverse_ref.shape)
    step_ref[...] = jnp.broadcast_to(1.0 / step, step_ref.shape)


def proxy_kernel(count, base, *refs):
    pieces, rest = refs[:count], refs[count:]
    total_ref, inverse_ref, step_ref, sign_ref, matrix_ref, sent_ref = rest
    cuts = [slice(start, start + base) for start in range(0, total_ref.shape[1], base)]
    totals = [total_ref[:, cut] for cut in cuts]
    totals = add_levels(pieces, 0, inverse_ref[:, 0:1], sign_ref, matrix_ref, base, totals)
    steps = step_ref[:, 0:1]
    for cut, total in zip(cuts, totals):
        value = jnp.clip(jnp.round(total * steps), -32767.0, 32767.0)
        sent_ref[:, cut] = value.astype(jnp.int16)


def owner_kernel(near, base, *refs):
    pieces, rest = refs[:near], refs[near:]
    sums_ref, sign_ref, matrix_ref, total_ref, scale_ref, step_ref = rest
    owned, width = total_ref.shape
    half = lax.axis_index("dp") // near
    scale, step = scale_rows(sums_ref, half * owned, owned, width, near)
    inverse = (1.0 / math.sqrt(width)) / scale
    totals = add_levels(pieces, half, inverse, sign_ref, matrix_ref, base)
    for g, total in enumerate(totals):
        total_ref[:, g * base : (g + 1) * base] = total
    scale_ref[...] = jnp.broadcast_to(scale / (2 * near), scale_ref.shape)
    step_ref[...] = jnp.broadcast_to(step, step_ref.shape)


def finish_kernel(near_ref, far_ref, scale_ref, step_ref, total_ref, square_ref):
    width = near_ref.shape[1]
    step = step_ref[...]
    squares = None
    for start in range(0, width, lanes):
        cut = slice(start, start + lanes)
        total = near_ref[:, cut] + far_ref[:, cut].astype(jnp.float32) * step
        total_ref[:, cut] = total
        squares = total * total if squares is None else squares + total * total
    scale = scale_ref[...]
    squares = jnp.sum(squares * (scale * scale), axis=0, keepdims=True)
    square_ref[...] = jnp.broadcast_to(squares[None], square_ref.shape)


def back_kernel(base, total_ref, scale_ref, sign_ref, matrix_ref, unrot_ref):
    owned, width = total_ref.shape
    total = total_ref[...]
    high = total.astype(jnp.bfloat16)
    low = (total - high.astype(jnp.float32)).astype(jnp.bfloat16)
    groups = rotate_groups([high, low], matrix_ref[...], base)
    back = scale_ref[:, 0:1] * (1.0 / math.sqrt(width))
    signs = sign_ref[...].astype(jnp.float32)
    for g, group in enumerate(groups):
        cut = slice(g * base, (g + 1) * base)
        unrot_ref[:, cut] = group * back * signs[:, cut]


def clip_factor(limit, square_ref):
    squares = jnp.sum(jnp.sum(square_ref[...], axis=0, keepdims=True), axis=1, keepdims=True)
    return limit / jnp.maximum(jnp.sqrt(squares), limit)


def weights_kernel(limit, square_ref, unrot_ref, weight_ref, comp_ref, new_ref):
    update = unrot_ref[...] * clip_factor(limit, square_ref)
    summed = weight_ref[...].astype(jnp.float32) + (
        comp_ref[...].astype(jnp.float32) - learn_rate * update
    )
    new_ref[...] = summed.astype(jnp.bfloat16)


def update_kernel(limit, square_ref, unrot_ref, update_ref):
    update_ref[...] = unrot_ref[...] * clip_factor(limit, square_ref)


def chips_along_x(replicas):
    return 1 << ((replicas.bit_length() - 1) // 2)


def swap(value, mask):
    size = lax.axis_size("dp")
    return lax.ppermute(value, "dp", [(i, i ^ mask) for i in range(size)])


def place_kernel(places, owned, *refs):
    pieces, out_ref, sem = refs[: len(places)], refs[-2], refs[-1]
    me = lax.axis_index("dp")
    copies = []
    for i, ((mask, row), piece) in enumerate(zip(places, pieces)):
        start = pl.multiple_of((me ^ mask) * owned + row, 16)
        rows = pl.ds(start, piece.shape[0])
        copies.append(pltpu.make_async_copy(piece, out_ref.at[rows], sem.at[i]))
    for copy in copies:
        copy.start()
    for copy in copies:
        copy.wait()


def place_pieces(items, owned, replicas, out, name):
    places = [(mask, row) for mask, row, _ in items]
    values = [piece for _, _, piece in items]
    operands, aliases = list(values), {}
    specs = [pl.BlockSpec(memory_space=pltpu.VMEM)] * len(values)
    if out is not None:
        aliases = {len(operands): 0}
        operands.append(out)
        specs.append(pl.BlockSpec(memory_space=pl.ANY))
    width = values[0].shape[1]
    return pl.pallas_call(
        functools.partial(place_kernel, places, owned),
        in_specs=specs,
        out_specs=pl.BlockSpec(memory_space=pl.ANY),
        out_shape=jax.ShapeDtypeStruct((replicas * owned, width), values[0].dtype),
        scratch_shapes=[pltpu.SemaphoreType.DMA((len(values),))],
        input_output_aliases=aliases,
        compiler_params=pltpu.CompilerParams(vmem_limit_bytes=vmem_bytes),
        name=name,
    )(*operands)


def gather_blocks(block, replicas):
    x_count = chips_along_x(replicas)
    near = replicas // 2
    owned, width = block.shape
    far = swap(block, near)
    own = {0: block}
    for m in range(1, near):
        own[m] = swap(block, m) if m < x_count or m % x_count == 0 else None
    for m in range(1, near):
        if own[m] is None:
            held, far = lax.optimization_barrier((own[m - m % x_count], far))
            own[m] = swap(held, m % x_count)
    own = [(m, 0, piece) for m, piece in own.items()]
    spread = [(near + m, 0, swap(far, m)) for m in range(1, near)]
    out = place_pieces(own + [(near, 0, far)], owned, replicas, None, "place_own")
    out = place_pieces(spread, owned, replicas, out, "place_far")
    return out.reshape(1, replicas * owned, width)


def on_device(grads, signs, weights, compensation):
    blocks, width = grads.shape[2:]
    replicas = lax.axis_size("dp")
    devices = replicas * lax.axis_size("expert")
    owned = blocks // replicas
    base = min(width, 256)
    matrix = jnp.asarray(hadamard(base), jnp.bfloat16)
    me = lax.axis_index("dp")
    near = replicas // 2
    params = pltpu.CompilerParams(vmem_limit_bytes=vmem_bytes)
    array = pl.BlockSpec(memory_space=pltpu.VMEM)

    def pair_of(source, index):
        source = source.reshape(2, near, owned, width)
        return lax.dynamic_slice_in_dim(source, index % near, 1, 1).reshape(2, owned, width)

    def block_of(source, index):
        source = source.reshape(replicas, owned, width)
        return lax.dynamic_slice_in_dim(source, index, 1, 0).reshape(owned, width)

    x_count = chips_along_x(replicas)
    aligned = [m for m in range(1, near) if m % x_count == 0 or m < x_count]
    diagonal = [m for m in range(1, near) if m not in aligned]
    pairs = [swap(pair_of(grads, me ^ mask), mask) for mask in aligned]
    sums = pl.pallas_call(
        sums_kernel,
        in_specs=[array],
        out_shape=jax.ShapeDtypeStruct((2, near, 1, 2 * owned), jnp.float32),
        compiler_params=params,
        name="sum_squares",
    )(grads.reshape(2, near, owned, width))
    later, sums = lax.optimization_barrier((grads, sums))
    sums = lax.all_to_all(
        sums.reshape(replicas, 1, 2 * owned), "dp", split_axis=0, concat_axis=0, tiled=True
    ).reshape(replicas, 2 * owned)
    far_pieces = [swap(block_of(later, me ^ mask ^ near), mask) for mask in diagonal]
    near_pieces = [swap(block_of(later, me ^ mask), mask) for mask in diagonal]
    pairs.append(pair_of(later, me))
    whole = jax.ShapeDtypeStruct((owned, width), jnp.float32)
    column = jax.ShapeDtypeStruct((owned, lanes), jnp.float32)
    part, inverse, step = pl.pallas_call(
        functools.partial(proxy_pairs_kernel, near, len(pairs), base),
        in_specs=[array] * (len(pairs) + 3),
        out_shape=(whole, column, column),
        compiler_params=params,
        name="proxy_pairs",
    )(*pairs, sums, signs, matrix)
    sent = pl.pallas_call(
        functools.partial(proxy_kernel, len(far_pieces), base),
        in_specs=[array] * (len(far_pieces) + 5),
        out_shape=jax.ShapeDtypeStruct((owned, width), jnp.int16),
        compiler_params=params,
        name="proxy_blocks",
    )(*far_pieces, part, inverse, step, signs, matrix)
    far_total = swap(sent, near)
    near_total, mean_scale, step = pl.pallas_call(
        functools.partial(owner_kernel, near, base),
        in_specs=[array] * (near + 3),
        out_shape=(whole, column, column),
        compiler_params=params,
        name="owner_blocks",
    )(*pairs, *near_pieces, sums, signs, matrix)
    total, squares = pl.pallas_call(
        finish_kernel,
        in_specs=[array] * 4,
        out_shape=(
            jax.ShapeDtypeStruct((owned, width), jnp.float32),
            jax.ShapeDtypeStruct((devices, 1, lanes), jnp.float32),
        ),
        compiler_params=params,
        name="finish_blocks",
    )(near_total, far_total, mean_scale, step)
    unrot = pl.pallas_call(
        functools.partial(back_kernel, base),
        out_shape=jax.ShapeDtypeStruct((owned, width), jnp.float32),
        compiler_params=params,
        name="rotate_back",
    )(total, mean_scale, signs, matrix)
    squares = lax.all_to_all(squares, ("dp", "expert"), split_axis=0, concat_axis=0, tiled=True)
    limit = target_rms * math.sqrt(blocks * width * lax.axis_size("expert"))
    squares = squares.reshape(devices, lanes)
    new_weights = pl.pallas_call(
        functools.partial(weights_kernel, limit),
        out_shape=jax.ShapeDtypeStruct((owned, width), jnp.bfloat16),
        compiler_params=params,
        name="new_weights",
    )(squares, unrot, weights.reshape(owned, width), compensation.reshape(owned, width))
    update_grad = pl.pallas_call(
        functools.partial(update_kernel, limit),
        out_shape=jax.ShapeDtypeStruct((owned, width), jnp.float32),
        compiler_params=params,
        name="update_grad",
    )(squares, unrot)
    return gather_blocks(new_weights, replicas), update_grad.reshape(weights.shape)


def solution(mesh):
    in_specs = (
        P("dp", "expert", None, None),
        P("expert", None),
        P("expert", "dp", None),
        P("expert", "dp", None),
    )
    out_specs = (P("expert", None, None), P("expert", "dp", None))
    return jax.shard_map(
        on_device, mesh=mesh, in_specs=in_specs, out_specs=out_specs, check_vma=False
    )
```

```python
import functools
import math

import jax
import jax.numpy as jnp
import numpy as np
from jax import lax
from jax.experimental import pallas as pl
from jax.experimental.pallas import tpu as pltpu
from jax.sharding import PartitionSpec as P

clamp_level = 2.0
target_rms = 0.2
learn_rate = 0.02
lanes = 128
vmem_bytes = 40 * 1024 * 1024


def hadamard(width):
    matrix = np.ones((1, 1), np.float32)
    while matrix.shape[0] < width:
        matrix = np.block([[matrix, matrix], [matrix, -matrix]])
    return matrix


def butterfly(groups):
    half = 1
    groups = list(groups)
    while half < len(groups):
        for start in range(0, len(groups), 2 * half):
            for i in range(start, start + half):
                upper, lower = groups[i], groups[i + half]
                groups[i], groups[i + half] = upper + lower, upper - lower
        half *= 2
    return groups


def rotate_groups(pieces, matrix, base):
    count = pieces[0].shape[1] // base
    groups = []
    for g in range(count):
        part = None
        for piece in pieces:
            term = jnp.dot(
                piece[:, g * base : (g + 1) * base], matrix, preferred_element_type=jnp.float32
            )
            part = term if part is None else part + term
        groups.append(part)
    return butterfly(groups)


def sums_kernel(x_ref, sums_ref):
    near, owned, width = x_ref.shape[1:]
    shape = (2 * owned, 2 * owned)
    row, lane = (lax.broadcasted_iota(jnp.int32, shape, axis) for axis in (0, 1))
    for j in range(near):
        rows = x_ref[:, j].reshape(2 * owned, width).astype(jnp.float32)
        squares = jnp.sum(rows * rows, axis=1, keepdims=True)
        line = jnp.sum(jnp.where(row == lane, squares, 0.0), axis=0, keepdims=True)
        sums_ref[0, j] = line
        sums_ref[1, j] = line


def scale_rows(sums_ref, offset, owned, width, near):
    biggest = jnp.max(sums_ref[...], axis=0, keepdims=True)
    shape = (owned, 2 * owned)
    row, lane = (lax.broadcasted_iota(jnp.int32, shape, axis) for axis in (0, 1))
    biggest = jnp.sum(jnp.where(lane == row + offset, biggest, 0.0), axis=1, keepdims=True)
    mean = biggest * (1.0 / width)
    scale = jnp.sqrt(mean + 1e-06)
    peak = jnp.sqrt(mean * width) / scale
    step = near * jnp.where(
        peak >= clamp_level, clamp_level / 32768.0, jnp.maximum(peak, 1e-20) / 32767.0
    )
    return scale, step


def add_levels(pieces, half, inverse, sign_ref, matrix_ref, base, totals=None):
    signs = sign_ref[...].astype(jnp.float32).astype(jnp.bfloat16)
    matrix = matrix_ref[...]
    for piece in pieces:
        rows = piece[...] if len(piece.shape) == 2 else piece[half]
        groups = rotate_groups([rows * signs], matrix, base)
        levels = [
            jnp.clip(group * inverse, -clamp_level, clamp_level)
            .astype(jnp.bfloat16)
            .astype(jnp.float32)
            for group in groups
        ]
        totals = levels if totals is None else [t + v for t, v in zip(totals, levels)]
    return totals


def proxy_pairs_kernel(near, count, base, *refs):
    pieces, rest = refs[:count], refs[count:]
    sums_ref, sign_ref, matrix_ref, total_ref, inverse_ref, step_ref = rest
    owned, width = total_ref.shape
    half = 1 - lax.axis_index("dp") // near
    scale, step = scale_rows(sums_ref, half * owned, owned, width, near)
    inverse = (1.0 / math.sqrt(width)) / scale
    totals = add_levels(pieces, half, inverse, sign_ref, matrix_ref, base)
    for g, total in enumerate(totals):
        total_ref[:, g * base : (g + 1) * base] = total
    inverse_ref[...] = jnp.broadcast_to(inverse, inverse_ref.shape)
    step_ref[...] = jnp.broadcast_to(1.0 / step, step_ref.shape)


def proxy_kernel(count, base, *refs):
    pieces, rest = refs[:count], refs[count:]
    total_ref, inverse_ref, step_ref, sign_ref, matrix_ref, sent_ref = rest
    cuts = [slice(start, start + base) for start in range(0, total_ref.shape[1], base)]
    totals = [total_ref[:, cut] for cut in cuts]
    totals = add_levels(pieces, 0, inverse_ref[:, 0:1], sign_ref, matrix_ref, base, totals)
    steps = step_ref[:, 0:1]
    for cut, total in zip(cuts, totals):
        value = jnp.clip(jnp.round(total * steps), -32767.0, 32767.0)
        sent_ref[:, cut] = value.astype(jnp.int16)


def owner_kernel(near, base, *refs):
    pieces, rest = refs[:near], refs[near:]
    sums_ref, sign_ref, matrix_ref, total_ref, scale_ref, step_ref = rest
    owned, width = total_ref.shape
    half = lax.axis_index("dp") // near
    scale, step = scale_rows(sums_ref, half * owned, owned, width, near)
    inverse = (1.0 / math.sqrt(width)) / scale
    totals = add_levels(pieces, half, inverse, sign_ref, matrix_ref, base)
    for g, total in enumerate(totals):
        total_ref[:, g * base : (g + 1) * base] = total
    scale_ref[...] = jnp.broadcast_to(scale / (2 * near), scale_ref.shape)
    step_ref[...] = jnp.broadcast_to(step, step_ref.shape)


def finish_kernel(near_ref, far_ref, scale_ref, step_ref, total_ref, square_ref):
    width = near_ref.shape[1]
    step = step_ref[...]
    squares = None
    for start in range(0, width, lanes):
        cut = slice(start, start + lanes)
        total = near_ref[:, cut] + far_ref[:, cut].astype(jnp.float32) * step
        total_ref[:, cut] = total
        squares = total * total if squares is None else squares + total * total
    scale = scale_ref[...]
    squares = jnp.sum(squares * (scale * scale), axis=0, keepdims=True)
    square_ref[...] = jnp.broadcast_to(squares[None], square_ref.shape)


def back_kernel(base, total_ref, scale_ref, sign_ref, matrix_ref, unrot_ref):
    owned, width = total_ref.shape
    total = total_ref[...]
    high = total.astype(jnp.bfloat16)
    low = (total - high.astype(jnp.float32)).astype(jnp.bfloat16)
    groups = rotate_groups([high, low], matrix_ref[...], base)
    back = scale_ref[:, 0:1] * (1.0 / math.sqrt(width))
    signs = sign_ref[...].astype(jnp.float32)
    for g, group in enumerate(groups):
        cut = slice(g * base, (g + 1) * base)
        unrot_ref[:, cut] = group * back * signs[:, cut]


def clip_factor(limit, square_ref):
    squares = jnp.sum(jnp.sum(square_ref[...], axis=0, keepdims=True), axis=1, keepdims=True)
    return limit / jnp.maximum(jnp.sqrt(squares), limit)


def weights_kernel(limit, square_ref, unrot_ref, weight_ref, comp_ref, new_ref):
    update = unrot_ref[...] * clip_factor(limit, square_ref)
    summed = weight_ref[...].astype(jnp.float32) + (
        comp_ref[...].astype(jnp.float32) - learn_rate * update
    )
    new_ref[...] = summed.astype(jnp.bfloat16)


def update_kernel(limit, square_ref, unrot_ref, update_ref):
    update_ref[...] = unrot_ref[...] * clip_factor(limit, square_ref)


def chips_along_x(replicas):
    return 1 << ((replicas.bit_length() - 1) // 2)


def swap(value, mask):
    size = lax.axis_size("dp")
    return lax.ppermute(value, "dp", [(i, i ^ mask) for i in range(size)])


def place_kernel(places, owned, *refs):
    pieces, out_ref, sem = refs[: len(places)], refs[-2], refs[-1]
    me = lax.axis_index("dp")
    copies = []
    for i, ((mask, row), piece) in enumerate(zip(places, pieces)):
        start = pl.multiple_of((me ^ mask) * owned + row, 16)
        rows = pl.ds(start, piece.shape[0])
        copies.append(pltpu.make_async_copy(piece, out_ref.at[rows], sem.at[i]))
    for copy in copies:
        copy.start()
    for copy in copies:
        copy.wait()


def place_pieces(items, owned, replicas, out, name):
    places = [(mask, row) for mask, row, _ in items]
    values = [piece for _, _, piece in items]
    operands, aliases = list(values), {}
    specs = [pl.BlockSpec(memory_space=pltpu.VMEM)] * len(values)
    if out is not None:
        aliases = {len(operands): 0}
        operands.append(out)
        specs.append(pl.BlockSpec(memory_space=pl.ANY))
    width = values[0].shape[1]
    return pl.pallas_call(
        functools.partial(place_kernel, places, owned),
        in_specs=specs,
        out_specs=pl.BlockSpec(memory_space=pl.ANY),
        out_shape=jax.ShapeDtypeStruct((replicas * owned, width), values[0].dtype),
        scratch_shapes=[pltpu.SemaphoreType.DMA((len(values),))],
        input_output_aliases=aliases,
        compiler_params=pltpu.CompilerParams(vmem_limit_bytes=vmem_bytes),
        name=name,
    )(*operands)


def gather_blocks(block, replicas):
    x_count = chips_along_x(replicas)
    near = replicas // 2
    owned, width = block.shape
    far = swap(block, near)
    own = {0: block}
    for m in range(1, near):
        own[m] = swap(block, m) if m < x_count or m % x_count == 0 else None
    for m in range(1, near):
        if own[m] is None:
            own[m] = swap(own[m - m % x_count], m % x_count)
    own = [(m, 0, piece) for m, piece in own.items()]
    spread = [(near + m, 0, swap(far, m)) for m in range(1, near)]
    out = place_pieces(own + [(near, 0, far)], owned, replicas, None, "place_own")
    out = place_pieces(spread, owned, replicas, out, "place_far")
    return out.reshape(1, replicas * owned, width)


def on_device(grads, signs, weights, compensation):
    blocks, width = grads.shape[2:]
    replicas = lax.axis_size("dp")
    devices = replicas * lax.axis_size("expert")
    owned = blocks // replicas
    base = min(width, 256)
    matrix = jnp.asarray(hadamard(base), jnp.bfloat16)
    me = lax.axis_index("dp")
    near = replicas // 2
    params = pltpu.CompilerParams(vmem_limit_bytes=vmem_bytes)
    array = pl.BlockSpec(memory_space=pltpu.VMEM)

    def pair_of(source, index):
        source = source.reshape(2, near, owned, width)
        return lax.dynamic_slice_in_dim(source, index % near, 1, 1).reshape(2, owned, width)

    def block_of(source, index):
        source = source.reshape(replicas, owned, width)
        return lax.dynamic_slice_in_dim(source, index, 1, 0).reshape(owned, width)

    x_count = chips_along_x(replicas)
    aligned = [m for m in range(1, near) if m % x_count == 0 or m < x_count]
    diagonal = [m for m in range(1, near) if m not in aligned]
    pairs = [swap(pair_of(grads, me ^ mask), mask) for mask in reversed(aligned)]
    sums = pl.pallas_call(
        sums_kernel,
        in_specs=[array],
        out_shape=jax.ShapeDtypeStruct((2, near, 1, 2 * owned), jnp.float32),
        compiler_params=params,
        name="sum_squares",
    )(grads.reshape(2, near, owned, width))
    later, sums = lax.optimization_barrier((grads, sums))
    sums = lax.all_to_all(
        sums.reshape(replicas, 1, 2 * owned), "dp", split_axis=0, concat_axis=0, tiled=True
    ).reshape(replicas, 2 * owned)
    far_pieces = [swap(block_of(later, me ^ mask ^ near), mask) for mask in diagonal]
    near_pieces = [swap(block_of(later, me ^ mask), mask) for mask in diagonal]
    pairs.append(pair_of(later, me))
    whole = jax.ShapeDtypeStruct((owned, width), jnp.float32)
    column = jax.ShapeDtypeStruct((owned, lanes), jnp.float32)
    part, inverse, step = pl.pallas_call(
        functools.partial(proxy_pairs_kernel, near, len(pairs), base),
        in_specs=[array] * (len(pairs) + 3),
        out_shape=(whole, column, column),
        compiler_params=params,
        name="proxy_pairs",
    )(*pairs, sums, signs, matrix)
    sent = pl.pallas_call(
        functools.partial(proxy_kernel, len(far_pieces), base),
        in_specs=[array] * (len(far_pieces) + 5),
        out_shape=jax.ShapeDtypeStruct((owned, width), jnp.int16),
        compiler_params=params,
        name="proxy_blocks",
    )(*far_pieces, part, inverse, step, signs, matrix)
    far_total = swap(sent, near)
    near_total, mean_scale, step = pl.pallas_call(
        functools.partial(owner_kernel, near, base),
        in_specs=[array] * (near + 3),
        out_shape=(whole, column, column),
        compiler_params=params,
        name="owner_blocks",
    )(*pairs, *near_pieces, sums, signs, matrix)
    total, squares = pl.pallas_call(
        finish_kernel,
        in_specs=[array] * 4,
        out_shape=(
            jax.ShapeDtypeStruct((owned, width), jnp.float32),
            jax.ShapeDtypeStruct((devices, 1, lanes), jnp.float32),
        ),
        compiler_params=params,
        name="finish_blocks",
    )(near_total, far_total, mean_scale, step)
    unrot = pl.pallas_call(
        functools.partial(back_kernel, base),
        out_shape=jax.ShapeDtypeStruct((owned, width), jnp.float32),
        compiler_params=params,
        name="rotate_back",
    )(total, mean_scale, signs, matrix)
    squares = lax.all_to_all(squares, ("dp", "expert"), split_axis=0, concat_axis=0, tiled=True)
    limit = target_rms * math.sqrt(blocks * width * lax.axis_size("expert"))
    squares = squares.reshape(devices, lanes)
    new_weights = pl.pallas_call(
        functools.partial(weights_kernel, limit),
        out_shape=jax.ShapeDtypeStruct((owned, width), jnp.bfloat16),
        compiler_params=params,
        name="new_weights",
    )(squares, unrot, weights.reshape(owned, width), compensation.reshape(owned, width))
    update_grad = pl.pallas_call(
        functools.partial(update_kernel, limit),
        out_shape=jax.ShapeDtypeStruct((owned, width), jnp.float32),
        compiler_params=params,
        name="update_grad",
    )(squares, unrot)
    return gather_blocks(new_weights, replicas), update_grad.reshape(weights.shape)


def solution(mesh):
    in_specs = (
        P("dp", "expert", None, None),
        P("expert", None),
        P("expert", "dp", None),
        P("expert", "dp", None),
    )
    out_specs = (P("expert", None, None), P("expert", "dp", None))
    return jax.shard_map(
        on_device, mesh=mesh, in_specs=in_specs, out_specs=out_specs, check_vma=False
    )
```

```python
import functools
import math

import jax
import jax.numpy as jnp
import numpy as np
from jax import lax
from jax.experimental import pallas as pl
from jax.experimental.pallas import tpu as pltpu
from jax.sharding import PartitionSpec as P

clamp_level = 2.0
target_rms = 0.2
learn_rate = 0.02
lanes = 128
vmem_bytes = 40 * 1024 * 1024


def hadamard(width):
    matrix = np.ones((1, 1), np.float32)
    while matrix.shape[0] < width:
        matrix = np.block([[matrix, matrix], [matrix, -matrix]])
    return matrix


def butterfly(groups):
    half = 1
    groups = list(groups)
    while half < len(groups):
        for start in range(0, len(groups), 2 * half):
            for i in range(start, start + half):
                upper, lower = groups[i], groups[i + half]
                groups[i], groups[i + half] = upper + lower, upper - lower
        half *= 2
    return groups


def rotate_groups(pieces, matrix, base):
    count = pieces[0].shape[1] // base
    groups = []
    for g in range(count):
        part = None
        for piece in pieces:
            term = jnp.dot(
                piece[:, g * base : (g + 1) * base], matrix, preferred_element_type=jnp.float32
            )
            part = term if part is None else part + term
        groups.append(part)
    return butterfly(groups)


def sums_kernel(x_ref, sums_ref):
    near, owned, width = x_ref.shape[1:]
    shape = (2 * owned, 2 * owned)
    row, lane = (lax.broadcasted_iota(jnp.int32, shape, axis) for axis in (0, 1))
    for j in range(near):
        rows = x_ref[:, j].reshape(2 * owned, width).astype(jnp.float32)
        squares = jnp.sum(rows * rows, axis=1, keepdims=True)
        line = jnp.sum(jnp.where(row == lane, squares, 0.0), axis=0, keepdims=True)
        sums_ref[0, j] = line
        sums_ref[1, j] = line


def scale_rows(sums_ref, offset, owned, width, near):
    biggest = jnp.max(sums_ref[...], axis=0, keepdims=True)
    shape = (owned, 2 * owned)
    row, lane = (lax.broadcasted_iota(jnp.int32, shape, axis) for axis in (0, 1))
    biggest = jnp.sum(jnp.where(lane == row + offset, biggest, 0.0), axis=1, keepdims=True)
    mean = biggest * (1.0 / width)
    scale = jnp.sqrt(mean + 1e-06)
    peak = jnp.sqrt(mean * width) / scale
    step = near * jnp.where(
        peak >= clamp_level, clamp_level / 32768.0, jnp.maximum(peak, 1e-20) / 32767.0
    )
    return scale, step


def add_levels(pieces, half, inverse, sign_ref, matrix_ref, base, totals=None):
    signs = sign_ref[...].astype(jnp.float32).astype(jnp.bfloat16)
    matrix = matrix_ref[...]
    for piece in pieces:
        rows = piece[...] if len(piece.shape) == 2 else piece[half]
        groups = rotate_groups([rows * signs], matrix, base)
        levels = [
            jnp.clip(group * inverse, -clamp_level, clamp_level)
            .astype(jnp.bfloat16)
            .astype(jnp.float32)
            for group in groups
        ]
        totals = levels if totals is None else [t + v for t, v in zip(totals, levels)]
    return totals


def proxy_pairs_kernel(near, count, base, *refs):
    pieces, rest = refs[:count], refs[count:]
    sums_ref, sign_ref, matrix_ref, total_ref, inverse_ref, step_ref = rest
    owned, width = total_ref.shape
    half = 1 - lax.axis_index("dp") // near
    scale, step = scale_rows(sums_ref, half * owned, owned, width, near)
    inverse = (1.0 / math.sqrt(width)) / scale
    totals = add_levels(pieces, half, inverse, sign_ref, matrix_ref, base)
    for g, total in enumerate(totals):
        total_ref[:, g * base : (g + 1) * base] = total
    inverse_ref[...] = jnp.broadcast_to(inverse, inverse_ref.shape)
    step_ref[...] = jnp.broadcast_to(1.0 / step, step_ref.shape)


def proxy_kernel(count, base, *refs):
    pieces, rest = refs[:count], refs[count:]
    total_ref, inverse_ref, step_ref, sign_ref, matrix_ref, sent_ref = rest
    cuts = [slice(start, start + base) for start in range(0, total_ref.shape[1], base)]
    totals = [total_ref[:, cut] for cut in cuts]
    totals = add_levels(pieces, 0, inverse_ref[:, 0:1], sign_ref, matrix_ref, base, totals)
    steps = step_ref[:, 0:1]
    for cut, total in zip(cuts, totals):
        value = jnp.clip(jnp.round(total * steps), -32767.0, 32767.0)
        sent_ref[:, cut] = value.astype(jnp.int16)


def owner_kernel(near, base, *refs):
    pieces, rest = refs[:near], refs[near:]
    sums_ref, sign_ref, matrix_ref, total_ref, scale_ref, step_ref = rest
    owned, width = total_ref.shape
    half = lax.axis_index("dp") // near
    scale, step = scale_rows(sums_ref, half * owned, owned, width, near)
    inverse = (1.0 / math.sqrt(width)) / scale
    totals = add_levels(pieces, half, inverse, sign_ref, matrix_ref, base)
    for g, total in enumerate(totals):
        total_ref[:, g * base : (g + 1) * base] = total
    scale_ref[...] = jnp.broadcast_to(scale / (2 * near), scale_ref.shape)
    step_ref[...] = jnp.broadcast_to(step, step_ref.shape)


def finish_kernel(near_ref, far_ref, scale_ref, step_ref, square_ref):
    width = near_ref.shape[1]
    step = step_ref[...]
    squares = None
    for start in range(0, width, lanes):
        cut = slice(start, start + lanes)
        total = near_ref[:, cut] + far_ref[:, cut].astype(jnp.float32) * step
        squares = total * total if squares is None else squares + total * total
    scale = scale_ref[...]
    squares = jnp.sum(squares * (scale * scale), axis=0, keepdims=True)
    square_ref[...] = jnp.broadcast_to(squares[None], square_ref.shape)


def back_kernel(base, near_ref, far_ref, scale_ref, step_ref, sign_ref, matrix_ref, unrot_ref):
    total = near_ref[...] + far_ref[...].astype(jnp.float32) * step_ref[:, 0:1]
    high = total.astype(jnp.bfloat16)
    low = (total - high.astype(jnp.float32)).astype(jnp.bfloat16)
    groups = rotate_groups([high, low], matrix_ref[...], base)
    back = scale_ref[:, 0:1] * (1.0 / math.sqrt(total.shape[1]))
    signs = sign_ref[...].astype(jnp.float32)
    for g, group in enumerate(groups):
        cut = slice(g * base, (g + 1) * base)
        unrot_ref[:, cut] = group * back * signs[:, cut]


def clip_factor(limit, square_ref):
    squares = jnp.sum(jnp.sum(square_ref[...], axis=0, keepdims=True), axis=1, keepdims=True)
    return limit / jnp.maximum(jnp.sqrt(squares), limit)


def weights_kernel(limit, square_ref, unrot_ref, weight_ref, comp_ref, new_ref):
    update = unrot_ref[...] * clip_factor(limit, square_ref)
    summed = weight_ref[...].astype(jnp.float32) + (
        comp_ref[...].astype(jnp.float32) - learn_rate * update
    )
    new_ref[...] = summed.astype(jnp.bfloat16)


def update_kernel(limit, square_ref, unrot_ref, update_ref):
    update_ref[...] = unrot_ref[...] * clip_factor(limit, square_ref)


def chips_along_x(replicas):
    return 1 << ((replicas.bit_length() - 1) // 2)


def swap(value, mask):
    size = lax.axis_size("dp")
    return lax.ppermute(value, "dp", [(i, i ^ mask) for i in range(size)])


def place_kernel(places, owned, *refs):
    pieces, out_ref, sem = refs[: len(places)], refs[-2], refs[-1]
    me = lax.axis_index("dp")
    copies = []
    for i, ((mask, row), piece) in enumerate(zip(places, pieces)):
        start = pl.multiple_of((me ^ mask) * owned + row, 16)
        rows = pl.ds(start, piece.shape[0])
        copies.append(pltpu.make_async_copy(piece, out_ref.at[rows], sem.at[i]))
    for copy in copies:
        copy.start()
    for copy in copies:
        copy.wait()


def place_pieces(items, owned, replicas, out, name):
    places = [(mask, row) for mask, row, _ in items]
    values = [piece for _, _, piece in items]
    operands, aliases = list(values), {}
    specs = [pl.BlockSpec(memory_space=pltpu.VMEM)] * len(values)
    if out is not None:
        aliases = {len(operands): 0}
        operands.append(out)
        specs.append(pl.BlockSpec(memory_space=pl.ANY))
    width = values[0].shape[1]
    return pl.pallas_call(
        functools.partial(place_kernel, places, owned),
        in_specs=specs,
        out_specs=pl.BlockSpec(memory_space=pl.ANY),
        out_shape=jax.ShapeDtypeStruct((replicas * owned, width), values[0].dtype),
        scratch_shapes=[pltpu.SemaphoreType.DMA((len(values),))],
        input_output_aliases=aliases,
        compiler_params=pltpu.CompilerParams(vmem_limit_bytes=vmem_bytes),
        name=name,
    )(*operands)


def gather_blocks(block, replicas):
    x_count = chips_along_x(replicas)
    near = replicas // 2
    owned, width = block.shape
    far = swap(block, near)
    own = {0: block}
    for m in range(1, near):
        own[m] = swap(block, m) if m < x_count or m % x_count == 0 else None
    for m in range(1, near):
        if own[m] is None:
            own[m] = swap(own[m - m % x_count], m % x_count)
    own = [(m, 0, piece) for m, piece in own.items()]
    spread = [(near + m, 0, swap(far, m)) for m in range(1, near)]
    out = place_pieces(own + [(near, 0, far)], owned, replicas, None, "place_own")
    out = place_pieces(spread[1:], owned, replicas, out, "place_far")
    out = place_pieces(spread[:1], owned, replicas, out, "place_last")
    return out.reshape(1, replicas * owned, width)


def on_device(grads, signs, weights, compensation):
    blocks, width = grads.shape[2:]
    replicas = lax.axis_size("dp")
    devices = replicas * lax.axis_size("expert")
    owned = blocks // replicas
    base = min(width, 256)
    matrix = jnp.asarray(hadamard(base), jnp.bfloat16)
    me = lax.axis_index("dp")
    near = replicas // 2
    params = pltpu.CompilerParams(vmem_limit_bytes=vmem_bytes)
    array = pl.BlockSpec(memory_space=pltpu.VMEM)

    def pair_of(source, index):
        source = source.reshape(2, near, owned, width)
        return lax.dynamic_slice_in_dim(source, index % near, 1, 1).reshape(2, owned, width)

    def block_of(source, index):
        source = source.reshape(replicas, owned, width)
        return lax.dynamic_slice_in_dim(source, index, 1, 0).reshape(owned, width)

    x_count = chips_along_x(replicas)
    aligned = [m for m in range(1, near) if m % x_count == 0 or m < x_count]
    diagonal = [m for m in range(1, near) if m not in aligned]
    pairs = [swap(pair_of(grads, me ^ mask), mask) for mask in aligned]
    sums = pl.pallas_call(
        sums_kernel,
        in_specs=[array],
        out_shape=jax.ShapeDtypeStruct((2, near, 1, 2 * owned), jnp.float32),
        compiler_params=params,
        name="sum_squares",
    )(grads.reshape(2, near, owned, width))
    later, sums = lax.optimization_barrier((grads, sums))
    sums = lax.all_to_all(
        sums.reshape(replicas, 1, 2 * owned), "dp", split_axis=0, concat_axis=0, tiled=True
    ).reshape(replicas, 2 * owned)
    far_pieces = [swap(block_of(later, me ^ mask ^ near), mask) for mask in diagonal]
    near_pieces = [swap(block_of(later, me ^ mask), mask) for mask in diagonal]
    pairs.append(pair_of(later, me))
    whole = jax.ShapeDtypeStruct((owned, width), jnp.float32)
    column = jax.ShapeDtypeStruct((owned, lanes), jnp.float32)
    part, inverse, step = pl.pallas_call(
        functools.partial(proxy_pairs_kernel, near, len(pairs), base),
        in_specs=[array] * (len(pairs) + 3),
        out_shape=(whole, column, column),
        compiler_params=params,
        name="proxy_pairs",
    )(*pairs, sums, signs, matrix)
    sent = pl.pallas_call(
        functools.partial(proxy_kernel, len(far_pieces), base),
        in_specs=[array] * (len(far_pieces) + 5),
        out_shape=jax.ShapeDtypeStruct((owned, width), jnp.int16),
        compiler_params=params,
        name="proxy_blocks",
    )(*far_pieces, part, inverse, step, signs, matrix)
    far_total = swap(sent, near)
    near_total, mean_scale, step = pl.pallas_call(
        functools.partial(owner_kernel, near, base),
        in_specs=[array] * (near + 3),
        out_shape=(whole, column, column),
        compiler_params=params,
        name="owner_blocks",
    )(*pairs, *near_pieces, sums, signs, matrix)
    squares = pl.pallas_call(
        finish_kernel,
        in_specs=[array] * 4,
        out_shape=jax.ShapeDtypeStruct((devices, 1, lanes), jnp.float32),
        compiler_params=params,
        name="finish_blocks",
    )(near_total, far_total, mean_scale, step)
    unrot = pl.pallas_call(
        functools.partial(back_kernel, base),
        out_shape=jax.ShapeDtypeStruct((owned, width), jnp.float32),
        compiler_params=params,
        name="rotate_back",
    )(near_total, far_total, mean_scale, step, signs, matrix)
    squares = lax.all_to_all(squares, ("dp", "expert"), split_axis=0, concat_axis=0, tiled=True)
    limit = target_rms * math.sqrt(blocks * width * lax.axis_size("expert"))
    squares = squares.reshape(devices, lanes)
    new_weights = pl.pallas_call(
        functools.partial(weights_kernel, limit),
        out_shape=jax.ShapeDtypeStruct((owned, width), jnp.bfloat16),
        compiler_params=params,
        name="new_weights",
    )(squares, unrot, weights.reshape(owned, width), compensation.reshape(owned, width))
    update_grad = pl.pallas_call(
        functools.partial(update_kernel, limit),
        out_shape=jax.ShapeDtypeStruct((owned, width), jnp.float32),
        compiler_params=params,
        name="update_grad",
    )(squares, unrot)
    return gather_blocks(new_weights, replicas), update_grad.reshape(weights.shape)


def solution(mesh):
    in_specs = (
        P("dp", "expert", None, None),
        P("expert", None),
        P("expert", "dp", None),
        P("expert", "dp", None),
    )
    out_specs = (P("expert", None, None), P("expert", "dp", None))
    return jax.shard_map(
        on_device, mesh=mesh, in_specs=in_specs, out_specs=out_specs, check_vma=False
    )
```
